32 devices in a mesh: rep: 8 (over y, x, core), shard: 4 (over z).
Axes of the slice: x: 2, y: 2, z: 4, core: 2. Of those that a mesh axis runs over, the one named last changes fastest.
Arguments:
- tokens: bfloat16 [32768, 1024], P(('rep', 'shard')), may hold values from -6 to 6
- cotangent: bfloat16 [32768, 1024], P(('rep', 'shard')), may hold values from -6 to 6
- seq_lengths: int32 [64], replicated, may hold values from 256 to 1024, as said below
- deal_order: int32 [64], replicated, may hold values from 0 to 63, as said below
- norm_gain: bfloat16 [1024], P('shard'), may hold values from 0.5 to 1.5
- in_proj: bfloat16 [1024, 4384], P('shard'), may hold values from -0.1875 to 0.1875
- conv_weight: bfloat16 [4, 2304], P(None, 'shard'), may hold values from -3 to 3
- conv_bias: bfloat16 [2304], P('shard'), may hold values from -1.5 to 0.5
- step_bias: bfloat16 [32], P('shard'), may hold values from -4.59375 to -2.296875
- decay_log: bfloat16 [32], P('shard'), may hold values from 0 to 2.078125
- skip_gain: bfloat16 [32], P('shard'), may hold values from 0.5 to 2
- gate_gain: bfloat16 [2048], P('shard'), may hold values from 0.5 to 1.5
- out_proj: bfloat16 [2048, 1024], P('shard'), may hold values from -0.125 to 0.125
Outputs:
- output: bfloat16 [32768, 1024], P(('rep', 'shard'))
- grad_tokens: bfloat16 [32768, 1024], P(('rep', 'shard'))
- grad_norm_gain: float32 [1024], P('shard')
- grad_in_proj: float32 [1024, 4384], P('shard')
- grad_conv_weight: float32 [4, 2304], P(None, 'shard')
- grad_conv_bias: float32 [2304], P('shard')
- grad_step_bias: float32 [32], P('shard')
- grad_decay_log: float32 [32], P('shard')
- grad_skip_gain: float32 [32], P('shard')
- grad_gate_gain: float32 [2048], P('shard')
- grad_out_proj: float32 [2048, 1024], P('shard')
The draws below stay inside these ranges and needn't reach their ends.
Inputs may be any that keep to these rules, and one draw needn't show every extreme that they name: `seq_lengths`: each length is a multiple of 256. Taken in the order deal_order gives, the sequences fill each device's 1024 tokens exactly, whole sequences only, at most 3 on one device; some device holds a single sequence and some holds 3. `deal_order`: A permutation of the 64 sequence indices; entry j is the initial index of the j-th dealt sequence.
All inputs are finite; a program needn't handle non-finite values.
Results may differ from the reference program's by a relative error of at most 0.0075.
Values may be sent and summed in bfloat16 or wider, within the bound.
No kernel may reach another device: no remote copies, remote signals or barrier semaphores. Data moves between devices by JAX's collectives and lax.ppermute only.
A program may use at most 320 MiB of HBM per device.

```python
import jax
import jax.numpy as jnp
from jax import lax

D = 1024
DI = 2048
H = 32
P_SIZE = 64
NS = 128
CONVW = 4
SPAN = 256
TOK_DEV = 1024
SEQ_MIN = 256
SEQ_AVG = 2
SEQ_MAX = 3
CH = 2304
PROJ = 4384
TOKENS = 32768
SEQS = 64


def dealing(key):
    base = jax.random.fold_in(key, 11)
    first, second, third, fourth = jax.random.split(base, 4)
    devices = TOKENS // TOK_DEV
    half = devices // 2
    grid = TOK_DEV // SEQ_MIN
    paired = jax.random.randint(first, (half,), 1, 2 * SEQ_AVG).astype(jnp.int32).at[0].set(1)
    counts = jnp.concatenate([paired, 2 * SEQ_AVG - paired])
    counts = counts[jax.random.permutation(second, devices)]

    def pick_cuts(subkey):
        return (jax.random.permutation(subkey, grid - 1)[:SEQ_MAX - 1].astype(jnp.int32) + 1) * SEQ_MIN
    candidates = jax.vmap(pick_cuts)(jax.random.split(third, devices))
    index = jnp.arange(SEQ_MAX - 1)
    cuts = jnp.sort(jnp.where(index[None, :] < counts[:, None] - 1, candidates, TOK_DEV), axis=1)
    bounds = jnp.concatenate([jnp.zeros((devices, 1), jnp.int32), cuts.astype(jnp.int32), jnp.full((devices, 1), TOK_DEV, jnp.int32)], 1)
    pieces = bounds[:, 1:] - bounds[:, :-1]
    offsets = jnp.cumsum(counts) - counts
    place = jnp.arange(SEQ_MAX)
    where_to = jnp.where(place[None, :] < counts[:, None], offsets[:, None] + place[None, :], SEQS)
    dealt = jnp.zeros((SEQS,), jnp.int32).at[where_to.reshape(-1)].set(pieces.reshape(-1), mode='drop')
    order = jax.random.permutation(fourth, SEQS).astype(jnp.int32)
    lengths = jnp.zeros((SEQS,), jnp.int32).at[order].set(dealt)
    return (lengths, order)


def draw_seq_lengths(key, part):
    return dealing(key)[0]


def draw_deal_order(key, part):
    return dealing(key)[1]


def block_scale(rng, shape, cuts, least, largest):
    level, own = 1.0, jax.random.fold_in(rng, 6)
    for position, parts in cuts:
        steps = jnp.exp(jax.random.uniform(jax.random.fold_in(own, position), (parts,), jnp.float32, least / len(cuts), largest / len(cuts)))
        level = level * jnp.repeat(steps, shape[position] // parts).reshape([-1 if axis == position else 1 for axis in range(len(shape))])
    return level


def noise(key, dims, scale, most, cuts=(), kind=jnp.bfloat16):
    values = jax.random.normal(key, dims, jnp.float32) * scale
    if len(cuts) > 0:
        values = block_scale(key, dims, cuts, -0.22, 0.18) * values
    return jnp.clip(values, min=-most, max=most).astype(kind)


def setup_inputs(seed: int = 0) -> dict:
    key_list = jax.random.split(jax.random.key(seed), 14)
    tokens = noise(key_list[0], (TOKENS, D), 1.0, 6.0, ((0, 32),))
    cotangent = noise(key_list[1], (TOKENS, D), 1.0, 6.0, ((0, 32),))
    seq_lengths = draw_seq_lengths(jax.random.fold_in(key_list[13], 71), 0)
    deal_order = draw_deal_order(jax.random.fold_in(key_list[13], 71), 0)
    norm_gain = jnp.clip(1.0 + 0.1 * jax.random.normal(key_list[4], (D,), jnp.float32), 0.5, 1.5).astype(jnp.bfloat16)
    in_proj = noise(key_list[5], (D, PROJ), D ** -0.5, 0.1875, ((0, 4),))
    conv_weight = noise(key_list[6], (CONVW, CH), CONVW ** -0.5, 3.0, ((1, 4),))
    conv_bias = jnp.clip(-1.5 + 2.0 * jax.random.uniform(key_list[7], (CH,), jnp.float32) ** block_scale(key_list[7], (CH,), ((0, 4),), -0.2, 0.2), -1.5, 0.5).astype(jnp.bfloat16)
    step_bias = jnp.clip(-4.59375 + 2.296875 * jax.random.uniform(key_list[8], (H,), jnp.float32) ** block_scale(key_list[8], (H,), ((0, 4),), -0.2, 0.2), -4.59375, -2.296875).astype(jnp.bfloat16)
    decay_log = jnp.clip(2.078125 * jax.random.uniform(key_list[9], (H,), jnp.float32) ** block_scale(key_list[9], (H,), ((0, 4),), -0.2, 0.2), 0.0, 2.078125).astype(jnp.bfloat16)
    skip_gain = jnp.clip(0.5 + 1.5 * jax.random.uniform(key_list[10], (H,), jnp.float32) ** block_scale(key_list[10], (H,), ((0, 4),), -0.2, 0.2), 0.5, 2.0).astype(jnp.bfloat16)
    gate_gain = jnp.clip(1.0 + 0.1 * jax.random.normal(key_list[11], (DI,), jnp.float32), 0.5, 1.5).astype(jnp.bfloat16)
    out_proj = noise(key_list[12], (DI, D), DI ** -0.5, 0.125, ((0, 4),))
    return dict(tokens=tokens, cotangent=cotangent, seq_lengths=seq_lengths, deal_order=deal_order, norm_gain=norm_gain, in_proj=in_proj, conv_weight=conv_weight, conv_bias=conv_bias, step_bias=step_bias, decay_log=decay_log, skip_gain=skip_gain, gate_gain=gate_gain, out_proj=out_proj)


EPSILON = 1e-05
HIGHEST = lax.Precision.HIGHEST

@jax.custom_vjp
def low(v):
    return lax.optimization_barrier(v.astype(jnp.bfloat16)).astype(jnp.float32)

@jax.custom_vjp
def low_back(v):
    return v

def low_keep(v):
    return (low(v), None)

def low_pass(kept, grad):
    return (grad,)

def back_keep(v):
    return (v, None)

def back_low(kept, grad):
    return (low(grad),)
low.defvjp(low_keep, low_pass)
low_back.defvjp(back_keep, back_low)

def span_step(carry, block):
    state, prior_seg = carry
    values, step, rate, keys, queries, segment = block
    length = rate.shape[0]
    total = jnp.cumsum(rate, 0)
    index = jnp.arange(length)
    causal = (index[:, None] >= index[None, :]) & (segment[:, None] == segment[None, :])
    spread = jnp.where(causal[:, :, None], total[:, None, :] - total[None, :, :], 0.0)
    decay = jnp.where(causal[:, :, None], jnp.exp(spread), 0.0)
    intersection = jnp.dot(queries, keys.T, precision=HIGHEST)
    weight = decay * intersection[:, :, None] * step[None, :, :]
    result = jnp.einsum('ijh,jhp->ihp', weight, values, precision=HIGHEST)
    carried = (segment == prior_seg).astype(jnp.float32)
    reach = jnp.exp(total) * carried[:, None]
    result = result + jnp.einsum('in,hpn->ihp', queries, state, precision=HIGHEST) * reach[:, :, None]
    final_seg = segment[-1]
    tail = jnp.exp(total[-1][None, :] - total) * step * (segment == final_seg).astype(jnp.float32)[:, None]
    keep_state = jnp.exp(total[-1]) * (final_seg == prior_seg).astype(jnp.float32)
    fresh = jnp.einsum('jn,jhp->hpn', keys, values * tail[:, :, None], precision=HIGHEST)
    return ((state * keep_state[:, None, None] + fresh, final_seg), result)

def mixer(projected, conv_weight, conv_bias, step_bias, decay_log, skip_gain, gate_gain, segment):
    length = projected.shape[0]
    width = DI + 2 * NS
    gate_part = projected[:, :DI]
    conv_part = projected[:, DI:DI + width]
    step_raw = projected[:, DI + width:]
    conv_sum = conv_bias[None, :] + conv_weight[CONVW - 1][None, :] * conv_part
    for back in range(1, CONVW):
        earlier = jnp.concatenate([jnp.zeros((back, width), jnp.float32), conv_part[:-back]], 0)
        earlier_seg = jnp.concatenate([jnp.full((back,), -1, jnp.int32), segment[:-back]], 0)
        same = (earlier_seg == segment).astype(jnp.float32)
        conv_sum = conv_sum + conv_weight[CONVW - 1 - back][None, :] * earlier * same[:, None]
    inner = jax.nn.silu(conv_sum)
    values = inner[:, :DI].reshape(length, H, P_SIZE)
    keys = inner[:, DI:DI + NS]
    queries = inner[:, DI + NS:]
    step = jax.nn.softplus(step_raw + step_bias[None, :])
    rate = -jnp.exp(decay_log)[None, :] * step
    blocks = length // SPAN
    stacked = (values.reshape(blocks, SPAN, H, P_SIZE), step.reshape(blocks, SPAN, H), rate.reshape(blocks, SPAN, H), keys.reshape(blocks, SPAN, NS), queries.reshape(blocks, SPAN, NS), segment.reshape(blocks, SPAN))
    start = (jnp.zeros((H, P_SIZE, NS), jnp.float32), jnp.array(-1, jnp.int32))
    final, scanned = lax.scan(jax.checkpoint(span_step), start, stacked)
    mixed = scanned.reshape(length, H, P_SIZE) + skip_gain[None, :, None] * values
    gated = mixed.reshape(length, DI) * jax.nn.silu(gate_part)
    return gated * lax.rsqrt(lax.optimization_barrier(jnp.mean(gated * gated, -1, keepdims=True)) + EPSILON) * gate_gain[None, :]

def normalize(values, gain):
    return values * lax.rsqrt(lax.optimization_barrier(jnp.mean(values * values, -1, keepdims=True)) + EPSILON) * gain[None, :]

def reference(tokens, cotangent, seq_lengths, deal_order, norm_gain, in_proj, conv_weight, conv_bias, step_bias, decay_log, skip_gain, gate_gain, out_proj):
    total_rows, width = tokens.shape
    dealt_len = seq_lengths[deal_order].astype(jnp.int32)
    orig_start = (jnp.cumsum(seq_lengths) - seq_lengths).astype(jnp.int32)
    dealt_start = (jnp.cumsum(dealt_len) - dealt_len).astype(jnp.int32)
    dealt_row = jnp.arange(total_rows, dtype=jnp.int32)
    segment = (jnp.searchsorted(dealt_start, dealt_row, side='right') - 1).astype(jnp.int32)
    orig_row = (orig_start[deal_order][segment] + dealt_row - dealt_start[segment]).astype(jnp.int32)
    blocks = total_rows // TOK_DEV
    inputs = tokens.astype(jnp.float32)[orig_row].reshape(blocks, TOK_DEV, width)
    grad_out = cotangent.astype(jnp.float32)[orig_row].reshape(blocks, TOK_DEV, width)
    seg_blocks = segment.reshape(blocks, TOK_DEV)

    def forward(values, ngain, wide_in, cweight, cbias, sbias, dlog, sgain, ggain, wide_out):

        def layer(pair):
            rows, seg_rows = pair
            normed = low(normalize(rows, ngain))
            projected = low_back(jnp.dot(normed, wide_in, precision=HIGHEST, preferred_element_type=jnp.float32))
            gated = mixer(projected, cweight, cbias, sbias, dlog, sgain, ggain, seg_rows)
            return rows + jnp.dot(low(gated), wide_out, precision=HIGHEST, preferred_element_type=jnp.float32)
        return lax.map(jax.checkpoint(layer), (values, seg_blocks))
    outputs, pullback = jax.vjp(forward, inputs, norm_gain.astype(jnp.float32), in_proj.astype(jnp.float32), conv_weight.astype(jnp.float32), conv_bias.astype(jnp.float32), step_bias.astype(jnp.float32), decay_log.astype(jnp.float32), skip_gain.astype(jnp.float32), gate_gain.astype(jnp.float32), out_proj.astype(jnp.float32))
    grads = pullback(grad_out)
    output = jnp.zeros((total_rows, width), jnp.bfloat16).at[orig_row].set(outputs.reshape(total_rows, width).astype(jnp.bfloat16))
    grad_tokens = jnp.zeros((total_rows, width), jnp.bfloat16).at[orig_row].set(grads[0].reshape(total_rows, width).astype(jnp.bfloat16))
    return (output, grad_tokens, grads[1], grads[2], grads[3], grads[4], grads[5], grads[6], grads[7], grads[8], grads[9])
```

```python
from functools import partial
from math import lcm

import jax
import jax.numpy as jnp
from jax import lax
from jax.experimental import pallas as pl
from jax.experimental.pallas import tpu as pltpu
from jax.sharding import PartitionSpec as P

D = 1024
DI = 2048
H = 32
P_SIZE = 64
NS = 128
CONVW = 4
CH = DI + 2 * NS
L = 256
LANES = 128
TILE = 256
EPSILON = 1e-05
VMEM = 58 << 20
F32 = jnp.float32
BF = jnp.bfloat16
NN = (((1,), (0,)), ((), ()))
NT = (((1,), (1,)), ((), ()))
TN = (((0,), (0,)), ((), ()))
BOTH = ("rep", "shard")


def dot(a, b, dims=NN):
    return lax.dot_general(a, b, dims, preferred_element_type=F32)


def sigmoid(v):
    return 0.5 * jnp.tanh(0.5 * v) + 0.5


def silu(v):
    half = 0.5 * v
    return half + half * jnp.tanh(half)


def silu_and_slope(v):
    half = 0.5 * v
    bent = jnp.tanh(half)
    part = half * bent
    return half + part, (0.5 + 0.5 * bent) * (1.0 + half - part)


def split2(v):
    hi = v.astype(BF)
    return jnp.concatenate([hi, (v - hi.astype(F32)).astype(BF)], 1)


def tri_sum(tri, v):
    hi = v.astype(BF)
    rest = v - hi.astype(F32)
    mid = rest.astype(BF)
    low = (rest - mid.astype(F32)).astype(BF)
    got = dot(tri, jnp.concatenate([hi, mid, low], 1))
    return got[:, :LANES] + got[:, LANES : 2 * LANES] + got[:, 2 * LANES :]


def head_spread():
    row = lax.broadcasted_iota(jnp.int32, (2 * LANES, DI), 0)
    col = lax.broadcasted_iota(jnp.int32, (2 * LANES, DI), 1)
    return jnp.where((row % LANES) == col // P_SIZE, 1.0, 0.0).astype(BF)


def head_sum(v, e2, at):
    hi = v.astype(BF)
    low = (v - hi.astype(F32)).astype(BF)
    return dot(hi, e2[0:LANES, at], NT) + dot(low, e2[0:LANES, at], NT)


def triangle(kind, up):
    row = lax.broadcasted_iota(jnp.int32, (L, L), 0)
    col = lax.broadcasted_iota(jnp.int32, (L, L), 1)
    return jnp.where(row <= col if up else row >= col, 1.0, 0.0).astype(kind)


def tile_at(t, size=TILE):
    return pl.ds(pl.multiple_of(t * size, size), size)


def tiles(width, size=TILE):
    return [slice(t, t + size) for t in range(0, width, size)]


def slot_of(rep, reps):
    return lax.rem(rep, 2) * (reps // 2) + rep // 2


def copies_of(refs, place, sems, shard, rep, reps, across):
    made = []

    def add(src, rows, lanes):
        made.append(pltpu.make_async_copy(src, place.at[rows, lanes], sems.at[len(made)]))

    own = refs[0]
    m = own.shape[1] if across else own.shape[0]
    part = refs[1].shape[1]

    def span(first, size):
        return pl.ds(pl.multiple_of(first, size if size % LANES == 0 else 16), size)

    everything = slice(None)
    if across:
        add(own, everything, span(shard * m, m))
    else:
        add(own, span(shard * m, m), everything)
    for i, ref in enumerate(refs[1:]):
        first = slot_of(rep ^ i, reps) * part
        for k in range(1, ref.shape[0] + 1):
            if across:
                add(ref.at[k - 1], span(first, part), span((shard ^ k) * m, m))
            else:
                add(ref.at[k - 1], span((shard ^ k) * m + first, part), everything)
    return made


def copy_count(reps, shards):
    return 1 + reps * (shards - 1)


def rms(x, gain):
    xf = x.astype(F32)
    inv = lax.rsqrt(jnp.mean(xf * xf, 1, keepdims=True) + EPSILON)
    return (xf * inv * gain).astype(BF)


def front_kernel(count, cont, x_ref, xh_ref, ng_ref, cw_ref, sp_ref, *rest):
    wrefs = rest[:count]
    (normed_ref, inner_ref, vp_ref, cs_ref, cin_ref, stp_ref, sig_ref, tot_ref, tott_ref, sloc_ref, fin_ref, nh_ref, ch_ref,
     cbuf, state, e2, wc, sems) = rest[count:]
    b = pl.program_id(0)
    nb = pl.num_programs(0)
    gain = ng_ref[...]

    @pl.when(b == 0)
    def _():
        loads = copies_of(wrefs, wc, sems, cont[nb + 1], cont[nb + 2], count - 1, True)
        for c in loads:
            c.start()
        e2[...] = head_spread()
        state[...] = jnp.zeros_like(state)
        halo = rms(xh_ref[...], gain)
        nh_ref[...] = halo
        for c in loads:
            c.wait()
        for at in tiles(CH):
            c = dot(halo, wc[at], NT)[8:16]
            ch_ref[:, at] = c
            for u in range(TILE // LANES):
                cbuf[at.start // LANES + u, 0:8, :] = c[:, u * LANES : (u + 1) * LANES]

    @pl.when(b > 0)
    def _():
        cbuf[:, 0:8, :] = cbuf[:, L : L + 8, :]

    keep = cont[b].astype(F32)
    cbuf[:, 0:8, :] = cbuf[:, 0:8, :] * keep
    normed = rms(x_ref[...], gain)
    normed_ref[...] = normed

    raw = dot(normed, wc[CH : CH + LANES], NT) + sp_ref[0:1, :]
    small = jnp.exp(-jnp.abs(raw))
    series = small * (1.0 - small * (0.5 - small * (1.0 / 3.0)))
    step = jnp.maximum(raw, 0.0) + jnp.where(small < 0.01, series, jnp.log(1.0 + small))
    rate = -sp_ref[1:2, :] * step
    total = tri_sum(triangle(BF, False), rate)
    stp_ref[...] = step
    sig_ref[...] = sigmoid(raw)
    tot_ref[...] = total
    tott_ref[0] = total.T
    last = total[L - 1 : L, :]
    steps = split2(step)
    leaving = split2(jnp.exp(last - total))
    kept = dot(split2(jnp.exp(jnp.broadcast_to(last, (8, LANES)))), e2[...])[0:1]
    state[...] = state[...] * keep
    sloc_ref[0] = state[...].astype(BF)

    def convolve(at):
        c = dot(normed, wc[at], NT)
        cin_ref[:, at] = c.astype(BF)
        for u in range(TILE // LANES):
            lt = at.start // LANES + u
            lanes = slice(lt * LANES, (lt + 1) * LANES)
            cbuf[lt, 8 : L + 8, :] = c[:, u * LANES : (u + 1) * LANES]
            for q in range(L // 64):
                lo = 8 + 64 * q
                acc = cw_ref[4:5, lanes] + cw_ref[3:4, lanes] * cbuf[lt, lo : lo + 64, :]
                for back in range(1, CONVW):
                    acc = acc + cw_ref[3 - back : 4 - back, lanes] * cbuf[lt, lo - back : lo - back + 64, :]
                cs_ref[64 * q : 64 * q + 64, lanes] = acc.astype(BF)
                inner_ref[64 * q : 64 * q + 64, lanes] = silu(acc).astype(BF)

    convolve(slice(DI, CH))
    keys = inner_ref[:, DI : DI + NS].T
    for at in tiles(DI):
        convolve(at)
        vp = (inner_ref[:, at].astype(F32) * dot(steps, e2[:, at])).astype(BF)
        vp_ref[:, at] = vp
        part = (vp.astype(F32) * dot(leaving, e2[:, at])).astype(BF)
        state[:, at] = state[:, at] * kept[:, at] + dot(keys, part)

    @pl.when(b == nb - 1)
    def _():
        fin_ref[...] = state[...].astype(BF)


def scan_kernel(cont, kq_ref, vp_ref, tot_ref, tott_ref, y_ref, gm):
    total = tot_ref[...]
    keys = kq_ref[:, :NS]
    queries = kq_ref[:, NS:]
    gm[...] = dot(queries, keys, NT) * triangle(F32, False)
    half = L // 2
    lane = lax.broadcasted_iota(jnp.int32, (L, LANES), 1)

    @pl.loop(0, H // 8)
    def _(g):
        cols = pltpu.roll(total, lax.rem(LANES - 8 * g, LANES), 1)
        rows = tott_ref[0, pl.ds(pl.multiple_of(g * 8, 8), 8), :]
        for pair in range(4):
            at = tile_at(g * 4 + pair, LANES)
            both = vp_ref[:, at]
            top, low = 0.0, 0.0
            for odd in range(2):
                i = 2 * pair + odd
                mine = jnp.where((lane >= P_SIZE) == (odd == 1), both, jnp.zeros_like(both))
                col = cols[:, i : i + 1]
                row = rows[i : i + 1, :]
                p0 = jnp.exp(jnp.minimum(col[:half] - row[:, :half], 0.0)) * gm[:half, :half]
                p1 = jnp.exp(jnp.minimum(col[half:] - row, 0.0)) * gm[half:, :]
                top = top + dot(p0.astype(BF), mine[:half])
                low = low + dot(p1.astype(BF), mine)
            y_ref[0:half, at] = top
            y_ref[half:L, at] = low


def gate_kernel(
    gates, outs, cont, x_ref, dy_ref, normed_ref, inner_ref, y_ref, tot_ref, sloc_ref, sin_ref, gg_ref, sk_ref, *rest
):
    grefs, orefs = rest[:gates], rest[gates : gates + outs]
    (out_ref, gn_ref, dgate_ref, dmix_ref, yd_ref, sc_ref, dlead_ref, sums_ref,
     e2, gate, gated, dn, etot, yfull, dlead, lead, wg, wo, gsems, osems) = rest[gates + outs :]
    b = pl.program_id(0)
    nb = pl.num_programs(0)

    @pl.when(b == 0)
    def _():
        loads = copies_of(grefs, wg, gsems, cont[nb + 1], cont[nb + 2], gates - 1, True)
        loads += copies_of(orefs, wo, osems, cont[nb + 1], cont[nb + 2], outs - 1, False)
        for c in loads:
            c.start()
        e2[...] = head_spread()
        dlead[...] = jnp.zeros_like(dlead)
        sums_ref[...] = jnp.zeros_like(sums_ref)
        lead[...] = jnp.ones_like(lead)
        for c in loads:
            c.wait()

    keep = cont[b].astype(F32)
    first = cont[0].astype(F32)
    lead[...] = lead[...] * jnp.where(b == 0, 1.0, keep)
    normed = normed_ref[...]
    queries = inner_ref[:, DI + NS :]
    reach = split2(jnp.exp(tot_ref[...]))
    square = jnp.zeros((L, TILE), F32)
    for at in tiles(DI):
        g = dot(normed, wg[at], NT)
        gate[:, at] = g
        start = (sloc_ref[0, :, at].astype(F32) + (lead[0:1, at] * first) * sin_ref[:, at].astype(F32)).astype(BF)
        sc_ref[0, :, at] = start
        e = dot(reach, e2[:, at])
        etot[:, at] = e
        y = y_ref[:, at] + e * dot(queries, start)
        yfull[:, at] = y
        v = (y + sk_ref[:, at] * inner_ref[:, at].astype(F32)) * silu(g)
        gated[:, at] = v
        square = square + v * v
    rinv = lax.rsqrt(jnp.sum(square, 1, keepdims=True) * (1.0 / DI) + EPSILON)
    for at in tiles(DI):
        gn_ref[:, at] = (gated[:, at] * rinv * gg_ref[:, at]).astype(BF)
    dy = dy_ref[...]
    inner_sum = jnp.zeros((L, TILE), F32)
    for at in tiles(DI):
        back = dot(dy, wo[at], NT)
        v = gated[:, at]
        sums_ref[0:1, at] += jnp.sum(back * (v * rinv), 0, keepdims=True)
        back = back * gg_ref[:, at]
        dn[:, at] = back
        inner_sum = inner_sum + back * v
    for at in tiles(D):
        out_ref[:, at] = (x_ref[:, at].astype(F32) + dot(gn_ref[...], wo[:, at])).astype(BF)
    shared = jnp.sum(inner_sum, 1, keepdims=True) * (1.0 / DI) * (rinv * rinv * rinv)
    turned = queries.T
    yd = jnp.zeros((L, LANES), F32)
    for at in tiles(DI):
        dgated = rinv * dn[:, at] - gated[:, at] * shared
        s, slope = silu_and_slope(gate[:, at])
        y = yfull[:, at]
        v = inner_ref[:, at].astype(F32)
        dgate_ref[:, at] = (dgated * (y + sk_ref[:, at] * v) * slope).astype(BF)
        dmix = (dgated * s).astype(BF)
        dmix_ref[:, at] = dmix
        dmix = dmix.astype(F32)
        sums_ref[1:2, at] += jnp.sum(dmix * v, 0, keepdims=True)
        yd = yd + head_sum(dmix * y, e2, at)
        dlead[:, at] += lead[0:1, at] * dot(turned, (dmix * etot[:, at]).astype(BF))
    yd_ref[...] = yd
    lead[...] = lead[...] * etot[L - 1 : L, :]

    @pl.when(b == nb - 1)
    def _():
        dlead_ref[...] = dlead[...].astype(BF)


def back_kernel(
    cont, kq_ref, vp_ref, cs_ref, cin_ref, stp_ref, sig_ref, tot_ref, tott_ref, sc_ref, dmix_ref, yd_ref, din_ref,
    cw_ref, sp_ref, sk_ref, ch_ref,
    gp_ref, gph_ref, csum_ref, hsum_ref,
    dstate, e2, z, dbuf, gt, dgt,
):
    nb = pl.num_programs(0)
    b = nb - 1 - pl.program_id(0)
    after = cont[b + 1].astype(F32)

    @pl.when(b == nb - 1)
    def _():
        e2[...] = head_spread()
        dstate[...] = din_ref[...].astype(F32)
        csum_ref[...] = jnp.zeros_like(csum_ref)
        hsum_ref[...] = jnp.zeros_like(hsum_ref)
        dbuf[:, L : L + 8, :] = jnp.zeros((CH // LANES, 8, LANES), F32)

    @pl.when(b < nb - 1)
    def _():
        dbuf[:, L : L + 8, :] = dbuf[:, 0:8, :] * after

    dstate[...] = dstate[...] * after
    step = stp_ref[...]
    total = tot_ref[...]
    last = total[L - 1 : L, :]
    keys = kq_ref[:, :NS]
    queries = kq_ref[:, NS:]
    gt[...] = dot(keys, queries, NT) * triangle(F32, True)
    dgt[...] = jnp.zeros_like(dgt)
    steps = split2(step)
    leaving = split2(jnp.exp(last - total))
    reach = split2(jnp.exp(total))
    kept = dot(split2(jnp.exp(jnp.broadcast_to(last, (8, LANES)))), e2[...])[0:1]

    turned = queries.T
    dk = jnp.zeros((L, NS), F32)
    dq = jnp.zeros((L, NS), F32)
    from_end = jnp.zeros((L, LANES), F32)
    through = jnp.zeros((8, LANES), F32)
    for at in tiles(DI):
        old = dstate[:, at]
        ds = old.astype(BF)
        w = dot(leaving, e2[:, at])
        scaled = w * dot(keys, ds)
        z[:, at] = scaled
        v = vp_ref[:, at].astype(F32)
        from_end = from_end + head_sum(v * scaled, e2, at)
        dk = dk + dot((v * w).astype(BF), ds, NT)
        reached = (dmix_ref[:, at].astype(F32) * dot(reach, e2[:, at])).astype(BF)
        start = sc_ref[0, :, at]
        dq = dq + dot(reached, start, NT)
        old = old * kept[:, at]
        passed = jnp.sum(old * start.astype(F32), 0, keepdims=True)
        through = through + head_sum(jnp.broadcast_to(passed, (8, TILE)), e2, at)
        dstate[:, at] = old + dot(turned, reached)

    half = L // 2
    lane = lax.broadcasted_iota(jnp.int32, (L, LANES), 1)

    @pl.loop(0, H // 8)
    def _(g):
        cols = pltpu.roll(total, lax.rem(LANES - 8 * g, LANES), 1)
        rows = tott_ref[0, pl.ds(pl.multiple_of(g * 8, 8), 8), :]
        for pair in range(4):
            at = tile_at(g * 4 + pair, LANES)
            dy = dmix_ref[:, at]
            v = vp_ref[:, at]
            top = z[0:half, at]
            low = z[half:L, at]
            for odd in range(2):
                i = 2 * pair + odd
                mine = jnp.where((lane >= P_SIZE) == (odd == 1), dy, jnp.zeros_like(dy))
                col = cols[:, i : i + 1]
                row = rows[i : i + 1, :]
                e0 = jnp.exp(jnp.minimum(row - col[:half], 0.0))
                e1 = jnp.exp(jnp.minimum(row[:, half:] - col[half:], 0.0))
                p0 = (e0 * gt[:half, :]).astype(BF)
                p1 = (e1 * gt[half:, half:]).astype(BF)
                top = top + dot(p0, mine)
                low = low + dot(p1, mine[half:])
                dgt[:half, :] += e0 * dot(v[:half], mine, NT)
                dgt[half:, half:] += e1 * dot(v[half:], mine[half:], NT)
            z[0:half, at] = top
            z[half:L, at] = low

    masked = (dgt[...] * triangle(F32, True)).astype(BF)
    dk = dk + dot(masked, queries)
    dq = dq + dot(masked, keys, TN)

    own = jnp.zeros((L, LANES), F32)
    for at in tiles(DI):
        dvp = z[:, at]
        own = own + head_sum(dvp * vp_ref[:, at].astype(F32), e2, at)
        dv = dot(steps, e2[:, at]) * dvp + sk_ref[:, at] * dmix_ref[:, at].astype(F32)
        dc = dv * silu_and_slope(cs_ref[:, at].astype(F32))[1]
        for u in range(TILE // LANES):
            dbuf[at.start // LANES + u, 0:L, :] = dc[:, u * LANES : (u + 1) * LANES]
    slope = silu_and_slope(cs_ref[:, DI:].astype(F32))[1]
    dbuf[DI // LANES, 0:L, :] = dk * slope[:, :NS]
    dbuf[DI // LANES + 1, 0:L, :] = dq * slope[:, NS:]

    row = lax.broadcasted_iota(jnp.int32, (L, LANES), 0)
    at_end = jnp.sum(from_end, 0, keepdims=True) + through[0:1]
    dtotal = yd_ref[...] - own + jnp.where(row == L - 1, at_end, 0.0)
    drate = tri_sum(triangle(BF, True), dtotal)
    decay = sp_ref[1:2, :]
    dstep = own / jnp.maximum(step, 1e-30) - decay * drate
    draw = jnp.where(lax.broadcasted_iota(jnp.int32, (L, LANES), 1) < H, dstep * sig_ref[...], 0.0)
    gp_ref[:, CH : CH + LANES] = draw.astype(BF)
    if gp_ref.shape[1] > CH + LANES:
        gp_ref[:, CH + LANES :] = jnp.zeros((L, gp_ref.shape[1] - CH - LANES), BF)
    hsum_ref[0:1, :] += jnp.sum(draw, 0, keepdims=True)
    hsum_ref[1:2, :] += jnp.sum(-decay * step * drate, 0, keepdims=True)

    for lt in range(CH // LANES):
        at = slice(lt * LANES, (lt + 1) * LANES)
        sums = [jnp.zeros((8, LANES), F32) for _ in range(CONVW + 1)]
        for q in range(L // 64):
            lo = 64 * q
            here = dbuf[lt, lo : lo + 64, :]
            c = cin_ref[lo : lo + 64, at].astype(F32)
            acc = cw_ref[3:4, at] * here
            sums[3] = sums[3] + jnp.sum((here * c).reshape(8, 8, LANES), 0)
            sums[4] = sums[4] + jnp.sum(here.reshape(8, 8, LANES), 0)
            for ahead in range(1, CONVW):
                there = dbuf[lt, lo + ahead : lo + ahead + 64, :]
                acc = acc + cw_ref[3 - ahead : 4 - ahead, at] * there
                sums[3 - ahead] = sums[3 - ahead] + jnp.sum((there * c).reshape(8, 8, LANES), 0)
            gp_ref[lo : lo + 64, at] = acc.astype(BF)
        for k in range(CONVW + 1):
            csum_ref[k : k + 1, at] += jnp.sum(sums[k], 0, keepdims=True)

    @pl.when(b == 0)
    def _():
        gph_ref[...] = jnp.zeros_like(gph_ref)
        for lt in range(CH // LANES):
            at = slice(lt * LANES, (lt + 1) * LANES)
            d = dbuf[lt, 0:8, :] * cont[0].astype(F32)
            d0, d1, d2 = d[0:1], d[1:2], d[2:3]
            w0, w1, w2 = cw_ref[0:1, at], cw_ref[1:2, at], cw_ref[2:3, at]
            c5, c6, c7 = ch_ref[5:6, at], ch_ref[6:7, at], ch_ref[7:8, at]
            made = [jnp.zeros((13, LANES), F32), w0 * d0, w1 * d0 + w0 * d1, w2 * d0 + w1 * d1 + w0 * d2]
            gph_ref[:, at] = jnp.concatenate(made, 0).astype(BF)
            csum_ref[0:1, at] += c5 * d0 + c6 * d1 + c7 * d2
            csum_ref[1:2, at] += c6 * d0 + c7 * d1
            csum_ref[2:3, at] += c7 * d0


def wide_grad_kernel(cont, gn_ref, dy_ref, normed_ref, dgate_ref, out_ref):
    k = pl.program_id(0)
    reps, shards, _, m = out_ref.shape
    o = dot(gn_ref[...], dy_ref[...], TN).astype(BF)
    part = o.shape[0] // reps
    for r in range(reps):
        for u in range(D // m):
            out_ref[r, k, u * part : (u + 1) * part, :] = o[r * part : (r + 1) * part, u * m : (u + 1) * m]
    g = dot(dgate_ref[...], normed_ref[...], TN).astype(BF)
    first = D // m * part
    part = DI // reps
    each = g.shape[0] // part
    for i in range(each):
        for s in range(shards):
            out_ref[k * each + i, s, first:, :] = g[i * part : (i + 1) * part, s * m : (s + 1) * m]


def conv_grad_kernel(nb, other, cont, normed_ref, gp_ref, nh_ref, gph_ref, out_ref, turned, turned_halo, full):
    k = pl.program_id(0)
    half, _, part, _ = out_ref.shape
    rep = cont[nb + 2]
    upper_half = lax.rem(rep, 2) ^ other
    width = turned.shape[0]
    base = half * part
    first = (base // LANES) * LANES

    @pl.when(k == 0)
    def _():
        lanes = pl.ds(pl.multiple_of(upper_half * first, LANES), width)
        turned[...] = gp_ref[:, lanes].T
        turned_halo[...] = gph_ref[:, lanes].T

    full[...] = dot(turned[...], normed_ref[...]) + dot(turned_halo[...], nh_ref[...])
    skip = upper_half * (base - first)
    for j in range(half):
        chip = (rep // 2) ^ j
        out_ref[j, 0] = full[pl.ds(pl.multiple_of(skip + chip * part, 16), part), :].astype(BF)


def input_grad_kernel(convs, gates, cont, x_ref, dy_ref, gp_ref, dgate_ref, ahead_ref, ng_ref, *rest):
    crefs, grefs = rest[:convs], rest[convs : convs + gates]
    gt_ref, gn_ref, wc, wg, csems, gsems, acc = rest[convs + gates :]
    b = pl.program_id(0)
    nb = pl.num_programs(0)

    @pl.when(b == 0)
    def _():
        loads = copies_of(crefs, wc, csems, cont[nb + 1], cont[nb + 2], convs - 1, True)
        loads += copies_of(grefs, wg, gsems, cont[nb + 1], cont[nb + 2], gates - 1, True)
        for c in loads:
            c.start()
        gn_ref[...] = jnp.zeros_like(gn_ref)
        for c in loads:
            c.wait()

    for at in tiles(D):
        acc[:, at] = dot(gp_ref[...], wc[:, at]) + dot(dgate_ref[...], wg[:, at])

    @pl.when(b == nb - 1)
    def _():
        keep = cont[nb].astype(F32)
        for at in tiles(D):
            acc[L - 16 : L, at] += keep * dot(ahead_ref[...], wc[:, at])

    for q in range(L // 32):
        rows = slice(32 * q, 32 * q + 32)
        x = x_ref[rows].astype(F32)
        inv = lax.rsqrt(jnp.mean(x * x, 1, keepdims=True) + EPSILON)
        g = acc[rows]
        gn_ref[...] += jnp.sum((g * (x * inv)).reshape(4, 8, D), 0)
        v = g * ng_ref[...]
        mean = jnp.mean(v * x, 1, keepdims=True)
        gt_ref[rows] = (inv * v - x * (inv * inv * inv * mean) + dy_ref[rows].astype(F32)).astype(BF)


def finish_wide_kernel(cont, wide_ref, gin_ref, gout_ref, buf, sem):
    reps, rows, m = wide_ref.shape
    part = DI // reps
    for r in range(reps):
        buf[r * part : (r + 1) * part, :] = wide_ref[r, rows - part :, :].astype(F32)
    copy = pltpu.make_async_copy(buf, gin_ref.at[pl.ds(0, DI)], sem)
    copy.start()
    part = (rows - part) * m // D
    for r in range(reps):
        for u in range(D // m):
            block = wide_ref[r, u * part : (u + 1) * part, :]
            gout_ref[r * part : (r + 1) * part, u * m : (u + 1) * m] = block.astype(F32)
    copy.wait()


def finish_conv_kernel(nb, count, cont, *rest):
    pieces = rest[:count]
    gin_ref, buf, sem = rest[count + 1 :]
    part = pieces[0].shape[0]
    for i, piece in enumerate(pieces):
        place = slot_of(cont[nb + 2] ^ i, count)
        buf[pl.ds(pl.multiple_of(place * part, 16), part), :] = piece[...].astype(F32)
    copy = pltpu.make_async_copy(buf.at[pl.ds(0, CH + H)], gin_ref.at[pl.ds(DI, CH + H)], sem)
    copy.start()
    copy.wait()


def rows_of(width, reverse=0, column=0):
    if reverse:
        return pl.BlockSpec((L, width), lambda b, cont: (reverse - 1 - b, column))
    return pl.BlockSpec((L, width), lambda b, cont: (b, column))


def whole(*shape):
    return pl.BlockSpec(shape, lambda b, cont: (0,) * len(shape), pipeline_mode=pl.Buffered(1))


def fixed(*shape):
    return pl.BlockSpec(shape, lambda b, cont: (0,) * len(shape))


def lead_of(reverse, *shape):
    if reverse:
        return pl.BlockSpec((1, *shape), lambda b, cont: (reverse - 1 - b, 0, 0))
    return pl.BlockSpec((1, *shape), lambda b, cont: (b, 0, 0))


def anywhere(count):
    return [pl.BlockSpec(memory_space=pl.ANY)] * count


def call(kernel, grid, in_specs, out_specs, outs, scratch, flops, nbytes, name, aliases=None):
    return pl.pallas_call(
        kernel,
        grid_spec=pltpu.PrefetchScalarGridSpec(
            num_scalar_prefetch=1, grid=(grid,), in_specs=in_specs, out_specs=out_specs, scratch_shapes=scratch
        ),
        out_shape=[jax.ShapeDtypeStruct(s, d) for s, d in outs],
        input_output_aliases=aliases or {},
        compiler_params=pltpu.CompilerParams(vmem_limit_bytes=VMEM),
        cost_estimate=pl.CostEstimate(flops=flops, bytes_accessed=nbytes, transcendentals=0),
        name=name,
    )


def loaded(count, shards, *shape):
    return [pltpu.VMEM(shape, BF), pltpu.SemaphoreType.DMA((copy_count(count - 1, shards),))]


def front(cont, x, xh, ng, wc, cw, sp, shards):
    rows = x.shape[0]
    nb = rows // L
    count = len(wc)
    return call(
        partial(front_kernel, count), nb,
        [rows_of(D), whole(16, D), whole(1, D), whole(8, CH), whole(8, LANES), *anywhere(count)],
        [rows_of(D), rows_of(CH), rows_of(DI), rows_of(CH), rows_of(CH), rows_of(LANES), rows_of(LANES), rows_of(LANES),
         lead_of(0, LANES, L), lead_of(0, NS, DI), fixed(NS, DI), fixed(16, D), fixed(8, CH)],
        [((rows, D), BF), ((rows, CH), BF), ((rows, DI), BF), ((rows, CH), BF), ((rows, CH), BF), ((rows, LANES), F32),
         ((rows, LANES), F32), ((rows, LANES), F32), ((nb, LANES, L), F32), ((nb, NS, DI), BF), ((NS, DI), BF),
         ((16, D), BF), ((8, CH), F32)],
        [pltpu.VMEM((CH // LANES, L + 8, LANES), F32), pltpu.VMEM((NS, DI), F32), pltpu.VMEM((2 * LANES, DI), BF),
         *loaded(count, shards, wc[0].shape[0], D)],
        20_000_000_000, 24 << 20, "front",
    )(cont, x, xh, ng, cw, sp, *wc)


def scan(cont, inner, vp, tot, tott):
    rows = inner.shape[0]
    nb = rows // L
    return call(
        scan_kernel, nb,
        [rows_of(2 * NS, 0, DI // (2 * NS)), rows_of(DI), rows_of(LANES), lead_of(0, LANES, L)],
        [rows_of(DI)],
        [((rows, DI), F32)],
        [pltpu.VMEM((L, L), F32)],
        30_000_000_000, 16 << 20, "scan",
    )(cont, inner, vp, tot, tott)[0]


def gating(cont, x, dy, normed, inner, y, tot, sloc, sin, wg, wo, gg, sk, shards):
    rows = x.shape[0]
    nb = rows // L
    gates, outs = len(wg), len(wo)
    wide = pltpu.VMEM((L, DI), F32)
    return call(
        partial(gate_kernel, gates, outs), nb,
        [rows_of(D), rows_of(D), rows_of(D), rows_of(CH), rows_of(DI), rows_of(LANES), lead_of(0, NS, DI), whole(NS, DI),
         whole(1, DI), whole(1, DI), *anywhere(gates + outs)],
        [rows_of(D), rows_of(DI), rows_of(DI), rows_of(DI), rows_of(LANES), lead_of(0, NS, DI), fixed(NS, DI),
         fixed(8, DI)],
        [((rows, D), BF), ((rows, DI), BF), ((rows, DI), BF), ((rows, DI), BF), ((rows, LANES), F32),
         ((nb, NS, DI), BF), ((NS, DI), BF), ((8, DI), F32)],
        [pltpu.VMEM((2 * LANES, DI), BF), wide, wide, wide, wide, wide,
         pltpu.VMEM((NS, DI), F32), pltpu.VMEM((1, DI), F32), pltpu.VMEM((DI, D), BF), pltpu.VMEM((DI, D), BF),
         pltpu.SemaphoreType.DMA((copy_count(gates - 1, shards),)), pltpu.SemaphoreType.DMA((copy_count(outs - 1, shards),))],
        35_000_000_000, 40 << 20, "gating",
    )(cont, x, dy, normed, inner, y, tot, sloc, sin, gg, sk, *wg, *wo)


def back(cont, inner, vp, cs, cin, stp, sig, tot, tott, sc, dmix, yd, din, cw, sp, sk, ch, width):
    rows = inner.shape[0]
    nb = rows // L
    return call(
        back_kernel, nb,
        [rows_of(2 * NS, nb, DI // (2 * NS)), rows_of(DI, nb), rows_of(CH, nb), rows_of(CH, nb), rows_of(LANES, nb),
         rows_of(LANES, nb), rows_of(LANES, nb), lead_of(nb, LANES, L), lead_of(nb, NS, DI), rows_of(DI, nb),
         rows_of(LANES, nb), whole(NS, DI), whole(8, CH), whole(8, LANES), whole(1, DI), whole(8, CH)],
        [rows_of(width, nb), fixed(16, width), fixed(8, CH), fixed(8, LANES)],
        [((rows, width), BF), ((16, width), BF), ((8, CH), F32), ((8, LANES), F32)],
        [pltpu.VMEM((NS, DI), F32), pltpu.VMEM((2 * LANES, DI), BF), pltpu.VMEM((L, DI), F32),
         pltpu.VMEM((CH // LANES, L + 8, LANES), F32), pltpu.VMEM((L, L), F32), pltpu.VMEM((L, L), F32)],
        60_000_000_000, 30 << 20, "back",
    )(cont, inner, vp, cs, cin, stp, sig, tot, tott, sc, dmix, yd, din, cw, sp, sk, ch)


def wide_grad(cont, gn, dy, normed, dgate, reps, shards):
    rows = dy.shape[0]
    block = DI // shards
    shape = (reps, shards, 2 * DI // reps, D // shards)
    return call(
        wide_grad_kernel, shards,
        [pl.BlockSpec((rows, block), lambda k, c: (0, k)), whole(rows, D), whole(rows, D),
         pl.BlockSpec((rows, block), lambda k, c: (0, k))],
        [fixed(*shape)],
        [(shape, BF)],
        [], 8_600_000_000, 24 << 20, "wide_grad",
    )(cont, gn, dy, normed, dgate)[0]


def conv_grad(cont, normed, gp, nh, gph, reps, shards, other):
    rows, width = gp.shape
    nb = rows // L
    m = D // shards
    part = width // reps
    half = width // 2
    span = width - (half // LANES) * LANES
    return call(
        partial(conv_grad_kernel, nb, other), shards,
        [pl.BlockSpec((rows, m), lambda k, c: (0, c[nb + 1] ^ k)), whole(rows, width),
         pl.BlockSpec((16, m), lambda k, c: (0, c[nb + 1] ^ k)), whole(16, width)],
        [pl.BlockSpec((reps // 2, 1, part, m), lambda k, c: (0, k, 0, 0))],
        [((reps // 2, shards, part, m), BF)],
        [pltpu.VMEM((span, rows), BF), pltpu.VMEM((span, 16), BF), pltpu.VMEM((span, m), F32)],
        5_000_000_000, 12 << 20, "conv_grad",
    )(cont, normed, gp, nh, gph)[0]


def input_grad(cont, x, dy, gp, dgate, ahead, ng, wc, wg, shards):
    rows, width = gp.shape
    nb = rows // L
    convs, gates = len(wc), len(wg)
    return call(
        partial(input_grad_kernel, convs, gates), nb,
        [rows_of(D), rows_of(D), rows_of(width), rows_of(DI), whole(16, width), whole(1, D), *anywhere(convs + gates)],
        [rows_of(D), fixed(8, D)],
        [((rows, D), BF), ((8, D), F32)],
        [pltpu.VMEM((width, D), BF), pltpu.VMEM((DI, D), BF),
         pltpu.SemaphoreType.DMA((copy_count(convs - 1, shards),)), pltpu.SemaphoreType.DMA((copy_count(gates - 1, shards),)),
         pltpu.VMEM((L, D), F32)],
        10_000_000_000, 24 << 20, "input_grad",
    )(cont, x, dy, gp, dgate, ahead, ng, *wc, *wg)


def finish_wide(cont, wide):
    reps, rows, m = wide.shape
    shards = D // m
    return call(
        finish_wide_kernel, 1,
        [whole(*wide.shape)],
        [pl.BlockSpec(memory_space=pl.ANY), fixed(DI // shards, D)],
        [((DI + CH + H, m), F32), ((DI // shards, D), F32)],
        [pltpu.VMEM((DI, m), F32), pltpu.SemaphoreType.DMA],
        1_000_000, 8 << 20, "finish_wide",
    )(cont, wide)


def finish_conv(cont, nb, pieces, gin):
    part, m = pieces[0].shape
    count = len(pieces)
    return call(
        partial(finish_conv_kernel, nb, count), 1,
        [*[whole(part, m)] * count, pl.BlockSpec(memory_space=pl.ANY)],
        [pl.BlockSpec(memory_space=pl.ANY)],
        [(gin.shape, F32)],
        [pltpu.VMEM((count * part, m), F32), pltpu.SemaphoreType.DMA],
        1_000_000, 5 << 20, "finish_conv", {1 + count: 0},
    )(cont, *pieces, gin)[0]


def shift(v, by):
    n = lax.axis_size(BOTH)
    return lax.ppermute(v, BOTH, [(i, (i + by) % n) for i in range(n)])


def swap(v, mask):
    n = lax.axis_size(BOTH)
    return lax.ppermute(v, BOTH, [(i, i ^ mask) for i in range(n)])


def over_shards(w):
    reps, shards = lax.axis_size("rep"), lax.axis_size("shard")
    part = w.shape[0] // reps
    mine = lax.dynamic_slice(w, (slot_of(lax.axis_index("rep"), reps) * part, 0), (part, w.shape[1]))
    return jnp.stack([swap(mine, k) for k in range(1, shards)])


def over_reps(column):
    reps, shards = lax.axis_size("rep"), lax.axis_size("shard")
    return [column] + [swap(column, 2 * shards * j) for j in range(1, reps // 2)]


def over_cores(plane):
    shards = lax.axis_size("shard")
    other = [swap(v, shards) for v in plane]
    return [v for pair in zip(plane, other) for v in pair]


def after(value, *first):
    return lax.optimization_barrier((value, first))[0]


def total_of(first, *others):
    out = first.astype(F32)
    for v in others:
        out = out + v.astype(F32)
    return out.astype(first.dtype)


def reduce_small(v):
    reps, shards = lax.axis_size("rep"), lax.axis_size("shard")
    mine = lax.axis_index("shard")

    def row(k):
        return lax.dynamic_slice(v, (mine ^ k, 0), (1, v.shape[1]))

    out = row(0)
    for got in [swap(row(k), k) for k in range(1, shards)]:
        out = out + got
    hop = shards
    while hop < shards * reps:
        out = out + swap(out, hop)
        hop *= 2
    return out[0]


def local(
    tokens, cotangent, seq_lengths, deal_order, norm_gain, in_proj, conv_weight, conv_bias, step_bias, decay_log,
    skip_gain, gate_gain, out_proj,
):
    n = lax.axis_size(BOTH)
    me = lax.axis_index(BOTH)
    reps, shards = lax.axis_size("rep"), lax.axis_size("shard")
    rep, mine = lax.axis_index("rep"), lax.axis_index("shard")
    rows = tokens.shape[0]
    nb = rows // L
    unit = lcm(LANES, 16 * reps)
    width = -(-(CH + LANES) // unit) * unit

    seqs = seq_lengths.shape[0]
    order = jnp.arange(seqs, dtype=jnp.int32)
    starts = jnp.sum(jnp.where(order[None, :] < order[:, None], seq_lengths[None, :], 0), 1)
    edge = (me * nb + jnp.arange(nb + 1, dtype=jnp.int32)) * L
    cont = jnp.where(jnp.any(starts[None, :] == edge[:, None], 1) | (edge >= n * rows), 0, 1)
    cont = jnp.concatenate([cont.astype(jnp.int32), jnp.stack([mine, rep]).astype(jnp.int32)])

    turned = in_proj.T
    wcs = jnp.pad(turned[DI:], ((0, width - CH - H), (0, 0)))
    wgs = turned[:DI]
    halo = shift(tokens[rows - 16 :], 1)
    conv_column = over_shards(wcs)

    small = jnp.concatenate(
        [conv_weight.reshape(-1), conv_bias, gate_gain, norm_gain, step_bias, decay_log, skip_gain]
    )
    small = jnp.stack([small] + [swap(small, k) for k in range(1, shards)])
    small = jnp.take(small, mine ^ jnp.arange(shards), axis=0).astype(F32)
    sizes = [conv_weight.size, conv_bias.size, gate_gain.size, norm_gain.size, step_bias.size, decay_log.size,
             skip_gain.size]
    parts, at = [], 0
    for size in sizes:
        parts.append(small[:, at : at + size])
        at += size
    taps = parts[0].reshape(shards, CONVW, -1).transpose(1, 0, 2).reshape(CONVW, CH)
    cw = jnp.concatenate([taps, parts[1].reshape(1, CH), jnp.zeros((3, CH), F32)], 0)
    gg = parts[2].reshape(1, DI)
    ng = parts[3].reshape(1, D)
    rate_scale = jnp.exp(parts[5].reshape(1, H))
    sp = jnp.pad(jnp.concatenate([parts[4].reshape(1, H), rate_scale], 0), ((0, 6), (0, LANES - H)))
    sk = jnp.repeat(parts[6].reshape(1, H), P_SIZE, axis=1)

    wc = [wcs, *over_cores(over_reps(conv_column))]
    gate_column = over_shards(after(wgs, conv_column))
    out_column = over_shards(after(out_proj, conv_column))
    wg = [wgs, *over_cores(over_reps(gate_column))]
    wo = [out_proj, *over_cores(over_reps(out_column))]

    normed, inner, vp, cs, cin, stp, sig, tot, tott, sloc, fin, nh, ch = front(cont, tokens, halo, ng, wc, cw, sp, shards)
    sin = shift(fin, 1)
    y = scan(cont, inner, vp, tot, tott)
    output, gn, dgate, dmix, yd, sc, dlead, sums = gating(
        cont, tokens, cotangent, normed, inner, y, tot, sloc, sin, wg, wo, gg, sk, shards
    )
    din = shift(dlead, -1)
    wide = after(wide_grad(cont, gn, cotangent, normed, dgate, reps, shards), din)
    wide = lax.psum_scatter(wide, "rep", scatter_dimension=0, tiled=True)[0]
    wide = lax.psum_scatter(wide, "shard", scatter_dimension=0, tiled=True)[0]
    wide = lax.all_gather(wide, "rep", axis=0)
    gp, gph, csum, hsum = back(cont, inner, vp, cs, cin, stp, sig, tot, tott, sc, dmix, yd, din, cw, sp, sk, ch, width)
    ahead = shift(gph, -1)

    theirs = swap(conv_grad(cont, normed, gp, nh, gph, reps, shards, 1), shards)
    w = conv_grad(cont, normed, gp, nh, gph, reps, shards, 0)
    w = [total_of(w[j], theirs[j]) for j in range(reps // 2)]
    gp = after(gp, w)
    w = total_of(w[0], *[swap(w[j], 2 * shards * j) for j in range(1, reps // 2)])
    w = total_of(w[0], *[swap(w[k], k) for k in range(1, shards)])
    pieces = over_cores(over_reps(w))
    gin, grad_out = finish_wide(cont, wide)
    grad_in = finish_conv(cont, nb, pieces, gin).T
    grad_tokens, grad_norm = input_grad(cont, tokens, cotangent, gp, dgate, ahead, ng, wc, wg, shards)

    packed = jnp.concatenate(
        [csum[0:CONVW].reshape(CONVW, shards, -1).transpose(1, 0, 2).reshape(shards, -1), csum[4].reshape(shards, -1),
         sums[0].reshape(shards, -1), grad_norm.sum(0).reshape(shards, -1), hsum[0, :H].reshape(shards, -1),
         hsum[1, :H].reshape(shards, -1), sums[1].reshape(H, P_SIZE).sum(1).reshape(shards, -1)], 1)
    own = reduce_small(packed)
    got, at = [], 0
    for size in sizes:
        got.append(own[at : at + size])
        at += size
    return (
        output, grad_tokens, got[3], grad_in, got[0].reshape(CONVW, -1), got[1], got[4], got[5], got[6], got[2],
        grad_out,
    )


def solution(mesh):
    both = P(BOTH, None)
    in_specs = (
        both, both, P(), P(), P("shard"), P("shard", None), P(None, "shard"), P("shard"), P("shard"), P("shard"),
        P("shard"), P("shard"), P("shard", None),
    )
    out_specs = (
        both, both, P("shard"), P("shard", None), P(None, "shard"), P("shard"), P("shard"), P("shard"), P("shard"),
        P("shard"), P("shard", None),
    )
    return jax.shard_map(local, mesh=mesh, in_specs=in_specs, out_specs=out_specs, check_vma=False)
```

```python
from functools import partial
from math import lcm

import jax
import jax.numpy as jnp
from jax import lax
from jax.experimental import pallas as pl
from jax.experimental.pallas import tpu as pltpu
from jax.sharding import PartitionSpec as P

D = 1024
DI = 2048
H = 32
P_SIZE = 64
NS = 128
CONVW = 4
CH = DI + 2 * NS
L = 256
LANES = 128
TILE = 256
EPSILON = 1e-05
LOG2E = 1.4426950408889634
VMEM = 58 << 20
F32 = jnp.float32
BF = jnp.bfloat16
NN = (((1,), (0,)), ((), ()))
NT = (((1,), (1,)), ((), ()))
TN = (((0,), (0,)), ((), ()))
BOTH = ("rep", "shard")


def dot(a, b, dims=NN):
    return lax.dot_general(a, b, dims, preferred_element_type=F32)


def sigmoid(v):
    return 0.5 * jnp.tanh(0.5 * v) + 0.5


def silu_and_slope(v):
    half = 0.5 * v
    bent = jnp.tanh(half)
    part = half * bent
    return half + part, (0.5 + 0.5 * bent) * (1.0 + half - part)


def split2(v):
    hi = v.astype(BF)
    return jnp.concatenate([hi, (v - hi.astype(F32)).astype(BF)], 1)


def tri_sum(tri, v):
    hi = v.astype(BF)
    rest = v - hi.astype(F32)
    mid = rest.astype(BF)
    low = (rest - mid.astype(F32)).astype(BF)
    got = dot(tri, jnp.concatenate([hi, mid, low], 1))
    return got[:, :LANES] + got[:, LANES : 2 * LANES] + got[:, 2 * LANES :]


def head_spread():
    row = lax.broadcasted_iota(jnp.int32, (2 * LANES, DI), 0)
    col = lax.broadcasted_iota(jnp.int32, (2 * LANES, DI), 1)
    return jnp.where((row % LANES) == col // P_SIZE, 1.0, 0.0).astype(BF)


def head_sum(v, e2, at):
    hi = v.astype(BF)
    low = (v - hi.astype(F32)).astype(BF)
    return dot(hi, e2[0:LANES, at], NT) + dot(low, e2[0:LANES, at], NT)


def triangle(kind, up):
    row = lax.broadcasted_iota(jnp.int32, (L, L), 0)
    col = lax.broadcasted_iota(jnp.int32, (L, L), 1)
    return jnp.where(row <= col if up else row >= col, 1.0, 0.0).astype(kind)


def tile_at(t, size=TILE):
    return pl.ds(pl.multiple_of(t * size, size), size)


def tiles(width, size=TILE):
    return [slice(t, t + size) for t in range(0, width, size)]


STEP = 64


def pieces_of(at):
    for lanes in range(at.start, at.stop, LANES):
        for q in range(0, L, STEP):
            yield slice(q, q + STEP), slice(lanes, lanes + LANES), slice(lanes - at.start, lanes - at.start + LANES)


def fold(v):
    return jnp.sum(v.reshape(STEP // 8, 8, LANES), 0)


def staged(parts, first, then):
    first(0, parts[0])
    for i, part in enumerate(parts):
        if i + 1 < len(parts):
            first(i + 1, parts[i + 1])
        then(i, part)


def slot_of(rep, reps):
    return lax.rem(rep, 2) * (reps // 2) + rep // 2


def span(first, size):
    return pl.ds(pl.multiple_of(first, 16), size)


def features(refs, place, part, shard, rep, reps):
    made = [(refs[0], place.at[shard])]
    for i, ref in enumerate(refs[1:]):
        first = slot_of(rep ^ i, reps) * part
        for k in range(1, ref.shape[0] + 1):
            source = ref.at[k - 1] if part == ref.shape[1] else ref.at[k - 1, pl.ds(0, part)]
            made.append((source, place.at[shard ^ k, span(first, part)]))
    return made


def rows_behind(own, refs, place, skip, shard, rep, reps):
    groups, n, _ = own.shape
    part = n // reps
    made = [(own.at[u], place.at[u, span(shard * n, n)]) for u in range(groups)]
    for i, ref in enumerate(refs):
        first = slot_of(rep ^ i, reps) * part
        for k in range(1, ref.shape[0] + 1):
            for u in range(groups):
                source = ref.at[k - 1, pl.ds(skip + u * part, part)]
                made.append((source, place.at[u, span((shard ^ k) * n + first, part)]))
    return made


def across(a, w, rows):
    m = w.shape[2]
    out = dot(a[:, 0:m], w[0, rows], NT)
    for s in range(1, w.shape[0]):
        out = out + dot(a[:, s * m : (s + 1) * m], w[s, rows], NT)
    return out


def copies_of(made, sems):
    return [pltpu.make_async_copy(source, place, sems.at[i]) for i, (source, place) in enumerate(made)]


def copy_count(reps, shards, each=1):
    return each + reps * (shards - 1) * each


def rms(x, gain):
    xf = x.astype(F32)
    inv = lax.rsqrt(jnp.mean(xf * xf, 1, keepdims=True) + EPSILON)
    return (xf * inv * gain).astype(BF)


def front_kernel(count, cont, x_ref, xh_ref, ng_ref, cw_ref, sp_ref, *rest):
    wrefs = rest[:count]
    (normed_ref, inner_ref, vp_ref, cs_ref, cin_ref, stp_ref, sig_ref, tot_ref, tott_ref, sloc_ref, fin_ref, nh_ref, ch_ref,
     cbuf, state, e2, part, weight, wc, sems) = rest[count:]
    b = pl.program_id(0)
    nb = pl.num_programs(0)
    gain = ng_ref[...]

    @pl.when(b == 0)
    def _():
        loads = copies_of(features(wrefs, wc, wc.shape[1] // (count - 1), cont[nb + 1], cont[nb + 2], count - 1), sems)
        for c in loads:
            c.start()
        e2[...] = head_spread()
        state[...] = jnp.zeros_like(state)
        halo = rms(xh_ref[...], gain)
        nh_ref[...] = halo
        for c in loads:
            c.wait()
        for at in tiles(CH):
            c = across(halo, wc, at)[8:16]
            ch_ref[:, at] = c
            for u in range(TILE // LANES):
                cbuf[at.start // LANES + u, 0:8, :] = c[:, u * LANES : (u + 1) * LANES]

    @pl.when(b > 0)
    def _():
        cbuf[:, 0:8, :] = cbuf[:, L : L + 8, :]

    keep = cont[b].astype(F32)
    cbuf[:, 0:8, :] = cbuf[:, 0:8, :] * keep
    normed = rms(x_ref[...], gain)
    normed_ref[...] = normed

    raw = across(normed, wc, slice(CH, CH + LANES)) + sp_ref[0:1, :]
    small = jnp.exp(-jnp.abs(raw))
    series = small * (1.0 - small * (0.5 - small * (1.0 / 3.0)))
    step = jnp.maximum(raw, 0.0) + jnp.where(small < 0.01, series, jnp.log(1.0 + small))
    rate = -sp_ref[1:2, :] * step
    total = tri_sum(triangle(BF, False), rate)
    stp_ref[...] = step
    sig_ref[...] = sigmoid(raw)
    tot_ref[...] = total
    tott_ref[0] = total.T
    last = total[L - 1 : L, :]
    steps = split2(step)
    leaving = split2(jnp.exp(last - total))
    kept = dot(split2(jnp.exp(jnp.broadcast_to(last, (8, LANES)))), e2[...])[0:1]
    state[...] = state[...] * keep
    sloc_ref[0] = state[...].astype(BF)

    def project(i, at):
        c = across(normed, wc, at)
        for u in range(TILE // LANES):
            cbuf[at.start // LANES + u, 8 : L + 8, :] = c[:, u * LANES : (u + 1) * LANES]
        if at.start < DI:
            weight[i % 2, 0] = dot(steps, e2[:, at])
            weight[i % 2, 1] = dot(leaving, e2[:, at])

    def convolve(i, at):
        for rows, lanes, within in pieces_of(at):
            lo = 8 + rows.start
            buf = cbuf.at[lanes.start // LANES]
            here = buf[lo : lo + STEP, :]
            cin_ref[rows, lanes] = here.astype(BF)
            acc = cw_ref[4:5, lanes] + cw_ref[3:4, lanes] * here
            for back in range(1, CONVW):
                acc = acc + cw_ref[3 - back : 4 - back, lanes] * buf[lo - back : lo - back + STEP, :]
            v, slope = silu_and_slope(acc)
            cs_ref[rows, lanes] = slope.astype(BF)
            inner_ref[rows, lanes] = v.astype(BF)
            if at.start < DI:
                v = v * weight[i % 2, 0, rows, within]
                vp_ref[rows, lanes] = v.astype(BF)
                part[rows, lanes] = (v * weight[i % 2, 1, rows, within]).astype(BF)

    staged([slice(DI, CH)] + tiles(DI), project, convolve)
    keys = inner_ref[:, DI : DI + NS].T
    for at in tiles(DI):
        state[:, at] = state[:, at] * kept[:, at] + dot(keys, part[:, at])

    @pl.when(b == nb - 1)
    def _():
        fin_ref[...] = state[...].astype(BF)


def scan_kernel(cont, kq_ref, vp_ref, tot_ref, tott_ref, y_ref, gm):
    total = tot_ref[...] * LOG2E
    keys = kq_ref[:, :NS]
    queries = kq_ref[:, NS:]
    gm[...] = dot(queries, keys, NT) * triangle(F32, False)
    half = L // 2
    lane = lax.broadcasted_iota(jnp.int32, (L, LANES), 1)

    @pl.loop(0, H // 8)
    def _(g):
        cols = pltpu.roll(total, lax.rem(LANES - 8 * g, LANES), 1)
        rows = tott_ref[0, pl.ds(pl.multiple_of(g * 8, 8), 8), :] * LOG2E
        for pair in range(4):
            at = tile_at(g * 4 + pair, LANES)
            both = vp_ref[:, at]
            top, low = 0.0, 0.0
            for odd in range(2):
                i = 2 * pair + odd
                mine = jnp.where((lane >= P_SIZE) == (odd == 1), both, jnp.zeros_like(both))
                col = cols[:, i : i + 1]
                row = rows[i : i + 1, :]
                p0 = jnp.exp2(jnp.minimum(col[:half] - row[:, :half], 0.0)) * gm[:half, :half]
                p1 = jnp.exp2(col[half:] - row[:, :half]) * gm[half:, :half]
                p2 = jnp.exp2(jnp.minimum(col[half:] - row[:, half:], 0.0)) * gm[half:, half:]
                top = top + dot(p0.astype(BF), mine[:half])
                low = low + dot(jnp.concatenate([p1.astype(BF), p2.astype(BF)], 1), mine)
            y_ref[0:half, at] = top
            y_ref[half:L, at] = low


def gate_kernel(
    count, cont, x_ref, dy_ref, normed_ref, inner_ref, y_ref, tot_ref, sloc_ref, sin_ref, gg_ref, sk_ref, *rest
):
    grefs, own_ref = rest[:count], rest[count]
    (out_ref, gn_ref, dgate_ref, dmix_ref, yd_ref, sc_ref, dlead_ref, sums_ref,
     e2, gate, gated, dn, etot, yfull, dlead, lead, wg, wo, gsems, osems) = rest[count + 1 :]
    b = pl.program_id(0)
    nb = pl.num_programs(0)

    @pl.when(b == 0)
    def _():
        place = cont[nb + 1], cont[nb + 2], count - 1
        part = DI // (count - 1)
        loads = copies_of(features(grefs, wg, part, *place), gsems)
        loads += copies_of(rows_behind(own_ref, grefs[1:], wo, part, *place), osems)
        for c in loads:
            c.start()
        e2[...] = head_spread()
        dlead[...] = jnp.zeros_like(dlead)
        sums_ref[...] = jnp.zeros_like(sums_ref)
        lead[...] = jnp.ones_like(lead)
        for c in loads:
            c.wait()

    keep = cont[b].astype(F32)
    first = cont[0].astype(F32)
    lead[...] = lead[...] * jnp.where(b == 0, 1.0, keep)
    normed = normed_ref[...]
    queries = inner_ref[:, DI + NS :]
    reach = split2(jnp.exp(tot_ref[...]))
    square = jnp.zeros((L, TILE), F32)
    for at in tiles(DI):
        g = across(normed, wg, at)
        gate[:, at] = g
        start = (sloc_ref[0, :, at].astype(F32) + (lead[0:1, at] * first) * sin_ref[:, at].astype(F32)).astype(BF)
        sc_ref[0, :, at] = start
        e = dot(reach, e2[:, at])
        etot[:, at] = e
        y = y_ref[:, at] + e * dot(queries, start)
        yfull[:, at] = y
        v = (y + sk_ref[:, at] * inner_ref[:, at].astype(F32)) * silu_and_slope(g)[0]
        gated[:, at] = v
        square = square + v * v
    rinv = lax.rsqrt(jnp.sum(square, 1, keepdims=True) * (1.0 / DI) + EPSILON)
    for at in tiles(DI):
        gn_ref[:, at] = (gated[:, at] * rinv * gg_ref[:, at]).astype(BF)
    dy = dy_ref[...]
    inner_sum = jnp.zeros((L, TILE), F32)
    for at in tiles(DI):
        back = across(dy, wo, at)
        v = gated[:, at]
        sums_ref[0:1, at] += jnp.sum(back * (v * rinv), 0, keepdims=True)
        back = back * gg_ref[:, at]
        dn[:, at] = back
        inner_sum = inner_sum + back * v
    for u, at in enumerate(tiles(D, wo.shape[2])):
        out_ref[:, at] = (x_ref[:, at].astype(F32) + dot(gn_ref[...], wo[u])).astype(BF)
    shared = jnp.sum(inner_sum, 1, keepdims=True) * (1.0 / DI) * (rinv * rinv * rinv)
    turned = queries.T
    yd = jnp.zeros((L, LANES), F32)
    for at in tiles(DI):
        dgated = rinv * dn[:, at] - gated[:, at] * shared
        s, slope = silu_and_slope(gate[:, at])
        y = yfull[:, at]
        v = inner_ref[:, at].astype(F32)
        dgate_ref[:, at] = (dgated * (y + sk_ref[:, at] * v) * slope).astype(BF)
        dmix = (dgated * s).astype(BF)
        dmix_ref[:, at] = dmix
        dmix = dmix.astype(F32)
        sums_ref[1:2, at] += jnp.sum(dmix * v, 0, keepdims=True)
        yd = yd + head_sum(dmix * y, e2, at)
        dlead[:, at] += lead[0:1, at] * dot(turned, (dmix * etot[:, at]).astype(BF))
    yd_ref[...] = yd
    lead[...] = lead[...] * etot[L - 1 : L, :]

    @pl.when(b == nb - 1)
    def _():
        dlead_ref[...] = dlead[...].astype(BF)


def back_kernel(
    cont, kq_ref, vp_ref, cs_ref, cin_ref, stp_ref, sig_ref, tot_ref, tott_ref, sc_ref, dmix_ref, yd_ref, din_ref,
    cw_ref, sp_ref, sk_ref, ch_ref,
    gp_ref, gph_ref, csum_ref, hsum_ref,
    dstate, e2, z, dbuf, gt, dgt, weight, sent, reached, ends, fine,
):
    nb = pl.num_programs(0)
    b = nb - 1 - pl.program_id(0)
    after = cont[b + 1].astype(F32)

    @pl.when(b == nb - 1)
    def _():
        e2[...] = head_spread()
        dstate[...] = din_ref[...].astype(F32)
        csum_ref[...] = jnp.zeros_like(csum_ref)
        hsum_ref[...] = jnp.zeros_like(hsum_ref)
        dbuf[:, L : L + 8, :] = jnp.zeros((CH // LANES, 8, LANES), F32)

    @pl.when(b < nb - 1)
    def _():
        dbuf[:, L : L + 8, :] = dbuf[:, 0:8, :] * after

    dstate[...] = dstate[...] * after
    step = stp_ref[...]
    total = tot_ref[...]
    last = total[L - 1 : L, :]
    keys = kq_ref[:, :NS]
    queries = kq_ref[:, NS:]
    gt[...] = dot(keys, queries, NT) * triangle(F32, True)
    dgt[...] = jnp.zeros_like(dgt)
    steps = split2(step)
    leaving = split2(jnp.exp(last - total))
    reach = split2(jnp.exp(total))
    kept = dot(split2(jnp.exp(jnp.broadcast_to(last, (8, LANES)))), e2[...])[0:1]

    turned = queries.T
    ended = dstate[...].astype(BF)

    def spread(i, at):
        z[:, at] = dot(keys, ended[:, at])
        weight[i % 2, 0] = dot(leaving, e2[:, at])
        weight[i % 2, 1] = dot(reach, e2[:, at])

    def reweigh(i, at):
        for u in range(TILE // LANES):
            summed = jnp.zeros((8, LANES), F32)
            for rows, lanes, _ in pieces_of(slice(at.start + u * LANES, at.start + (u + 1) * LANES)):
                within = slice(u * LANES, (u + 1) * LANES)
                w = weight[i % 2, 0, rows, within]
                scaled = w * z[rows, lanes]
                z[rows, lanes] = scaled
                v = vp_ref[rows, lanes].astype(F32)
                summed = summed + fold(v * scaled)
                sent[rows, lanes] = (v * w).astype(BF)
                reached[rows, lanes] = (dmix_ref[rows, lanes].astype(F32) * weight[i % 2, 1, rows, within]).astype(BF)
            ends[:, lanes] = summed

    staged(tiles(DI), spread, reweigh)
    dk = dot(sent[...], ended, NT)
    dq = dot(reached[...], sc_ref[0], NT)
    for at in tiles(DI):
        old = dstate[:, at] * kept[:, at]
        ends[:, at] += jnp.sum((old * sc_ref[0, :, at].astype(F32)).reshape(NS // 8, 8, TILE), 0)
        dstate[:, at] = old + dot(turned, reached[:, at])
    ends_hi = ends[...].astype(BF)
    ends_lo = (ends[...] - ends_hi.astype(F32)).astype(BF)
    at_end = dot(ends_hi, e2[0:LANES], NT) + dot(ends_lo, e2[0:LANES], NT)
    at_end = jnp.sum(at_end, 0, keepdims=True)
    scaled_total = total * LOG2E

    half = L // 2
    lane = lax.broadcasted_iota(jnp.int32, (L, LANES), 1)

    @pl.loop(0, H // 8)
    def _(g):
        cols = pltpu.roll(scaled_total, lax.rem(LANES - 8 * g, LANES), 1)
        rows = tott_ref[0, pl.ds(pl.multiple_of(g * 8, 8), 8), :] * LOG2E
        for pair in range(4):
            at = tile_at(g * 4 + pair, LANES)
            dy = dmix_ref[:, at]
            v = vp_ref[:, at]
            top = z[0:half, at]
            low = z[half:L, at]
            for odd in range(2):
                i = 2 * pair + odd
                mine = jnp.where((lane >= P_SIZE) == (odd == 1), dy, jnp.zeros_like(dy))
                col = cols[:, i : i + 1]
                row = rows[i : i + 1, :]
                e0 = jnp.exp2(jnp.minimum(row[:, :half] - col[:half], 0.0))
                e1 = jnp.exp2(row[:, half:] - col[:half])
                e2_ = jnp.exp2(jnp.minimum(row[:, half:] - col[half:], 0.0))
                p0 = (e0 * gt[:half, :half]).astype(BF)
                p1 = (e1 * gt[:half, half:]).astype(BF)
                p2 = (e2_ * gt[half:, half:]).astype(BF)
                top = top + dot(jnp.concatenate([p0, p1], 1), mine)
                low = low + dot(p2, mine[half:])
                d = dot(v[:half], mine, NT)
                dgt[:half, :half] += e0 * d[:, :half]
                dgt[:half, half:] += e1 * d[:, half:]
                dgt[half:, half:] += e2_ * dot(v[half:], mine[half:], NT)
            z[0:half, at] = top
            z[half:L, at] = low

    masked = (dgt[...] * triangle(F32, True)).astype(BF)
    dk = dk + dot(masked, queries)
    dq = dq + dot(masked, keys, TN)

    def respread(i, at):
        weight[i % 2, 0] = dot(steps, e2[:, at])

    def unwind(i, at):
        for rows, lanes, within in pieces_of(at):
            dvp = z[rows, lanes]
            p = dvp * vp_ref[rows, lanes].astype(F32)
            hi = p.astype(BF)
            fine[0, rows, lanes] = hi
            fine[1, rows, lanes] = (p - hi.astype(F32)).astype(BF)
            dv = weight[i % 2, 0, rows, within] * dvp + sk_ref[:, lanes] * dmix_ref[rows, lanes].astype(F32)
            dbuf[lanes.start // LANES, rows, :] = dv * cs_ref[rows, lanes].astype(F32)

    staged(tiles(DI), respread, unwind)
    own = dot(fine[0], e2[0:LANES], NT) + dot(fine[1], e2[0:LANES], NT)
    slope = cs_ref[:, DI:].astype(F32)
    dbuf[DI // LANES, 0:L, :] = dk * slope[:, :NS]
    dbuf[DI // LANES + 1, 0:L, :] = dq * slope[:, NS:]

    row = lax.broadcasted_iota(jnp.int32, (L, LANES), 0)
    dtotal = yd_ref[...] - own + jnp.where(row == L - 1, at_end, 0.0)
    drate = tri_sum(triangle(BF, True), dtotal)
    decay = sp_ref[1:2, :]
    dstep = own / jnp.maximum(step, 1e-30) - decay * drate
    draw = jnp.where(lax.broadcasted_iota(jnp.int32, (L, LANES), 1) < H, dstep * sig_ref[...], 0.0)
    gp_ref[:, CH : CH + LANES] = draw.astype(BF)
    if gp_ref.shape[1] > CH + LANES:
        gp_ref[:, CH + LANES :] = jnp.zeros((L, gp_ref.shape[1] - CH - LANES), BF)
    hsum_ref[0:1, :] += jnp.sum(draw, 0, keepdims=True)
    hsum_ref[1:2, :] += jnp.sum(-decay * step * drate, 0, keepdims=True)

    for lt in range(CH // LANES):
        at = slice(lt * LANES, (lt + 1) * LANES)
        sums = [jnp.zeros((8, LANES), F32) for _ in range(CONVW + 1)]
        for q in range(L // 64):
            lo = 64 * q
            here = dbuf[lt, lo : lo + 64, :]
            c = cin_ref[lo : lo + 64, at].astype(F32)
            acc = cw_ref[3:4, at] * here
            sums[3] = sums[3] + jnp.sum((here * c).reshape(8, 8, LANES), 0)
            sums[4] = sums[4] + jnp.sum(here.reshape(8, 8, LANES), 0)
            for ahead in range(1, CONVW):
                there = dbuf[lt, lo + ahead : lo + ahead + 64, :]
                acc = acc + cw_ref[3 - ahead : 4 - ahead, at] * there
                sums[3 - ahead] = sums[3 - ahead] + jnp.sum((there * c).reshape(8, 8, LANES), 0)
            gp_ref[lo : lo + 64, at] = acc.astype(BF)
        for k in range(CONVW + 1):
            csum_ref[k : k + 1, at] += jnp.sum(sums[k], 0, keepdims=True)

    @pl.when(b == 0)
    def _():
        gph_ref[...] = jnp.zeros_like(gph_ref)
        for lt in range(CH // LANES):
            at = slice(lt * LANES, (lt + 1) * LANES)
            d = dbuf[lt, 0:8, :] * cont[0].astype(F32)
            d0, d1, d2 = d[0:1], d[1:2], d[2:3]
            w0, w1, w2 = cw_ref[0:1, at], cw_ref[1:2, at], cw_ref[2:3, at]
            c5, c6, c7 = ch_ref[5:6, at], ch_ref[6:7, at], ch_ref[7:8, at]
            made = [jnp.zeros((13, LANES), F32), w0 * d0, w1 * d0 + w0 * d1, w2 * d0 + w1 * d1 + w0 * d2]
            gph_ref[:, at] = jnp.concatenate(made, 0).astype(BF)
            csum_ref[0:1, at] += c5 * d0 + c6 * d1 + c7 * d2
            csum_ref[1:2, at] += c6 * d0 + c7 * d1
            csum_ref[2:3, at] += c7 * d0


def wide_grad_kernel(cont, gn_ref, dy_ref, normed_ref, dgate_ref, out_ref):
    k = pl.program_id(0)
    reps, shards, _, m = out_ref.shape
    o = dot(gn_ref[...], dy_ref[...], TN).astype(BF)
    part = o.shape[0] // reps
    for r in range(reps):
        for u in range(D // m):
            out_ref[r, k, u * part : (u + 1) * part, :] = o[r * part : (r + 1) * part, u * m : (u + 1) * m]
    g = dot(dgate_ref[...], normed_ref[...], TN).astype(BF)
    first = D // m * part
    part = DI // reps
    each = g.shape[0] // part
    for i in range(each):
        for s in range(shards):
            out_ref[k * each + i, s, first:, :] = g[i * part : (i + 1) * part, s * m : (s + 1) * m]


def conv_grad_kernel(nb, other, cont, normed_ref, gp_ref, nh_ref, gph_ref, out_ref, turned, turned_halo):
    half, _, part, _ = out_ref.shape
    rep = cont[nb + 2]
    upper_half = lax.rem(rep, 2) ^ other
    base = half * part
    first = (base // LANES) * LANES
    width = 2 * base

    @pl.when(pl.program_id(0) == 0)
    def _():
        @pl.when(upper_half == 0)
        def _():
            end = base if base == first else first + LANES
            turned[...] = gp_ref[:, 0:end].T[0:base]
            turned_halo[...] = gph_ref[:, 0:end].T[0:base]

        @pl.when(upper_half == 1)
        def _():
            turned[...] = gp_ref[:, first:width].T[base - first :]
            turned_halo[...] = gph_ref[:, first:width].T[base - first :]

    full = (dot(turned[...], normed_ref[...]) + dot(turned_halo[...], nh_ref[...])).astype(BF)
    for chip in range(half):
        out_ref[(rep // 2) ^ chip, 0] = full[chip * part : (chip + 1) * part]


def input_grad_kernel(convs, gates, cont, x_ref, dy_ref, gp_ref, dgate_ref, ahead_ref, ng_ref, *rest):
    crefs, grefs = rest[:convs], rest[convs : convs + gates]
    gt_ref, gn_ref, wc, wg, csems, gsems, acc = rest[convs + gates :]
    b = pl.program_id(0)
    nb = pl.num_programs(0)

    @pl.when(b == 0)
    def _():
        place = cont[nb + 1], cont[nb + 2], convs - 1
        loads = copies_of(features(crefs, wc, wc.shape[1] // (convs - 1), *place), csems)
        loads += copies_of(features(grefs, wg, DI // (convs - 1), *place), gsems)
        for c in loads:
            c.start()
        gn_ref[...] = jnp.zeros_like(gn_ref)
        for c in loads:
            c.wait()

    m = wc.shape[2]
    for s, at in enumerate(tiles(D, m)):
        acc[:, at] = dot(gp_ref[...], wc[s]) + dot(dgate_ref[...], wg[s])

    @pl.when(b == nb - 1)
    def _():
        keep = cont[nb].astype(F32)
        for s, at in enumerate(tiles(D, m)):
            acc[L - 16 : L, at] += keep * dot(ahead_ref[...], wc[s])

    for q in range(L // 32):
        rows = slice(32 * q, 32 * q + 32)
        x = x_ref[rows].astype(F32)
        inv = lax.rsqrt(jnp.mean(x * x, 1, keepdims=True) + EPSILON)
        g = acc[rows]
        gn_ref[...] += jnp.sum((g * (x * inv)).reshape(4, 8, D), 0)
        v = g * ng_ref[...]
        mean = jnp.mean(v * x, 1, keepdims=True)
        gt_ref[rows] = (inv * v - x * (inv * inv * inv * mean) + dy_ref[rows].astype(F32)).astype(BF)


def finish_wide_kernel(cont, wide_ref, gin_ref, gout_ref, buf, sem):
    reps, rows, m = wide_ref.shape
    part = DI // reps
    for r in range(reps):
        buf[r * part : (r + 1) * part, :] = wide_ref[r, rows - part :, :].astype(F32)
    copy = pltpu.make_async_copy(buf, gin_ref.at[pl.ds(0, DI)], sem)
    copy.start()
    part = (rows - part) * m // D
    for r in range(reps):
        for u in range(D // m):
            block = wide_ref[r, u * part : (u + 1) * part, :]
            gout_ref[r * part : (r + 1) * part, u * m : (u + 1) * m] = block.astype(F32)
    copy.wait()


def finish_conv_kernel(nb, count, cont, *rest):
    pieces = rest[:count]
    gin_ref, buf, sem = rest[count + 1 :]
    part = pieces[0].shape[0]
    for i, piece in enumerate(pieces):
        place = slot_of(cont[nb + 2] ^ i, count)
        buf[pl.ds(pl.multiple_of(place * part, 16), part), :] = piece[...].astype(F32)
    copy = pltpu.make_async_copy(buf.at[pl.ds(0, CH + H)], gin_ref.at[pl.ds(DI, CH + H)], sem)
    copy.start()
    copy.wait()


def rows_of(width, reverse=0, column=0):
    if reverse:
        return pl.BlockSpec((L, width), lambda b, cont: (reverse - 1 - b, column))
    return pl.BlockSpec((L, width), lambda b, cont: (b, column))


def whole(*shape):
    return pl.BlockSpec(shape, lambda b, cont: (0,) * len(shape), pipeline_mode=pl.Buffered(1))


def fixed(*shape):
    return pl.BlockSpec(shape, lambda b, cont: (0,) * len(shape))


def lead_of(reverse, *shape):
    if reverse:
        return pl.BlockSpec((1, *shape), lambda b, cont: (reverse - 1 - b, 0, 0))
    return pl.BlockSpec((1, *shape), lambda b, cont: (b, 0, 0))


def anywhere(count):
    return [pl.BlockSpec(memory_space=pl.ANY)] * count


def call(kernel, grid, in_specs, out_specs, outs, scratch, flops, nbytes, name, aliases=None):
    return pl.pallas_call(
        kernel,
        grid_spec=pltpu.PrefetchScalarGridSpec(
            num_scalar_prefetch=1, grid=(grid,), in_specs=in_specs, out_specs=out_specs, scratch_shapes=scratch
        ),
        out_shape=[jax.ShapeDtypeStruct(s, d) for s, d in outs],
        input_output_aliases=aliases or {},
        compiler_params=pltpu.CompilerParams(vmem_limit_bytes=VMEM),
        cost_estimate=pl.CostEstimate(flops=flops, bytes_accessed=nbytes, transcendentals=0),
        name=name,
    )


def loaded(count, shards, *shape):
    return [pltpu.VMEM(shape, BF), pltpu.SemaphoreType.DMA((copy_count(count - 1, shards),))]


def front(cont, x, xh, ng, wc, cw, sp, shards):
    rows = x.shape[0]
    nb = rows // L
    count = len(wc)
    return call(
        partial(front_kernel, count), nb,
        [rows_of(D), whole(16, D), whole(1, D), whole(8, CH), whole(8, LANES), *anywhere(count)],
        [rows_of(D), rows_of(CH), rows_of(DI), rows_of(CH), rows_of(CH), rows_of(LANES), rows_of(LANES), rows_of(LANES),
         lead_of(0, LANES, L), lead_of(0, NS, DI), fixed(NS, DI), fixed(16, D), fixed(8, CH)],
        [((rows, D), BF), ((rows, CH), BF), ((rows, DI), BF), ((rows, CH), BF), ((rows, CH), BF), ((rows, LANES), F32),
         ((rows, LANES), F32), ((rows, LANES), F32), ((nb, LANES, L), F32), ((nb, NS, DI), BF), ((NS, DI), BF),
         ((16, D), BF), ((8, CH), F32)],
        [pltpu.VMEM((CH // LANES, L + 8, LANES), F32), pltpu.VMEM((NS, DI), F32), pltpu.VMEM((2 * LANES, DI), BF),
         pltpu.VMEM((L, DI), BF), pltpu.VMEM((2, 2, L, TILE), F32), *loaded(count, shards, shards, *wc[0].shape)],
        20_000_000_000, 24 << 20, "front",
    )(cont, x, xh, ng, cw, sp, *wc)


def scan(cont, inner, vp, tot, tott):
    rows = inner.shape[0]
    nb = rows // L
    return call(
        scan_kernel, nb,
        [rows_of(2 * NS, 0, DI // (2 * NS)), rows_of(DI), rows_of(LANES), lead_of(0, LANES, L)],
        [rows_of(DI)],
        [((rows, DI), F32)],
        [pltpu.VMEM((L, L), F32)],
        30_000_000_000, 16 << 20, "scan",
    )(cont, inner, vp, tot, tott)[0]


def gating(cont, x, dy, normed, inner, y, tot, sloc, sin, wg, wo_own, gg, sk, shards):
    rows = x.shape[0]
    nb = rows // L
    count = len(wg)
    wide = pltpu.VMEM((L, DI), F32)
    return call(
        partial(gate_kernel, count), nb,
        [rows_of(D), rows_of(D), rows_of(D), rows_of(CH), rows_of(DI), rows_of(LANES), lead_of(0, NS, DI), whole(NS, DI),
         whole(1, DI), whole(1, DI), *anywhere(count + 1)],
        [rows_of(D), rows_of(DI), rows_of(DI), rows_of(DI), rows_of(LANES), lead_of(0, NS, DI), fixed(NS, DI),
         fixed(8, DI)],
        [((rows, D), BF), ((rows, DI), BF), ((rows, DI), BF), ((rows, DI), BF), ((rows, LANES), F32),
         ((nb, NS, DI), BF), ((NS, DI), BF), ((8, DI), F32)],
        [pltpu.VMEM((2 * LANES, DI), BF), wide, wide, wide, wide, wide,
         pltpu.VMEM((NS, DI), F32), pltpu.VMEM((1, DI), F32), pltpu.VMEM((shards, *wg[0].shape), BF),
         pltpu.VMEM((wo_own.shape[0], DI, wo_own.shape[2]), BF),
         pltpu.SemaphoreType.DMA((copy_count(count - 1, shards),)),
         pltpu.SemaphoreType.DMA((copy_count(count - 1, shards, shards),))],
        35_000_000_000, 40 << 20, "gating",
    )(cont, x, dy, normed, inner, y, tot, sloc, sin, gg, sk, *wg, wo_own)


def back(cont, inner, vp, cs, cin, stp, sig, tot, tott, sc, dmix, yd, din, cw, sp, sk, ch, width):
    rows = inner.shape[0]
    nb = rows // L
    return call(
        back_kernel, nb,
        [rows_of(2 * NS, nb, DI // (2 * NS)), rows_of(DI, nb), rows_of(CH, nb), rows_of(CH, nb), rows_of(LANES, nb),
         rows_of(LANES, nb), rows_of(LANES, nb), lead_of(nb, LANES, L), lead_of(nb, NS, DI), rows_of(DI, nb),
         rows_of(LANES, nb), whole(NS, DI), whole(8, CH), whole(8, LANES), whole(1, DI), whole(8, CH)],
        [rows_of(width, nb), fixed(16, width), fixed(8, CH), fixed(8, LANES)],
        [((rows, width), BF), ((16, width), BF), ((8, CH), F32), ((8, LANES), F32)],
        [pltpu.VMEM((NS, DI), F32), pltpu.VMEM((2 * LANES, DI), BF), pltpu.VMEM((L, DI), F32),
         pltpu.VMEM((CH // LANES, L + 8, LANES), F32), pltpu.VMEM((L, L), F32), pltpu.VMEM((L, L), F32),
         pltpu.VMEM((2, 2, L, TILE), F32), pltpu.VMEM((L, DI), BF), pltpu.VMEM((L, DI), BF), pltpu.VMEM((8, DI), F32),
         pltpu.VMEM((2, L, DI), BF)],
        60_000_000_000, 30 << 20, "back",
    )(cont, inner, vp, cs, cin, stp, sig, tot, tott, sc, dmix, yd, din, cw, sp, sk, ch)


def wide_grad(cont, gn, dy, normed, dgate, reps, shards):
    rows = dy.shape[0]
    block = DI // shards
    shape = (reps, shards, 2 * DI // reps, D // shards)
    return call(
        wide_grad_kernel, shards,
        [pl.BlockSpec((rows, block), lambda k, c: (0, k)), whole(rows, D), whole(rows, D),
         pl.BlockSpec((rows, block), lambda k, c: (0, k))],
        [fixed(*shape)],
        [(shape, BF)],
        [], 8_600_000_000, 24 << 20, "wide_grad",
    )(cont, gn, dy, normed, dgate)[0]


def conv_grad(cont, normed, gp, nh, gph, reps, shards, other):
    rows, width = gp.shape
    nb = rows // L
    m = D // shards
    part = width // reps
    half = width // 2
    return call(
        partial(conv_grad_kernel, nb, other), shards,
        [pl.BlockSpec((rows, m), lambda k, c: (0, c[nb + 1] ^ k)), whole(rows, width),
         pl.BlockSpec((16, m), lambda k, c: (0, c[nb + 1] ^ k)), whole(16, width)],
        [pl.BlockSpec((reps // 2, 1, part, m), lambda k, c: (0, k, 0, 0))],
        [((reps // 2, shards, part, m), BF)],
        [pltpu.VMEM((half, rows), BF), pltpu.VMEM((half, 16), BF)],
        5_000_000_000, 12 << 20, "conv_grad",
    )(cont, normed, gp, nh, gph)[0]


def input_grad(cont, x, dy, gp, dgate, ahead, ng, wc, wg, shards):
    rows, width = gp.shape
    nb = rows // L
    convs, gates = len(wc), len(wg)
    return call(
        partial(input_grad_kernel, convs, gates), nb,
        [rows_of(D), rows_of(D), rows_of(width), rows_of(DI), whole(16, width), whole(1, D), *anywhere(convs + gates)],
        [rows_of(D), fixed(8, D)],
        [((rows, D), BF), ((8, D), F32)],
        [pltpu.VMEM((shards, *wc[0].shape), BF), pltpu.VMEM((shards, *wg[0].shape), BF),
         pltpu.SemaphoreType.DMA((copy_count(convs - 1, shards),)), pltpu.SemaphoreType.DMA((copy_count(gates - 1, shards),)),
         pltpu.VMEM((L, D), F32)],
        10_000_000_000, 24 << 20, "input_grad",
    )(cont, x, dy, gp, dgate, ahead, ng, *wc, *wg)


def finish_wide(cont, wide):
    reps, rows, m = wide.shape
    shards = D // m
    return call(
        finish_wide_kernel, 1,
        [whole(*wide.shape)],
        [pl.BlockSpec(memory_space=pl.ANY), fixed(DI // shards, D)],
        [((DI + CH + H, m), F32), ((DI // shards, D), F32)],
        [pltpu.VMEM((DI, m), F32), pltpu.SemaphoreType.DMA],
        1_000_000, 8 << 20, "finish_wide",
    )(cont, wide)


def finish_conv(cont, nb, pieces, gin):
    part, m = pieces[0].shape
    count = len(pieces)
    return call(
        partial(finish_conv_kernel, nb, count), 1,
        [*[whole(part, m)] * count, pl.BlockSpec(memory_space=pl.ANY)],
        [pl.BlockSpec(memory_space=pl.ANY)],
        [(gin.shape, F32)],
        [pltpu.VMEM((count * part, m), F32), pltpu.SemaphoreType.DMA],
        1_000_000, 5 << 20, "finish_conv", {1 + count: 0},
    )(cont, *pieces, gin)[0]


def shift(v, by):
    n = lax.axis_size(BOTH)
    return lax.ppermute(v, BOTH, [(i, (i + by) % n) for i in range(n)])


def swap(v, mask):
    n = lax.axis_size(BOTH)
    return lax.ppermute(v, BOTH, [(i, i ^ mask) for i in range(n)])


def part_of(w):
    reps = lax.axis_size("rep")
    part = w.shape[0] // reps
    return lax.dynamic_slice(w, (slot_of(lax.axis_index("rep"), reps) * part, 0), (part, w.shape[1]))


def over_reps(column):
    reps, shards = lax.axis_size("rep"), lax.axis_size("shard")
    return [column] + [swap(column, 2 * shards * j) for j in range(1, reps // 2)]


def over_cores(plane):
    shards = lax.axis_size("shard")
    other = [swap(v, shards) for v in plane]
    return [v for pair in zip(plane, other) for v in pair]


def after(value, *first):
    return lax.optimization_barrier((value, first))[0]


def total_of(first, *others):
    out = first.astype(F32)
    for v in others:
        out = out + v.astype(F32)
    return out.astype(first.dtype)


def reduce_small(v):
    reps, shards = lax.axis_size("rep"), lax.axis_size("shard")
    mine = lax.axis_index("shard")

    def row(k):
        return lax.dynamic_slice(v, (mine ^ k, 0), (1, v.shape[1]))

    out = row(0)
    for got in [swap(row(k), k) for k in range(1, shards)]:
        out = out + got
    hop = shards
    while hop < shards * reps:
        out = out + swap(out, hop)
        hop *= 2
    return out[0]


def local(
    tokens, cotangent, seq_lengths, deal_order, norm_gain, in_proj, conv_weight, conv_bias, step_bias, decay_log,
    skip_gain, gate_gain, out_proj,
):
    n = lax.axis_size(BOTH)
    me = lax.axis_index(BOTH)
    reps, shards = lax.axis_size("rep"), lax.axis_size("shard")
    rep, mine = lax.axis_index("rep"), lax.axis_index("shard")
    rows = tokens.shape[0]
    nb = rows // L
    unit = lcm(LANES, 16 * reps)
    width = -(-(CH + LANES) // unit) * unit

    seqs = seq_lengths.shape[0]
    order = jnp.arange(seqs, dtype=jnp.int32)
    starts = jnp.sum(jnp.where(order[None, :] < order[:, None], seq_lengths[None, :], 0), 1)
    edge = (me * nb + jnp.arange(nb + 1, dtype=jnp.int32)) * L
    cont = jnp.where(jnp.any(starts[None, :] == edge[:, None], 1) | (edge >= n * rows), 0, 1)
    cont = jnp.concatenate([cont.astype(jnp.int32), jnp.stack([mine, rep]).astype(jnp.int32)])

    turned = in_proj.T
    wcs = jnp.pad(turned[DI:], ((0, width - CH - H), (0, 0)))
    wgs = turned[:DI]
    m = wcs.shape[1]
    small = jnp.concatenate(
        [conv_weight.reshape(-1), conv_bias, gate_gain, norm_gain, step_bias, decay_log, skip_gain]
    )
    extra = -(-small.size // (16 * m)) * 16
    extra = jnp.pad(small, (0, extra * m - small.size)).reshape(extra, m)
    piece = jnp.concatenate([part_of(wcs), extra], 0)
    part = width // reps
    column = [swap(piece, k) for k in range(1, shards)]
    small = jnp.stack([small] + [v[part:].reshape(-1)[: small.size] for v in column])
    conv_column = jnp.stack([v[:part] for v in column])
    halo = shift(tokens[rows - 16 :], 1)
    out_part = part_of(out_proj)
    piece = jnp.concatenate([part_of(wgs)] + [out_part[:, at] for at in tiles(D, m)], 0)
    wo_own = jnp.stack([out_proj[:, at] for at in tiles(D, m)])
    gate_column = lax.all_gather(piece, "shard", axis=0)
    gate_column = jnp.take(gate_column, mine ^ jnp.arange(1, shards), axis=0)
    small = jnp.take(small, mine ^ jnp.arange(shards), axis=0).astype(F32)
    sizes = [conv_weight.size, conv_bias.size, gate_gain.size, norm_gain.size, step_bias.size, decay_log.size,
             skip_gain.size]
    parts, at = [], 0
    for size in sizes:
        parts.append(small[:, at : at + size])
        at += size
    taps = parts[0].reshape(shards, CONVW, -1).transpose(1, 0, 2).reshape(CONVW, CH)
    cw = jnp.concatenate([taps, parts[1].reshape(1, CH), jnp.zeros((3, CH), F32)], 0)
    gg = parts[2].reshape(1, DI)
    ng = parts[3].reshape(1, D)
    rate_scale = jnp.exp(parts[5].reshape(1, H))
    sp = jnp.pad(jnp.concatenate([parts[4].reshape(1, H), rate_scale], 0), ((0, 6), (0, LANES - H)))
    sk = jnp.repeat(parts[6].reshape(1, H), P_SIZE, axis=1)

    conv_plane = over_reps(conv_column)
    wc = [wcs, *over_cores(conv_plane)]
    wg = [wgs, *over_cores(over_reps(after(gate_column, conv_plane)))]

    normed, inner, vp, cs, cin, stp, sig, tot, tott, sloc, fin, nh, ch = front(cont, tokens, halo, ng, wc, cw, sp, shards)
    sin = shift(fin, 1)
    y = scan(cont, inner, vp, tot, tott)
    output, gn, dgate, dmix, yd, sc, dlead, sums = gating(
        cont, tokens, cotangent, normed, inner, y, tot, sloc, sin, wg, wo_own, gg, sk, shards
    )
    din = shift(dlead, -1)
    wide = after(wide_grad(cont, gn, cotangent, normed, dgate, reps, shards), din)
    wide = lax.psum_scatter(wide, "rep", scatter_dimension=0, tiled=True)[0]
    gp, gph, csum, hsum = back(cont, inner, vp, cs, cin, stp, sig, tot, tott, sc, dmix, yd, din, cw, sp, sk, ch, width)

    theirs = swap(conv_grad(cont, normed, gp, nh, gph, reps, shards, 1), shards)
    w = conv_grad(cont, normed, gp, nh, gph, reps, shards, 0)
    w = [total_of(w[j], theirs[j]) for j in range(reps // 2)]
    gp, wide, gph = after((gp, wide, gph), w)
    wide = lax.psum_scatter(wide, "shard", scatter_dimension=0, tiled=True)[0]
    ahead = shift(gph, -1)
    grad_tokens, grad_norm = input_grad(cont, tokens, cotangent, gp, dgate, ahead, ng, wc, wg, shards)
    others = [swap(w[j], 2 * shards * j) for j in range(1, reps // 2)]
    others, wide, grad_norm = lax.optimization_barrier((others, wide, grad_norm))
    w = total_of(w[0], *others)
    wide = lax.all_gather(wide, "rep", axis=0)
    w = total_of(w[0], *[swap(w[k], k) for k in range(1, shards)])
    pieces = over_cores(over_reps(w))
    gin, grad_out = finish_wide(cont, wide)
    grad_in = finish_conv(cont, nb, pieces, gin).T

    packed = jnp.concatenate(
        [csum[0:CONVW].reshape(CONVW, shards, -1).transpose(1, 0, 2).reshape(shards, -1), csum[4].reshape(shards, -1),
         sums[0].reshape(shards, -1), grad_norm.sum(0).reshape(shards, -1), hsum[0, :H].reshape(shards, -1),
         hsum[1, :H].reshape(shards, -1), sums[1].reshape(H, P_SIZE).sum(1).reshape(shards, -1)], 1)
    own = reduce_small(packed)
    got, at = [], 0
    for size in sizes:
        got.append(own[at : at + size])
        at += size
    return (
        output, grad_tokens, got[3], grad_in, got[0].reshape(CONVW, -1), got[1], got[4], got[5], got[6], got[2],
        grad_out,
    )


def solution(mesh):
    both = P(BOTH, None)
    in_specs = (
        both, both, P(), P(), P("shard"), P("shard", None), P(None, "shard"), P("shard"), P("shard"), P("shard"),
        P("shard"), P("shard"), P("shard", None),
    )
    out_specs = (
        both, both, P("shard"), P("shard", None), P(None, "shard"), P("shard"), P("shard"), P("shard"), P("shard"),
        P("shard"), P("shard", None),
    )
    return jax.shard_map(local, mesh=mesh, in_specs=in_specs, out_specs=out_specs, check_vma=False)
```

```python
from functools import partial
from math import lcm

import jax
import jax.numpy as jnp
from jax import lax
from jax.experimental import pallas as pl
from jax.experimental.pallas import tpu as pltpu
from jax.sharding import PartitionSpec as P

D = 1024
DI = 2048
H = 32
P_SIZE = 64
NS = 128
CONVW = 4
CH = DI + 2 * NS
L = 256
LANES = 128
TILE = 256
EPSILON = 1e-05
LOG2E = 1.4426950408889634
VMEM = 58 << 20
F32 = jnp.float32
BF = jnp.bfloat16
NN = (((1,), (0,)), ((), ()))
NT = (((1,), (1,)), ((), ()))
TN = (((0,), (0,)), ((), ()))
BOTH = ("rep", "shard")


def dot(a, b, dims=NN):
    return lax.dot_general(a, b, dims, preferred_element_type=F32)


def sigmoid(v):
    return 0.5 * jnp.tanh(0.5 * v) + 0.5


def silu_and_slope(v):
    half = 0.5 * v
    bent = jnp.tanh(half)
    part = half * bent
    return half + part, (0.5 + 0.5 * bent) * (1.0 + half - part)


def split2(v):
    hi = v.astype(BF)
    return jnp.concatenate([hi, (v - hi.astype(F32)).astype(BF)], 1)


def tri_sum(tri, v):
    hi = v.astype(BF)
    rest = v - hi.astype(F32)
    mid = rest.astype(BF)
    low = (rest - mid.astype(F32)).astype(BF)
    got = dot(tri, jnp.concatenate([hi, mid, low], 1))
    return got[:, :LANES] + got[:, LANES : 2 * LANES] + got[:, 2 * LANES :]


def head_spread():
    row = lax.broadcasted_iota(jnp.int32, (2 * LANES, DI), 0)
    col = lax.broadcasted_iota(jnp.int32, (2 * LANES, DI), 1)
    return jnp.where((row % LANES) == col // P_SIZE, 1.0, 0.0).astype(BF)


def head_sum(v, e2, at):
    hi = v.astype(BF)
    low = (v - hi.astype(F32)).astype(BF)
    return dot(hi, e2[0:LANES, at], NT) + dot(low, e2[0:LANES, at], NT)


def triangle(kind, up):
    row = lax.broadcasted_iota(jnp.int32, (L, L), 0)
    col = lax.broadcasted_iota(jnp.int32, (L, L), 1)
    return jnp.where(row <= col if up else row >= col, 1.0, 0.0).astype(kind)


def tile_at(t, size=TILE):
    return pl.ds(pl.multiple_of(t * size, size), size)


def tiles(width, size=TILE):
    return [slice(t, t + size) for t in range(0, width, size)]


STEP = 64


def pieces_of(at):
    for lanes in range(at.start, at.stop, LANES):
        for q in range(0, L, STEP):
            yield slice(q, q + STEP), slice(lanes, lanes + LANES), slice(lanes - at.start, lanes - at.start + LANES)


def fold(v):
    return jnp.sum(v.reshape(STEP // 8, 8, LANES), 0)


def staged(parts, first, then):
    first(0, parts[0])
    for i, part in enumerate(parts):
        if i + 1 < len(parts):
            first(i + 1, parts[i + 1])
        then(i, part)


def slot_of(rep, reps):
    return lax.rem(rep, 2) * (reps // 2) + rep // 2


def span(first, size):
    return pl.ds(pl.multiple_of(first, 16), size)


def features(refs, place, part, shard, rep, reps):
    made = [(refs[0], place.at[shard])]
    for i, ref in enumerate(refs[1:]):
        first = slot_of(rep ^ i, reps) * part
        for k in range(1, ref.shape[0] + 1):
            source = ref.at[k - 1] if part == ref.shape[1] else ref.at[k - 1, pl.ds(0, part)]
            made.append((source, place.at[shard ^ k, span(first, part)]))
    return made


def rows_behind(own, refs, place, skip, shard, rep, reps):
    groups, n, _ = own.shape
    part = n // reps
    made = [(own.at[u], place.at[u, span(shard * n, n)]) for u in range(groups)]
    for i, ref in enumerate(refs):
        first = slot_of(rep ^ i, reps) * part
        for k in range(1, ref.shape[0] + 1):
            for u in range(groups):
                source = ref.at[k - 1, pl.ds(skip + u * part, part)]
                made.append((source, place.at[u, span((shard ^ k) * n + first, part)]))
    return made


def across(a, w, rows):
    m = w.shape[2]
    out = dot(a[:, 0:m], w[0, rows], NT)
    for s in range(1, w.shape[0]):
        out = out + dot(a[:, s * m : (s + 1) * m], w[s, rows], NT)
    return out


def copies_of(made, sems):
    return [pltpu.make_async_copy(source, place, sems.at[i]) for i, (source, place) in enumerate(made)]


def copy_count(reps, shards, each=1):
    return each + reps * (shards - 1) * each


def rms(x, gain):
    xf = x.astype(F32)
    inv = lax.rsqrt(jnp.mean(xf * xf, 1, keepdims=True) + EPSILON)
    return (xf * inv * gain).astype(BF)


def front_kernel(count, cont, x_ref, xh_ref, ng_ref, cw_ref, sp_ref, *rest):
    wrefs = rest[:count]
    (normed_ref, inner_ref, vp_ref, cs_ref, cin_ref, stp_ref, sig_ref, tot_ref, tott_ref, sloc_ref, fin_ref, nh_ref, ch_ref,
     cbuf, state, e2, part, weight, wc, sems) = rest[count:]
    b = pl.program_id(0)
    nb = pl.num_programs(0)
    gain = ng_ref[...]

    @pl.when(b == 0)
    def _():
        loads = copies_of(features(wrefs, wc, wc.shape[1] // (count - 1), cont[nb + 1], cont[nb + 2], count - 1), sems)
        for c in loads:
            c.start()
        e2[...] = head_spread()
        state[...] = jnp.zeros_like(state)
        halo = rms(xh_ref[...], gain)
        nh_ref[...] = jnp.zeros_like(nh_ref)
        nh_ref[0:16] = halo
        for c in loads:
            c.wait()
        for at in tiles(CH):
            c = across(halo, wc, at)[8:16]
            ch_ref[:, at] = c
            for u in range(TILE // LANES):
                cbuf[at.start // LANES + u, 0:8, :] = c[:, u * LANES : (u + 1) * LANES]

    @pl.when(b > 0)
    def _():
        cbuf[:, 0:8, :] = cbuf[:, L : L + 8, :]

    keep = cont[b].astype(F32)
    cbuf[:, 0:8, :] = cbuf[:, 0:8, :] * keep
    normed = rms(x_ref[...], gain)
    normed_ref[...] = normed

    raw = across(normed, wc, slice(CH, CH + LANES)) + sp_ref[0:1, :]
    small = jnp.exp(-jnp.abs(raw))
    series = small * (1.0 - small * (0.5 - small * (1.0 / 3.0)))
    step = jnp.maximum(raw, 0.0) + jnp.where(small < 0.01, series, jnp.log(1.0 + small))
    rate = -sp_ref[1:2, :] * step
    total = tri_sum(triangle(BF, False), rate)
    stp_ref[...] = step
    sig_ref[...] = sigmoid(raw)
    tot_ref[...] = total
    tott_ref[0] = total.T
    last = total[L - 1 : L, :]
    steps = split2(step)
    leaving = split2(jnp.exp(last - total))
    kept = dot(split2(jnp.exp(jnp.broadcast_to(last, (8, LANES)))), e2[...])[0:1]
    state[...] = state[...] * keep
    sloc_ref[0] = state[...].astype(BF)

    def project(i, at):
        c = across(normed, wc, at)
        for u in range(TILE // LANES):
            cbuf[at.start // LANES + u, 8 : L + 8, :] = c[:, u * LANES : (u + 1) * LANES]
        if at.start < DI:
            weight[i % 2, 0] = dot(steps, e2[:, at])
            weight[i % 2, 1] = dot(leaving, e2[:, at])

    def convolve(i, at):
        for rows, lanes, within in pieces_of(at):
            lo = 8 + rows.start
            buf = cbuf.at[lanes.start // LANES]
            here = buf[lo : lo + STEP, :]
            cin_ref[rows, lanes] = here.astype(BF)
            acc = cw_ref[4:5, lanes] + cw_ref[3:4, lanes] * here
            for back in range(1, CONVW):
                acc = acc + cw_ref[3 - back : 4 - back, lanes] * buf[lo - back : lo - back + STEP, :]
            v, slope = silu_and_slope(acc)
            cs_ref[rows, lanes] = slope.astype(BF)
            inner_ref[rows, lanes] = v.astype(BF)
            if at.start < DI:
                v = v * weight[i % 2, 0, rows, within]
                vp_ref[rows, lanes] = v.astype(BF)
                part[rows, lanes] = (v * weight[i % 2, 1, rows, within]).astype(BF)

    staged([slice(DI, CH)] + tiles(DI), project, convolve)
    keys = inner_ref[:, DI : DI + NS].T
    for at in tiles(DI):
        state[:, at] = state[:, at] * kept[:, at] + dot(keys, part[:, at])

    @pl.when(b == nb - 1)
    def _():
        fin_ref[...] = state[...].astype(BF)


def scan_kernel(cont, kq_ref, vp_ref, tot_ref, tott_ref, y_ref, gm):
    total = tot_ref[...] * LOG2E
    keys = kq_ref[:, :NS]
    queries = kq_ref[:, NS:]
    gm[...] = dot(queries, keys, NT) * triangle(F32, False)
    half = L // 2
    lane = lax.broadcasted_iota(jnp.int32, (L, LANES), 1)

    @pl.loop(0, H // 8)
    def _(g):
        cols = pltpu.roll(total, lax.rem(LANES - 8 * g, LANES), 1)
        rows = tott_ref[0, pl.ds(pl.multiple_of(g * 8, 8), 8), :] * LOG2E
        for pair in range(4):
            at = tile_at(g * 4 + pair, LANES)
            both = vp_ref[:, at]
            top, low = 0.0, 0.0
            for odd in range(2):
                i = 2 * pair + odd
                mine = jnp.where((lane >= P_SIZE) == (odd == 1), both, jnp.zeros_like(both))
                col = cols[:, i : i + 1]
                row = rows[i : i + 1, :]
                p0 = jnp.exp2(jnp.minimum(col[:half] - row[:, :half], 0.0)) * gm[:half, :half]
                p1 = jnp.exp2(col[half:] - row[:, :half]) * gm[half:, :half]
                p2 = jnp.exp2(jnp.minimum(col[half:] - row[:, half:], 0.0)) * gm[half:, half:]
                top = top + dot(p0.astype(BF), mine[:half])
                low = low + dot(jnp.concatenate([p1.astype(BF), p2.astype(BF)], 1), mine)
            y_ref[0:half, at] = top
            y_ref[half:L, at] = low


def gate_kernel(
    count, cont, x_ref, dy_ref, normed_ref, inner_ref, y_ref, tot_ref, sloc_ref, sin_ref, gg_ref, sk_ref, *rest
):
    grefs, own_ref = rest[:count], rest[count]
    (out_ref, gn_ref, dgate_ref, dmix_ref, yd_ref, sc_ref, dlead_ref, sums_ref,
     e2, gate, gated, dn, etot, yfull, dlead, lead, wg, wo, gsems, osems) = rest[count + 1 :]
    b = pl.program_id(0)
    nb = pl.num_programs(0)

    @pl.when(b == 0)
    def _():
        place = cont[nb + 1], cont[nb + 2], count - 1
        part = DI // (count - 1)
        loads = copies_of(features(grefs, wg, part, *place), gsems)
        loads += copies_of(rows_behind(own_ref, grefs[1:], wo, part, *place), osems)
        for c in loads:
            c.start()
        e2[...] = head_spread()
        dlead[...] = jnp.zeros_like(dlead)
        sums_ref[...] = jnp.zeros_like(sums_ref)
        lead[...] = jnp.ones_like(lead)
        for c in loads:
            c.wait()

    keep = cont[b].astype(F32)
    first = cont[0].astype(F32)
    lead[...] = lead[...] * jnp.where(b == 0, 1.0, keep)
    normed = normed_ref[...]
    queries = inner_ref[:, DI + NS :]
    reach = split2(jnp.exp(tot_ref[...]))
    square = jnp.zeros((L, TILE), F32)
    for at in tiles(DI):
        g = across(normed, wg, at)
        gate[:, at] = g
        start = (sloc_ref[0, :, at].astype(F32) + (lead[0:1, at] * first) * sin_ref[:, at].astype(F32)).astype(BF)
        sc_ref[0, :, at] = start
        e = dot(reach, e2[:, at])
        etot[:, at] = e
        y = y_ref[:, at] + e * dot(queries, start)
        yfull[:, at] = y
        v = (y + sk_ref[:, at] * inner_ref[:, at].astype(F32)) * silu_and_slope(g)[0]
        gated[:, at] = v
        square = square + v * v
    rinv = lax.rsqrt(jnp.sum(square, 1, keepdims=True) * (1.0 / DI) + EPSILON)
    for at in tiles(DI):
        gn_ref[:, at] = (gated[:, at] * rinv * gg_ref[:, at]).astype(BF)
    dy = dy_ref[...]
    inner_sum = jnp.zeros((L, TILE), F32)
    for at in tiles(DI):
        back = across(dy, wo, at)
        v = gated[:, at]
        sums_ref[0:1, at] += jnp.sum(back * (v * rinv), 0, keepdims=True)
        back = back * gg_ref[:, at]
        dn[:, at] = back
        inner_sum = inner_sum + back * v
    for u, at in enumerate(tiles(D, wo.shape[2])):
        out_ref[:, at] = (x_ref[:, at].astype(F32) + dot(gn_ref[...], wo[u])).astype(BF)
    shared = jnp.sum(inner_sum, 1, keepdims=True) * (1.0 / DI) * (rinv * rinv * rinv)
    turned = queries.T
    yd = jnp.zeros((L, LANES), F32)
    for at in tiles(DI):
        dgated = rinv * dn[:, at] - gated[:, at] * shared
        s, slope = silu_and_slope(gate[:, at])
        y = yfull[:, at]
        v = inner_ref[:, at].astype(F32)
        dgate_ref[:, at] = (dgated * (y + sk_ref[:, at] * v) * slope).astype(BF)
        dmix = (dgated * s).astype(BF)
        dmix_ref[:, at] = dmix
        dmix = dmix.astype(F32)
        sums_ref[1:2, at] += jnp.sum(dmix * v, 0, keepdims=True)
        yd = yd + head_sum(dmix * y, e2, at)
        dlead[:, at] += lead[0:1, at] * dot(turned, (dmix * etot[:, at]).astype(BF))
    yd_ref[...] = yd
    lead[...] = lead[...] * etot[L - 1 : L, :]

    @pl.when(b == nb - 1)
    def _():
        dlead_ref[...] = dlead[...].astype(BF)


def back_kernel(
    cont, kq_ref, vp_ref, cs_ref, cin_ref, stp_ref, sig_ref, tot_ref, tott_ref, sc_ref, dmix_ref, yd_ref, din_ref,
    cw_ref, sp_ref, sk_ref, ch_ref,
    gp_ref, turned_ref, gph_ref, turned_halo_ref, csum_ref, hsum_ref,
    dstate, e2, z, dbuf, gt, dgt, weight, sent, reached, ends, fine,
):
    nb = pl.num_programs(0)
    b = nb - 1 - pl.program_id(0)
    after = cont[b + 1].astype(F32)

    @pl.when(b == nb - 1)
    def _():
        e2[...] = head_spread()
        dstate[...] = din_ref[...].astype(F32)
        csum_ref[...] = jnp.zeros_like(csum_ref)
        hsum_ref[...] = jnp.zeros_like(hsum_ref)
        dbuf[:, L : L + 8, :] = jnp.zeros((CH // LANES, 8, LANES), F32)

    @pl.when(b < nb - 1)
    def _():
        dbuf[:, L : L + 8, :] = dbuf[:, 0:8, :] * after

    dstate[...] = dstate[...] * after
    step = stp_ref[...]
    total = tot_ref[...]
    last = total[L - 1 : L, :]
    keys = kq_ref[:, :NS]
    queries = kq_ref[:, NS:]
    gt[...] = dot(keys, queries, NT) * triangle(F32, True)
    dgt[...] = jnp.zeros_like(dgt)
    steps = split2(step)
    leaving = split2(jnp.exp(last - total))
    reach = split2(jnp.exp(total))
    kept = dot(split2(jnp.exp(jnp.broadcast_to(last, (8, LANES)))), e2[...])[0:1]

    turned = queries.T
    ended = dstate[...].astype(BF)

    def spread(i, at):
        z[:, at] = dot(keys, ended[:, at])
        weight[i % 2, 0] = dot(leaving, e2[:, at])
        weight[i % 2, 1] = dot(reach, e2[:, at])

    def reweigh(i, at):
        for u in range(TILE // LANES):
            summed = jnp.zeros((8, LANES), F32)
            for rows, lanes, _ in pieces_of(slice(at.start + u * LANES, at.start + (u + 1) * LANES)):
                within = slice(u * LANES, (u + 1) * LANES)
                w = weight[i % 2, 0, rows, within]
                scaled = w * z[rows, lanes]
                z[rows, lanes] = scaled
                v = vp_ref[rows, lanes].astype(F32)
                summed = summed + fold(v * scaled)
                sent[rows, lanes] = (v * w).astype(BF)
                reached[rows, lanes] = (dmix_ref[rows, lanes].astype(F32) * weight[i % 2, 1, rows, within]).astype(BF)
            ends[:, lanes] = summed

    staged(tiles(DI), spread, reweigh)
    dk = dot(sent[...], ended, NT)
    dq = dot(reached[...], sc_ref[0], NT)
    for at in tiles(DI):
        old = dstate[:, at] * kept[:, at]
        ends[:, at] += jnp.sum((old * sc_ref[0, :, at].astype(F32)).reshape(NS // 8, 8, TILE), 0)
        dstate[:, at] = old + dot(turned, reached[:, at])
    ends_hi = ends[...].astype(BF)
    ends_lo = (ends[...] - ends_hi.astype(F32)).astype(BF)
    at_end = dot(ends_hi, e2[0:LANES], NT) + dot(ends_lo, e2[0:LANES], NT)
    at_end = jnp.sum(at_end, 0, keepdims=True)
    scaled_total = total * LOG2E

    half = L // 2
    lane = lax.broadcasted_iota(jnp.int32, (L, LANES), 1)

    @pl.loop(0, H // 8)
    def _(g):
        cols = pltpu.roll(scaled_total, lax.rem(LANES - 8 * g, LANES), 1)
        rows = tott_ref[0, pl.ds(pl.multiple_of(g * 8, 8), 8), :] * LOG2E
        for pair in range(4):
            at = tile_at(g * 4 + pair, LANES)
            dy = dmix_ref[:, at]
            v = vp_ref[:, at]
            top = z[0:half, at]
            low = z[half:L, at]
            for odd in range(2):
                i = 2 * pair + odd
                mine = jnp.where((lane >= P_SIZE) == (odd == 1), dy, jnp.zeros_like(dy))
                col = cols[:, i : i + 1]
                row = rows[i : i + 1, :]
                e0 = jnp.exp2(jnp.minimum(row[:, :half] - col[:half], 0.0))
                e1 = jnp.exp2(row[:, half:] - col[:half])
                e2_ = jnp.exp2(jnp.minimum(row[:, half:] - col[half:], 0.0))
                p0 = (e0 * gt[:half, :half]).astype(BF)
                p1 = (e1 * gt[:half, half:]).astype(BF)
                p2 = (e2_ * gt[half:, half:]).astype(BF)
                top = top + dot(jnp.concatenate([p0, p1], 1), mine)
                low = low + dot(p2, mine[half:])
                d = dot(v[:half], mine, NT)
                dgt[:half, :half] += e0 * d[:, :half]
                dgt[:half, half:] += e1 * d[:, half:]
                dgt[half:, half:] += e2_ * dot(v[half:], mine[half:], NT)
            z[0:half, at] = top
            z[half:L, at] = low

    masked = (dgt[...] * triangle(F32, True)).astype(BF)
    dk = dk + dot(masked, queries)
    dq = dq + dot(masked, keys, TN)

    def respread(i, at):
        weight[i % 2, 0] = dot(steps, e2[:, at])

    def unwind(i, at):
        for rows, lanes, within in pieces_of(at):
            dvp = z[rows, lanes]
            p = dvp * vp_ref[rows, lanes].astype(F32)
            hi = p.astype(BF)
            fine[0, rows, lanes] = hi
            fine[1, rows, lanes] = (p - hi.astype(F32)).astype(BF)
            dv = weight[i % 2, 0, rows, within] * dvp + sk_ref[:, lanes] * dmix_ref[rows, lanes].astype(F32)
            dbuf[lanes.start // LANES, rows, :] = dv * cs_ref[rows, lanes].astype(F32)

    staged(tiles(DI), respread, unwind)
    own = dot(fine[0], e2[0:LANES], NT) + dot(fine[1], e2[0:LANES], NT)
    slope = cs_ref[:, DI:].astype(F32)
    dbuf[DI // LANES, 0:L, :] = dk * slope[:, :NS]
    dbuf[DI // LANES + 1, 0:L, :] = dq * slope[:, NS:]

    row = lax.broadcasted_iota(jnp.int32, (L, LANES), 0)
    dtotal = yd_ref[...] - own + jnp.where(row == L - 1, at_end, 0.0)
    drate = tri_sum(triangle(BF, True), dtotal)
    decay = sp_ref[1:2, :]
    dstep = own / jnp.maximum(step, 1e-30) - decay * drate
    draw = jnp.where(lax.broadcasted_iota(jnp.int32, (L, LANES), 1) < H, dstep * sig_ref[...], 0.0)
    gp_ref[:, CH : CH + LANES] = draw.astype(BF)
    turned_ref[CH : CH + LANES, :] = draw.astype(BF).T
    if gp_ref.shape[1] > CH + LANES:
        gp_ref[:, CH + LANES :] = jnp.zeros((L, gp_ref.shape[1] - CH - LANES), BF)
        turned_ref[CH + LANES :, :] = jnp.zeros((gp_ref.shape[1] - CH - LANES, L), BF)
    hsum_ref[0:1, :] += jnp.sum(draw, 0, keepdims=True)
    hsum_ref[1:2, :] += jnp.sum(-decay * step * drate, 0, keepdims=True)

    for lt in range(CH // LANES):
        at = slice(lt * LANES, (lt + 1) * LANES)
        sums = [jnp.zeros((8, LANES), F32) for _ in range(CONVW + 1)]
        made = []
        for q in range(L // 64):
            lo = 64 * q
            here = dbuf[lt, lo : lo + 64, :]
            c = cin_ref[lo : lo + 64, at].astype(F32)
            acc = cw_ref[3:4, at] * here
            sums[3] = sums[3] + jnp.sum((here * c).reshape(8, 8, LANES), 0)
            sums[4] = sums[4] + jnp.sum(here.reshape(8, 8, LANES), 0)
            for ahead in range(1, CONVW):
                there = dbuf[lt, lo + ahead : lo + ahead + 64, :]
                acc = acc + cw_ref[3 - ahead : 4 - ahead, at] * there
                sums[3 - ahead] = sums[3 - ahead] + jnp.sum((there * c).reshape(8, 8, LANES), 0)
            made.append(acc.astype(BF))
            gp_ref[lo : lo + 64, at] = made[-1]
        turned_ref[at, :] = jnp.concatenate(made, 0).T
        for k in range(CONVW + 1):
            csum_ref[k : k + 1, at] += jnp.sum(sums[k], 0, keepdims=True)

    @pl.when(b == 0)
    def _():
        gph_ref[...] = jnp.zeros_like(gph_ref)
        turned_halo_ref[...] = jnp.zeros_like(turned_halo_ref)
        for lt in range(CH // LANES):
            at = slice(lt * LANES, (lt + 1) * LANES)
            d = dbuf[lt, 0:8, :] * cont[0].astype(F32)
            d0, d1, d2 = d[0:1], d[1:2], d[2:3]
            w0, w1, w2 = cw_ref[0:1, at], cw_ref[1:2, at], cw_ref[2:3, at]
            c5, c6, c7 = ch_ref[5:6, at], ch_ref[6:7, at], ch_ref[7:8, at]
            made = [jnp.zeros((13, LANES), F32), w0 * d0, w1 * d0 + w0 * d1, w2 * d0 + w1 * d1 + w0 * d2]
            made = jnp.concatenate(made, 0)
            gph_ref[:, at] = made.astype(BF)
            turned_halo_ref[at, :] = jnp.concatenate([made, jnp.zeros((LANES - 16, LANES), F32)], 0).T.astype(BF)
            csum_ref[0:1, at] += c5 * d0 + c6 * d1 + c7 * d2
            csum_ref[1:2, at] += c6 * d0 + c7 * d1
            csum_ref[2:3, at] += c7 * d0


def wide_grad_kernel(cont, gn_ref, dy_ref, normed_ref, dgate_ref, out_ref, buf, sems):
    k = pl.program_id(0)
    reps, shards, _, m = buf.shape
    o = dot(gn_ref[...], dy_ref[...], TN).astype(BF)
    part = o.shape[0] // reps
    first = D // m * part
    each = reps // shards

    def copies(step):
        made = [(r, step, pl.ds(0, first)) for r in range(reps)]
        made += [(step * each + i, s, pl.ds(first, DI // reps)) for i in range(each) for s in range(shards)]
        return [
            pltpu.make_async_copy(buf.at[at], out_ref.at[at], sems.at[step, i]) for i, at in enumerate(made)
        ]

    for r in range(reps):
        for u in range(D // m):
            buf[r, k, u * part : (u + 1) * part, :] = o[r * part : (r + 1) * part, u * m : (u + 1) * m]
    part = DI // reps
    g = dot(dgate_ref[...], normed_ref[...], TN).astype(BF)
    for i in range(each):
        for s in range(shards):
            buf[k * each + i, s, first:, :] = g[i * part : (i + 1) * part, s * m : (s + 1) * m]
    for c in copies(k):
        c.start()

    @pl.when(k == shards - 1)
    def _():
        for step in range(shards):
            for c in copies(step):
                c.wait()


def conv_grad_kernel(nb, cont, normed_ref, turned_ref, nh_ref, turned_halo_ref, out_ref):
    half, _, part, _ = out_ref.shape
    full = (dot(turned_ref[...], normed_ref[...]) + dot(turned_halo_ref[...], nh_ref[...])).astype(BF)
    for chip in range(half):
        out_ref[(cont[nb + 2] // 2) ^ chip, 0] = full[chip * part : (chip + 1) * part]


def input_grad_kernel(convs, gates, cont, x_ref, dy_ref, gp_ref, dgate_ref, ahead_ref, ng_ref, *rest):
    crefs, grefs = rest[:convs], rest[convs : convs + gates]
    gt_ref, gn_ref, wc, wg, csems, gsems, acc = rest[convs + gates :]
    b = pl.program_id(0)
    nb = pl.num_programs(0)

    @pl.when(b == 0)
    def _():
        place = cont[nb + 1], cont[nb + 2], convs - 1
        loads = copies_of(features(crefs, wc, wc.shape[1] // (convs - 1), *place), csems)
        loads += copies_of(features(grefs, wg, DI // (convs - 1), *place), gsems)
        for c in loads:
            c.start()
        gn_ref[...] = jnp.zeros_like(gn_ref)
        for c in loads:
            c.wait()

    m = wc.shape[2]
    for s, at in enumerate(tiles(D, m)):
        acc[:, at] = dot(gp_ref[...], wc[s]) + dot(dgate_ref[...], wg[s])

    @pl.when(b == nb - 1)
    def _():
        keep = cont[nb].astype(F32)
        for s, at in enumerate(tiles(D, m)):
            acc[L - 16 : L, at] += keep * dot(ahead_ref[...], wc[s])

    for q in range(L // 32):
        rows = slice(32 * q, 32 * q + 32)
        x = x_ref[rows].astype(F32)
        inv = lax.rsqrt(jnp.mean(x * x, 1, keepdims=True) + EPSILON)
        g = acc[rows]
        gn_ref[...] += jnp.sum((g * (x * inv)).reshape(4, 8, D), 0)
        v = g * ng_ref[...]
        mean = jnp.mean(v * x, 1, keepdims=True)
        gt_ref[rows] = (inv * v - x * (inv * inv * inv * mean) + dy_ref[rows].astype(F32)).astype(BF)


def finish_wide_kernel(cont, wide_ref, gin_ref, gout_ref, buf, sem):
    reps, rows, m = wide_ref.shape
    part = DI // reps
    for r in range(reps):
        buf[r * part : (r + 1) * part, :] = wide_ref[r, rows - part :, :].astype(F32)
    copy = pltpu.make_async_copy(buf, gin_ref.at[pl.ds(0, DI)], sem)
    copy.start()
    part = (rows - part) * m // D
    for r in range(reps):
        for u in range(D // m):
            block = wide_ref[r, u * part : (u + 1) * part, :]
            gout_ref[r * part : (r + 1) * part, u * m : (u + 1) * m] = block.astype(F32)
    copy.wait()


def finish_conv_kernel(nb, count, part, cont, *rest):
    pieces = rest[:count]
    gin_ref, small_ref, buf, sem = rest[count + 1 :]
    for i, piece in enumerate(pieces):
        place = slot_of(cont[nb + 2] ^ i, count)
        buf[pl.ds(pl.multiple_of(place * part, 16), part), :] = piece[0:part].astype(F32)
    copy = pltpu.make_async_copy(buf.at[pl.ds(0, CH + H)], gin_ref.at[pl.ds(DI, CH + H)], sem)
    copy.start()
    half = small_ref.shape[0]
    small = jnp.zeros(small_ref.shape, F32)
    for piece in pieces:
        small = small + (piece[part : part + half].astype(F32) + piece[part + half :].astype(F32))
    small_ref[...] = small
    copy.wait()


def rows_of(width, reverse=0, column=0):
    if reverse:
        return pl.BlockSpec((L, width), lambda b, cont: (reverse - 1 - b, column))
    return pl.BlockSpec((L, width), lambda b, cont: (b, column))


def whole(*shape):
    return pl.BlockSpec(shape, lambda b, cont: (0,) * len(shape), pipeline_mode=pl.Buffered(1))


def fixed(*shape):
    return pl.BlockSpec(shape, lambda b, cont: (0,) * len(shape))


def lead_of(reverse, *shape):
    if reverse:
        return pl.BlockSpec((1, *shape), lambda b, cont: (reverse - 1 - b, 0, 0))
    return pl.BlockSpec((1, *shape), lambda b, cont: (b, 0, 0))


def anywhere(count):
    return [pl.BlockSpec(memory_space=pl.ANY)] * count


def call(kernel, grid, in_specs, out_specs, outs, scratch, flops, nbytes, name, aliases=None):
    return pl.pallas_call(
        kernel,
        grid_spec=pltpu.PrefetchScalarGridSpec(
            num_scalar_prefetch=1, grid=(grid,), in_specs=in_specs, out_specs=out_specs, scratch_shapes=scratch
        ),
        out_shape=[jax.ShapeDtypeStruct(s, d) for s, d in outs],
        input_output_aliases=aliases or {},
        compiler_params=pltpu.CompilerParams(vmem_limit_bytes=VMEM),
        cost_estimate=pl.CostEstimate(flops=flops, bytes_accessed=nbytes, transcendentals=0),
        name=name,
    )


def loaded(count, shards, *shape):
    return [pltpu.VMEM(shape, BF), pltpu.SemaphoreType.DMA((copy_count(count - 1, shards),))]


def front(cont, x, xh, ng, wc, cw, sp, shards):
    rows = x.shape[0]
    nb = rows // L
    count = len(wc)
    return call(
        partial(front_kernel, count), nb,
        [rows_of(D), whole(16, D), whole(1, D), whole(8, CH), whole(8, LANES), *anywhere(count)],
        [rows_of(D), rows_of(CH), rows_of(DI), rows_of(CH), rows_of(CH), rows_of(LANES), rows_of(LANES), rows_of(LANES),
         lead_of(0, LANES, L), lead_of(0, NS, DI), fixed(NS, DI), fixed(LANES, D), fixed(8, CH)],
        [((rows, D), BF), ((rows, CH), BF), ((rows, DI), BF), ((rows, CH), BF), ((rows, CH), BF), ((rows, LANES), F32),
         ((rows, LANES), F32), ((rows, LANES), F32), ((nb, LANES, L), F32), ((nb, NS, DI), BF), ((NS, DI), BF),
         ((LANES, D), BF), ((8, CH), F32)],
        [pltpu.VMEM((CH // LANES, L + 8, LANES), F32), pltpu.VMEM((NS, DI), F32), pltpu.VMEM((2 * LANES, DI), BF),
         pltpu.VMEM((L, DI), BF), pltpu.VMEM((2, 2, L, TILE), F32), *loaded(count, shards, shards, *wc[0].shape)],
        1_000_000, 1 << 20, "front",
    )(cont, x, xh, ng, cw, sp, *wc)


def scan(cont, inner, vp, tot, tott):
    rows = inner.shape[0]
    nb = rows // L
    return call(
        scan_kernel, nb,
        [rows_of(2 * NS, 0, DI // (2 * NS)), rows_of(DI), rows_of(LANES), lead_of(0, LANES, L)],
        [rows_of(DI)],
        [((rows, DI), F32)],
        [pltpu.VMEM((L, L), F32)],
        1_000_000, 1 << 20, "scan",
    )(cont, inner, vp, tot, tott)[0]


def gating(cont, x, dy, normed, inner, y, tot, sloc, sin, wg, wo_own, gg, sk, shards):
    rows = x.shape[0]
    nb = rows // L
    count = len(wg)
    wide = pltpu.VMEM((L, DI), F32)
    return call(
        partial(gate_kernel, count), nb,
        [rows_of(D), rows_of(D), rows_of(D), rows_of(CH), rows_of(DI), rows_of(LANES), lead_of(0, NS, DI), whole(NS, DI),
         whole(1, DI), whole(1, DI), *anywhere(count + 1)],
        [rows_of(D), rows_of(DI), rows_of(DI), rows_of(DI), rows_of(LANES), lead_of(0, NS, DI), fixed(NS, DI),
         fixed(8, DI)],
        [((rows, D), BF), ((rows, DI), BF), ((rows, DI), BF), ((rows, DI), BF), ((rows, LANES), F32),
         ((nb, NS, DI), BF), ((NS, DI), BF), ((8, DI), F32)],
        [pltpu.VMEM((2 * LANES, DI), BF), wide, wide, wide, wide, wide,
         pltpu.VMEM((NS, DI), F32), pltpu.VMEM((1, DI), F32), pltpu.VMEM((shards, *wg[0].shape), BF),
         pltpu.VMEM((wo_own.shape[0], DI, wo_own.shape[2]), BF),
         pltpu.SemaphoreType.DMA((copy_count(count - 1, shards),)),
         pltpu.SemaphoreType.DMA((copy_count(count - 1, shards, shards),))],
        35_000_000_000, 40 << 20, "gating",
    )(cont, x, dy, normed, inner, y, tot, sloc, sin, gg, sk, *wg, wo_own)


def back(cont, inner, vp, cs, cin, stp, sig, tot, tott, sc, dmix, yd, din, cw, sp, sk, ch, width):
    rows = inner.shape[0]
    nb = rows // L
    return call(
        back_kernel, nb,
        [rows_of(2 * NS, nb, DI // (2 * NS)), rows_of(DI, nb), rows_of(CH, nb), rows_of(CH, nb), rows_of(LANES, nb),
         rows_of(LANES, nb), rows_of(LANES, nb), lead_of(nb, LANES, L), lead_of(nb, NS, DI), rows_of(DI, nb),
         rows_of(LANES, nb), whole(NS, DI), whole(8, CH), whole(8, LANES), whole(1, DI), whole(8, CH)],
        [rows_of(width, nb), pl.BlockSpec((width, L), lambda b, cont: (0, nb - 1 - b)), fixed(16, width),
         fixed(width, LANES), fixed(8, CH), fixed(8, LANES)],
        [((rows, width), BF), ((width, rows), BF), ((16, width), BF), ((width, LANES), BF), ((8, CH), F32),
         ((8, LANES), F32)],
        [pltpu.VMEM((NS, DI), F32), pltpu.VMEM((2 * LANES, DI), BF), pltpu.VMEM((L, DI), F32),
         pltpu.VMEM((CH // LANES, L + 8, LANES), F32), pltpu.VMEM((L, L), F32), pltpu.VMEM((L, L), F32),
         pltpu.VMEM((2, 2, L, TILE), F32), pltpu.VMEM((L, DI), BF), pltpu.VMEM((L, DI), BF), pltpu.VMEM((8, DI), F32),
         pltpu.VMEM((2, L, DI), BF)],
        60_000_000_000, 30 << 20, "back",
    )(cont, inner, vp, cs, cin, stp, sig, tot, tott, sc, dmix, yd, din, cw, sp, sk, ch)


def wide_grad(cont, gn, dy, normed, dgate, reps, shards):
    rows = dy.shape[0]
    block = DI // shards
    shape = (reps, shards, 2 * DI // reps, D // shards)
    return call(
        wide_grad_kernel, shards,
        [pl.BlockSpec((rows, block), lambda k, c: (0, k)), whole(rows, D), whole(rows, D),
         pl.BlockSpec((rows, block), lambda k, c: (0, k))],
        anywhere(1),
        [(shape, BF)],
        [pltpu.VMEM(shape, BF), pltpu.SemaphoreType.DMA((shards, 2 * reps))], 8_600_000_000, 24 << 20, "wide_grad",
    )(cont, gn, dy, normed, dgate)[0]


def conv_grad(cont, normed, turned, nh, turned_halo, reps, shards, other):
    width, rows = turned.shape
    nb = rows // L
    m = D // shards
    half, part = width // 2, width // reps
    return call(
        partial(conv_grad_kernel, nb), shards,
        [pl.BlockSpec((rows, m), lambda k, c: (0, c[nb + 1] ^ k)),
         pl.BlockSpec((half, rows), lambda k, c: (lax.rem(c[nb + 2], 2) ^ other, 0)),
         pl.BlockSpec((LANES, m), lambda k, c: (0, c[nb + 1] ^ k)),
         pl.BlockSpec((half, LANES), lambda k, c: (lax.rem(c[nb + 2], 2) ^ other, 0))],
        [pl.BlockSpec((reps // 2, 1, part, m), lambda k, c: (0, k, 0, 0))],
        [((reps // 2, shards, part, m), BF)],
        [], 5_000_000_000, 8 << 20, "conv_grad",
    )(cont, normed, turned, nh, turned_halo)[0]


def input_grad(cont, x, dy, gp, dgate, ahead, ng, wc, wg, shards):
    rows, width = gp.shape
    nb = rows // L
    convs, gates = len(wc), len(wg)
    return call(
        partial(input_grad_kernel, convs, gates), nb,
        [rows_of(D), rows_of(D), rows_of(width), rows_of(DI), whole(16, width), whole(1, D), *anywhere(convs + gates)],
        [rows_of(D), fixed(8, D)],
        [((rows, D), BF), ((8, D), F32)],
        [pltpu.VMEM((shards, *wc[0].shape), BF), pltpu.VMEM((shards, *wg[0].shape), BF),
         pltpu.SemaphoreType.DMA((copy_count(convs - 1, shards),)), pltpu.SemaphoreType.DMA((copy_count(gates - 1, shards),)),
         pltpu.VMEM((L, D), F32)],
        10_000_000_000, 24 << 20, "input_grad",
    )(cont, x, dy, gp, dgate, ahead, ng, *wc, *wg)


def finish_wide(cont, wide):
    reps, rows, m = wide.shape
    shards = D // m
    return call(
        finish_wide_kernel, 1,
        [whole(*wide.shape)],
        [pl.BlockSpec(memory_space=pl.ANY), fixed(DI // shards, D)],
        [((DI + CH + H, m), F32), ((DI // shards, D), F32)],
        [pltpu.VMEM((DI, m), F32), pltpu.SemaphoreType.DMA],
        1_000_000, 8 << 20, "finish_wide",
    )(cont, wide)


def finish_conv(cont, nb, pieces, gin, part):
    rows, m = pieces[0].shape
    count = len(pieces)
    return call(
        partial(finish_conv_kernel, nb, count, part), 1,
        [*[whole(rows, m)] * count, pl.BlockSpec(memory_space=pl.ANY)],
        [pl.BlockSpec(memory_space=pl.ANY), fixed((rows - part) // 2, m)],
        [(gin.shape, F32), (((rows - part) // 2, m), F32)],
        [pltpu.VMEM((count * part, m), F32), pltpu.SemaphoreType.DMA],
        1_000_000, 5 << 20, "finish_conv", {1 + count: 0},
    )(cont, *pieces, gin)


def shift(v, by):
    n = lax.axis_size(BOTH)
    return lax.ppermute(v, BOTH, [(i, (i + by) % n) for i in range(n)])


def swap(v, mask):
    n = lax.axis_size(BOTH)
    return lax.ppermute(v, BOTH, [(i, i ^ mask) for i in range(n)])


def part_of(w):
    reps = lax.axis_size("rep")
    part = w.shape[0] // reps
    return lax.dynamic_slice(w, (slot_of(lax.axis_index("rep"), reps) * part, 0), (part, w.shape[1]))


def over_reps(column):
    reps, shards = lax.axis_size("rep"), lax.axis_size("shard")
    return [column] + [swap(column, 2 * shards * j) for j in range(1, reps // 2)]


def over_cores(plane):
    shards = lax.axis_size("shard")
    other = [swap(v, shards) for v in plane]
    return [v for pair in zip(plane, other) for v in pair]


def after(value, *first):
    return lax.optimization_barrier((value, first))[0]


def total_of(first, *others):
    out = first.astype(F32)
    for v in others:
        out = out + v.astype(F32)
    return out.astype(first.dtype)


def two_halves(v, m):
    rows = -(-v.size // (16 * m)) * 16
    v = jnp.pad(v, (0, rows * m - v.size)).reshape(rows, m)
    hi = v.astype(BF)
    return jnp.concatenate([hi, (v - hi.astype(F32)).astype(BF)], 0)


def one_value(v):
    half = v.shape[0] // 2
    return v[:half].astype(F32) + v[half:].astype(F32)


def local(
    tokens, cotangent, seq_lengths, deal_order, norm_gain, in_proj, conv_weight, conv_bias, step_bias, decay_log,
    skip_gain, gate_gain, out_proj,
):
    n = lax.axis_size(BOTH)
    me = lax.axis_index(BOTH)
    reps, shards = lax.axis_size("rep"), lax.axis_size("shard")
    rep, mine = lax.axis_index("rep"), lax.axis_index("shard")
    rows = tokens.shape[0]
    nb = rows // L
    unit = lcm(LANES, 16 * reps)
    width = -(-(CH + LANES) // unit) * unit

    seqs = seq_lengths.shape[0]
    order = jnp.arange(seqs, dtype=jnp.int32)
    starts = jnp.sum(jnp.where(order[None, :] < order[:, None], seq_lengths[None, :], 0), 1)
    edge = (me * nb + jnp.arange(nb + 1, dtype=jnp.int32)) * L
    cont = jnp.where(jnp.any(starts[None, :] == edge[:, None], 1) | (edge >= n * rows), 0, 1)
    cont = jnp.concatenate([cont.astype(jnp.int32), jnp.stack([mine, rep]).astype(jnp.int32)])

    turned = in_proj.T
    wcs = jnp.pad(turned[DI:], ((0, width - CH - H), (0, 0)))
    wgs = turned[:DI]
    m = wcs.shape[1]
    own_small = [*conv_weight, conv_bias, gate_gain, norm_gain, step_bias, decay_log, skip_gain]
    count = sum(v.size for v in own_small)
    extra = -(-count // (16 * m)) * 16
    small, at = jnp.zeros((extra * m,), BF), 0
    for v in own_small:
        small = small + lax.pad(v, jnp.zeros((), BF), [(at, extra * m - at - v.size, 0)])
        at += v.size
    piece = jnp.concatenate([part_of(wcs), small.reshape(extra, m)], 0)
    small = small[:count]
    part = width // reps
    column = [swap(piece, k) for k in range(1, shards)]
    small = jnp.stack([small] + [v[part:].reshape(-1)[:count] for v in column])
    conv_column = jnp.stack(column)
    halo = shift(tokens[rows - 16 :], 1)
    wo_own = jnp.stack([out_proj[:, at] for at in tiles(D, m)])
    out_rows = out_proj.shape[0] // reps
    out_part = lax.dynamic_slice(wo_own, (0, slot_of(rep, reps) * out_rows, 0), (D // m, out_rows, m))
    piece = jnp.concatenate([part_of(wgs), out_part.reshape(-1, m)], 0)
    gate_column = lax.all_gather(piece, "shard", axis=0)
    gate_column = jnp.take(gate_column, mine ^ jnp.arange(1, shards), axis=0)
    small = jnp.take(small, mine ^ jnp.arange(shards), axis=0).astype(F32)
    sizes = [conv_weight.size, conv_bias.size, gate_gain.size, norm_gain.size, step_bias.size, decay_log.size,
             skip_gain.size]
    parts, at = [], 0
    for size in sizes:
        parts.append(small[:, at : at + size])
        at += size
    taps = parts[0].reshape(shards, CONVW, -1).transpose(1, 0, 2).reshape(CONVW, CH)
    cw = jnp.concatenate([taps, parts[1].reshape(1, CH), jnp.zeros((3, CH), F32)], 0)
    gg = parts[2].reshape(1, DI)
    ng = parts[3].reshape(1, D)
    rate_scale = jnp.exp(parts[5].reshape(1, H))
    sp = jnp.pad(jnp.concatenate([parts[4].reshape(1, H), rate_scale], 0), ((0, 6), (0, LANES - H)))
    sk = jnp.repeat(parts[6].reshape(1, H), P_SIZE, axis=1)

    conv_plane = over_reps(conv_column)
    wc = [wcs, *over_cores(conv_plane[:1] + after(conv_plane[1:], gate_column))]
    gate_plane = over_reps(after(gate_column, conv_plane))

    normed, inner, vp, cs, cin, stp, sig, tot, tott, sloc, fin, nh, ch = front(cont, tokens, halo, ng, wc, cw, sp, shards)
    sin = shift(fin, 1)
    y = scan(cont, inner, vp, tot, tott)
    wg = [wgs, *over_cores(gate_plane[:1] + after(gate_plane[1:], y, sin))]
    output, gn, dgate, dmix, yd, sc, dlead, sums = gating(
        cont, tokens, cotangent, normed, inner, y, tot, sloc, sin, wg, wo_own, gg, sk, shards
    )
    din = shift(dlead, -1)
    wide = after(wide_grad(cont, gn, cotangent, normed, dgate, reps, shards), din)
    wide = lax.psum_scatter(wide, "rep", scatter_dimension=0, tiled=True)[0]
    gp, turned_gp, gph, turned_gph, csum, hsum = back(cont, inner, vp, cs, cin, stp, sig, tot, tott, sc, dmix, yd, din, cw, sp, sk, ch, width)

    ahead = shift(gph, -1)
    theirs = swap(after(conv_grad(cont, normed, turned_gp, nh, turned_gph, reps, shards, 1), ahead), shards)
    w = conv_grad(cont, normed, turned_gp, nh, turned_gph, reps, shards, 0)
    w = [total_of(w[j], theirs[j]) for j in range(reps // 2)]
    gp = after(gp, w, wide)
    wide = lax.psum_scatter(after(wide, w), "shard", scatter_dimension=0, tiled=True)[0]
    grad_tokens, grad_norm = input_grad(cont, tokens, cotangent, gp, dgate, ahead, ng, wc, wg, shards)
    packed = jnp.concatenate(
        [csum[0:CONVW].reshape(CONVW, shards, -1).transpose(1, 0, 2).reshape(shards, -1), csum[4].reshape(shards, -1),
         sums[0].reshape(shards, -1), grad_norm.sum(0).reshape(shards, -1), hsum[0, :H].reshape(shards, -1),
         hsum[1, :H].reshape(shards, -1), sums[1].reshape(H, P_SIZE).sum(1).reshape(shards, -1)], 1)
    packed = jnp.take(packed, mine ^ jnp.arange(shards), axis=0)
    others = [swap(w[j], 2 * shards * j) for j in range(1, reps // 2)]
    others, wide, packed = lax.optimization_barrier((others, wide, packed))
    w = total_of(w[0], *others)
    wide = lax.all_gather(wide, "rep", axis=0)
    w = [jnp.concatenate([w[k], two_halves(packed[k], m)], 0) for k in range(shards)]
    w = w[:1] + [swap(w[k], k) for k in range(1, shards)]
    rest = sum(one_value(v[part:]) for v in w)
    w = jnp.concatenate([total_of(*[v[:part] for v in w]), two_halves(rest.reshape(-1), m)], 0)
    pieces = over_cores(over_reps(w))
    gin, grad_out = finish_wide(cont, wide)
    grad_in, small = finish_conv(cont, nb, pieces, gin, part)
    grad_in = grad_in.T
    own = small.reshape(-1)
    got, at = [], 0
    for size in sizes:
        got.append(own[at : at + size])
        at += size
    return (
        output, grad_tokens, got[3], grad_in, got[0].reshape(CONVW, -1), got[1], got[4], got[5], got[6], got[2],
        grad_out,
    )


def solution(mesh):
    both = P(BOTH, None)
    in_specs = (
        both, both, P(), P(), P("shard"), P("shard", None), P(None, "shard"), P("shard"), P("shard"), P("shard"),
        P("shard"), P("shard"), P("shard", None),
    )
    out_specs = (
        both, both, P("shard"), P("shard", None), P(None, "shard"), P("shard"), P("shard"), P("shard"), P("shard"),
        P("shard"), P("shard", None),
    )
    return jax.shard_map(local, mesh=mesh, in_specs=in_specs, out_specs=out_specs, check_vma=False)
```

```python
from functools import partial
from math import lcm

import jax
import jax.numpy as jnp
from jax import lax
from jax.experimental import pallas as pl
from jax.experimental.pallas import tpu as pltpu
from jax.sharding import PartitionSpec as P

D = 1024
DI = 2048
H = 32
P_SIZE = 64
NS = 128
CONVW = 4
CH = DI + 2 * NS
L = 256
LANES = 128
TILE = 256
EPSILON = 1e-05
LOG2E = 1.4426950408889634
VMEM = 58 << 20
F32 = jnp.float32
BF = jnp.bfloat16
NN = (((1,), (0,)), ((), ()))
NT = (((1,), (1,)), ((), ()))
TN = (((0,), (0,)), ((), ()))
BOTH = ("rep", "shard")


def dot(a, b, dims=NN):
    return lax.dot_general(a, b, dims, preferred_element_type=F32)


def sigmoid(v):
    return 0.5 * jnp.tanh(0.5 * v) + 0.5


def silu_and_slope(v):
    half = 0.5 * v
    bent = jnp.tanh(half)
    part = half * bent
    return half + part, (0.5 + 0.5 * bent) * (1.0 + half - part)


def split2(v):
    hi = v.astype(BF)
    return jnp.concatenate([hi, (v - hi.astype(F32)).astype(BF)], 1)


def tri_sum(tri, v):
    hi = v.astype(BF)
    rest = v - hi.astype(F32)
    mid = rest.astype(BF)
    low = (rest - mid.astype(F32)).astype(BF)
    got = dot(tri, jnp.concatenate([hi, mid, low], 1))
    return got[:, :LANES] + got[:, LANES : 2 * LANES] + got[:, 2 * LANES :]


def head_spread():
    row = lax.broadcasted_iota(jnp.int32, (2 * LANES, DI), 0)
    col = lax.broadcasted_iota(jnp.int32, (2 * LANES, DI), 1)
    return jnp.where((row % LANES) == col // P_SIZE, 1.0, 0.0).astype(BF)


def head_sum(v, e2, at):
    hi = v.astype(BF)
    low = (v - hi.astype(F32)).astype(BF)
    return dot(hi, e2[0:LANES, at], NT) + dot(low, e2[0:LANES, at], NT)


def triangle(kind, up):
    row = lax.broadcasted_iota(jnp.int32, (L, L), 0)
    col = lax.broadcasted_iota(jnp.int32, (L, L), 1)
    return jnp.where(row <= col if up else row >= col, 1.0, 0.0).astype(kind)


def tile_at(t, size=TILE):
    return pl.ds(pl.multiple_of(t * size, size), size)


def tiles(width, size=TILE):
    return [slice(t, t + size) for t in range(0, width, size)]


STEP = 64


def pieces_of(at):
    for lanes in range(at.start, at.stop, LANES):
        for q in range(0, L, STEP):
            yield slice(q, q + STEP), slice(lanes, lanes + LANES), slice(lanes - at.start, lanes - at.start + LANES)


def fold(v):
    return jnp.sum(v.reshape(STEP // 8, 8, LANES), 0)


def staged(parts, first, then):
    first(0, parts[0])
    for i, part in enumerate(parts):
        if i + 1 < len(parts):
            first(i + 1, parts[i + 1])
        then(i, part)


def slot_of(rep, reps):
    return lax.rem(rep, 2) * (reps // 2) + rep // 2


def span(first, size):
    return pl.ds(pl.multiple_of(first, 16), size)


def features(refs, place, part, shard, rep, reps):
    made = [(refs[0], place.at[shard])]
    for i, ref in enumerate(refs[1:]):
        first = slot_of(rep ^ i, reps) * part
        for k in range(1, ref.shape[0] + 1):
            source = ref.at[k - 1] if part == ref.shape[1] else ref.at[k - 1, pl.ds(0, part)]
            made.append((source, place.at[shard ^ k, span(first, part)]))
    return made


def rows_behind(own, refs, place, skip, shard, rep, reps):
    groups, n, _ = own.shape
    part = n // reps
    made = [(own.at[u], place.at[u, span(shard * n, n)]) for u in range(groups)]
    for i, ref in enumerate(refs):
        first = slot_of(rep ^ i, reps) * part
        for k in range(1, ref.shape[0] + 1):
            for u in range(groups):
                source = ref.at[k - 1, pl.ds(skip + u * part, part)]
                made.append((source, place.at[u, span((shard ^ k) * n + first, part)]))
    return made


def across(a, w, rows):
    m = w.shape[2]
    out = dot(a[:, 0:m], w[0, rows], NT)
    for s in range(1, w.shape[0]):
        out = out + dot(a[:, s * m : (s + 1) * m], w[s, rows], NT)
    return out


def copies_of(made, sems):
    return [pltpu.make_async_copy(source, place, sems.at[i]) for i, (source, place) in enumerate(made)]


def copy_count(reps, shards, each=1):
    return each + reps * (shards - 1) * each


def rms(x, gain):
    xf = x.astype(F32)
    inv = lax.rsqrt(jnp.mean(xf * xf, 1, keepdims=True) + EPSILON)
    return (xf * inv * gain).astype(BF)


def front_kernel(count, cont, x_ref, xh_ref, ng_ref, cw_ref, sp_ref, *rest):
    wrefs = rest[:count]
    (normed_ref, inner_ref, vp_ref, cs_ref, cin_ref, stp_ref, sig_ref, tot_ref, tott_ref, sloc_ref, fin_ref, nh_ref, ch_ref,
     cbuf, state, e2, part, weight, wc, sems) = rest[count:]
    b = pl.program_id(0)
    nb = pl.num_programs(0)
    gain = ng_ref[...]

    @pl.when(b == 0)
    def _():
        loads = copies_of(features(wrefs, wc, wc.shape[1] // (count - 1), cont[nb + 1], cont[nb + 2], count - 1), sems)
        for c in loads:
            c.start()
        e2[...] = head_spread()
        state[...] = jnp.zeros_like(state)
        halo = rms(xh_ref[...], gain)
        nh_ref[...] = jnp.zeros_like(nh_ref)
        nh_ref[0:16] = halo
        for c in loads:
            c.wait()
        for at in tiles(CH):
            c = across(halo, wc, at)[8:16]
            ch_ref[:, at] = c
            for u in range(TILE // LANES):
                cbuf[at.start // LANES + u, 0:8, :] = c[:, u * LANES : (u + 1) * LANES]

    @pl.when(b > 0)
    def _():
        cbuf[:, 0:8, :] = cbuf[:, L : L + 8, :]

    keep = cont[b].astype(F32)
    cbuf[:, 0:8, :] = cbuf[:, 0:8, :] * keep
    normed = rms(x_ref[...], gain)
    normed_ref[...] = normed

    raw = across(normed, wc, slice(CH, CH + LANES)) + sp_ref[0:1, :]
    small = jnp.exp(-jnp.abs(raw))
    series = small * (1.0 - small * (0.5 - small * (1.0 / 3.0)))
    step = jnp.maximum(raw, 0.0) + jnp.where(small < 0.01, series, jnp.log(1.0 + small))
    rate = -sp_ref[1:2, :] * step
    total = tri_sum(triangle(BF, False), rate)
    stp_ref[...] = step
    sig_ref[...] = sigmoid(raw)
    tot_ref[...] = total
    tott_ref[0] = total.T
    last = total[L - 1 : L, :]
    steps = split2(step)
    leaving = split2(jnp.exp(last - total))
    kept = dot(split2(jnp.exp(jnp.broadcast_to(last, (8, LANES)))), e2[...])[0:1]
    state[...] = state[...] * keep
    sloc_ref[0] = state[...].astype(BF)

    def project(i, at):
        c = across(normed, wc, at)
        for u in range(TILE // LANES):
            cbuf[at.start // LANES + u, 8 : L + 8, :] = c[:, u * LANES : (u + 1) * LANES]
        if at.start < DI:
            weight[i % 2, 0] = dot(steps, e2[:, at])
            weight[i % 2, 1] = dot(leaving, e2[:, at])

    def convolve(i, at):
        for rows, lanes, within in pieces_of(at):
            lo = 8 + rows.start
            buf = cbuf.at[lanes.start // LANES]
            here = buf[lo : lo + STEP, :]
            cin_ref[rows, lanes] = here.astype(BF)
            acc = cw_ref[4:5, lanes] + cw_ref[3:4, lanes] * here
            for back in range(1, CONVW):
                acc = acc + cw_ref[3 - back : 4 - back, lanes] * buf[lo - back : lo - back + STEP, :]
            v, slope = silu_and_slope(acc)
            cs_ref[rows, lanes] = slope.astype(BF)
            inner_ref[rows, lanes] = v.astype(BF)
            if at.start < DI:
                v = v * weight[i % 2, 0, rows, within]
                vp_ref[rows, lanes] = v.astype(BF)
                part[rows, lanes] = (v * weight[i % 2, 1, rows, within]).astype(BF)

    staged([slice(DI, CH)] + tiles(DI), project, convolve)
    keys = inner_ref[:, DI : DI + NS].T
    for at in tiles(DI):
        state[:, at] = state[:, at] * kept[:, at] + dot(keys, part[:, at])

    @pl.when(b == nb - 1)
    def _():
        fin_ref[...] = state[...].astype(BF)


def scan_kernel(cont, kq_ref, vp_ref, tot_ref, tott_ref, y_ref, gm):
    total = tot_ref[...] * LOG2E
    keys = kq_ref[:, :NS]
    queries = kq_ref[:, NS:]
    gm[...] = dot(queries, keys, NT) * triangle(F32, False)
    half = L // 2
    lane = lax.broadcasted_iota(jnp.int32, (L, LANES), 1)

    @pl.loop(0, H // 8)
    def _(g):
        cols = pltpu.roll(total, lax.rem(LANES - 8 * g, LANES), 1)
        rows = tott_ref[0, pl.ds(pl.multiple_of(g * 8, 8), 8), :] * LOG2E
        for pair in range(4):
            at = tile_at(g * 4 + pair, LANES)
            both = vp_ref[:, at]
            top, low = 0.0, 0.0
            for odd in range(2):
                i = 2 * pair + odd
                mine = jnp.where((lane >= P_SIZE) == (odd == 1), both, jnp.zeros_like(both))
                col = cols[:, i : i + 1]
                row = rows[i : i + 1, :]
                p0 = jnp.exp2(jnp.minimum(col[:half] - row[:, :half], 0.0)) * gm[:half, :half]
                p1 = jnp.exp2(col[half:] - row[:, :half]) * gm[half:, :half]
                p2 = jnp.exp2(jnp.minimum(col[half:] - row[:, half:], 0.0)) * gm[half:, half:]
                top = top + dot(p0.astype(BF), mine[:half])
                low = low + dot(jnp.concatenate([p1.astype(BF), p2.astype(BF)], 1), mine)
            y_ref[0:half, at] = top
            y_ref[half:L, at] = low


def gate_kernel(
    count, cont, x_ref, dy_ref, normed_ref, inner_ref, y_ref, tot_ref, sloc_ref, sin_ref, gg_ref, sk_ref, *rest
):
    grefs, own_ref = rest[:count], rest[count]
    (out_ref, gn_ref, dgate_ref, dmix_ref, yd_ref, sc_ref, dlead_ref, sums_ref,
     e2, gate, gated, dn, etot, yfull, dlead, lead, wg, wo, gsems, osems) = rest[count + 1 :]
    b = pl.program_id(0)
    nb = pl.num_programs(0)

    @pl.when(b == 0)
    def _():
        place = cont[nb + 1], cont[nb + 2], count - 1
        part = DI // (count - 1)
        loads = copies_of(features(grefs, wg, part, *place), gsems)
        loads += copies_of(rows_behind(own_ref, grefs[1:], wo, part, *place), osems)
        for c in loads:
            c.start()
        e2[...] = head_spread()
        dlead[...] = jnp.zeros_like(dlead)
        sums_ref[...] = jnp.zeros_like(sums_ref)
        lead[...] = jnp.ones_like(lead)
        for c in loads:
            c.wait()

    keep = cont[b].astype(F32)
    first = cont[0].astype(F32)
    lead[...] = lead[...] * jnp.where(b == 0, 1.0, keep)
    normed = normed_ref[...]
    queries = inner_ref[:, DI + NS :]
    reach = split2(jnp.exp(tot_ref[...]))
    square = jnp.zeros((L, TILE), F32)
    for at in tiles(DI):
        g = across(normed, wg, at)
        gate[:, at] = g
        start = (sloc_ref[0, :, at].astype(F32) + (lead[0:1, at] * first) * sin_ref[:, at].astype(F32)).astype(BF)
        sc_ref[0, :, at] = start
        e = dot(reach, e2[:, at])
        etot[:, at] = e
        y = y_ref[:, at] + e * dot(queries, start)
        yfull[:, at] = y
        v = (y + sk_ref[:, at] * inner_ref[:, at].astype(F32)) * silu_and_slope(g)[0]
        gated[:, at] = v
        square = square + v * v
    rinv = lax.rsqrt(jnp.sum(square, 1, keepdims=True) * (1.0 / DI) + EPSILON)
    for at in tiles(DI):
        gn_ref[:, at] = (gated[:, at] * rinv * gg_ref[:, at]).astype(BF)
    dy = dy_ref[...]
    inner_sum = jnp.zeros((L, TILE), F32)
    for at in tiles(DI):
        back = across(dy, wo, at)
        v = gated[:, at]
        sums_ref[0:1, at] += jnp.sum(back * (v * rinv), 0, keepdims=True)
        back = back * gg_ref[:, at]
        dn[:, at] = back
        inner_sum = inner_sum + back * v
    for u, at in enumerate(tiles(D, wo.shape[2])):
        out_ref[:, at] = (x_ref[:, at].astype(F32) + dot(gn_ref[...], wo[u])).astype(BF)
    shared = jnp.sum(inner_sum, 1, keepdims=True) * (1.0 / DI) * (rinv * rinv * rinv)
    turned = queries.T
    yd = jnp.zeros((L, LANES), F32)
    for at in tiles(DI):
        dgated = rinv * dn[:, at] - gated[:, at] * shared
        s, slope = silu_and_slope(gate[:, at])
        y = yfull[:, at]
        v = inner_ref[:, at].astype(F32)
        dgate_ref[:, at] = (dgated * (y + sk_ref[:, at] * v) * slope).astype(BF)
        dmix = (dgated * s).astype(BF)
        dmix_ref[:, at] = dmix
        dmix = dmix.astype(F32)
        sums_ref[1:2, at] += jnp.sum(dmix * v, 0, keepdims=True)
        yd = yd + head_sum(dmix * y, e2, at)
        dlead[:, at] += lead[0:1, at] * dot(turned, (dmix * etot[:, at]).astype(BF))
    yd_ref[...] = yd
    lead[...] = lead[...] * etot[L - 1 : L, :]

    @pl.when(b == nb - 1)
    def _():
        dlead_ref[...] = dlead[...].astype(BF)


def back_kernel(
    cont, kq_ref, vp_ref, cs_ref, cin_ref, stp_ref, sig_ref, tot_ref, tott_ref, sc_ref, dmix_ref, yd_ref, din_ref,
    cw_ref, sp_ref, sk_ref, ch_ref,
    gp_ref, turned_ref, gph_ref, turned_halo_ref, csum_ref, hsum_ref,
    dstate, e2, z, dbuf, gt, dgt, weight, sent, reached, ends, fine,
):
    nb = pl.num_programs(0)
    b = nb - 1 - pl.program_id(0)
    after = cont[b + 1].astype(F32)

    @pl.when(b == nb - 1)
    def _():
        e2[...] = head_spread()
        dstate[...] = din_ref[...].astype(F32)
        csum_ref[...] = jnp.zeros_like(csum_ref)
        hsum_ref[...] = jnp.zeros_like(hsum_ref)
        dbuf[:, L : L + 8, :] = jnp.zeros((CH // LANES, 8, LANES), F32)

    @pl.when(b < nb - 1)
    def _():
        dbuf[:, L : L + 8, :] = dbuf[:, 0:8, :] * after

    dstate[...] = dstate[...] * after
    step = stp_ref[...]
    total = tot_ref[...]
    last = total[L - 1 : L, :]
    keys = kq_ref[:, :NS]
    queries = kq_ref[:, NS:]
    gt[...] = dot(keys, queries, NT) * triangle(F32, True)
    dgt[...] = jnp.zeros_like(dgt)
    steps = split2(step)
    leaving = split2(jnp.exp(last - total))
    reach = split2(jnp.exp(total))
    kept = dot(split2(jnp.exp(jnp.broadcast_to(last, (8, LANES)))), e2[...])[0:1]

    turned = queries.T
    ended = dstate[...].astype(BF)

    def spread(i, at):
        z[:, at] = dot(keys, ended[:, at])
        weight[i % 2, 0] = dot(leaving, e2[:, at])
        weight[i % 2, 1] = dot(reach, e2[:, at])

    def reweigh(i, at):
        for u in range(TILE // LANES):
            summed = jnp.zeros((8, LANES), F32)
            for rows, lanes, _ in pieces_of(slice(at.start + u * LANES, at.start + (u + 1) * LANES)):
                within = slice(u * LANES, (u + 1) * LANES)
                w = weight[i % 2, 0, rows, within]
                scaled = w * z[rows, lanes]
                z[rows, lanes] = scaled
                v = vp_ref[rows, lanes].astype(F32)
                summed = summed + fold(v * scaled)
                sent[rows, lanes] = (v * w).astype(BF)
                reached[rows, lanes] = (dmix_ref[rows, lanes].astype(F32) * weight[i % 2, 1, rows, within]).astype(BF)
            ends[:, lanes] = summed

    staged(tiles(DI), spread, reweigh)
    dk = dot(sent[...], ended, NT)
    dq = dot(reached[...], sc_ref[0], NT)
    for at in tiles(DI):
        old = dstate[:, at] * kept[:, at]
        ends[:, at] += jnp.sum((old * sc_ref[0, :, at].astype(F32)).reshape(NS // 8, 8, TILE), 0)
        dstate[:, at] = old + dot(turned, reached[:, at])
    ends_hi = ends[...].astype(BF)
    ends_lo = (ends[...] - ends_hi.astype(F32)).astype(BF)
    at_end = dot(ends_hi, e2[0:LANES], NT) + dot(ends_lo, e2[0:LANES], NT)
    at_end = jnp.sum(at_end, 0, keepdims=True)
    scaled_total = total * LOG2E

    half = L // 2
    lane = lax.broadcasted_iota(jnp.int32, (L, LANES), 1)

    @pl.loop(0, H // 8)
    def _(g):
        cols = pltpu.roll(scaled_total, lax.rem(LANES - 8 * g, LANES), 1)
        rows = tott_ref[0, pl.ds(pl.multiple_of(g * 8, 8), 8), :] * LOG2E
        for pair in range(4):
            at = tile_at(g * 4 + pair, LANES)
            dy = dmix_ref[:, at]
            v = vp_ref[:, at]
            top = z[0:half, at]
            low = z[half:L, at]
            for odd in range(2):
                i = 2 * pair + odd
                mine = jnp.where((lane >= P_SIZE) == (odd == 1), dy, jnp.zeros_like(dy))
                col = cols[:, i : i + 1]
                row = rows[i : i + 1, :]
                e0 = jnp.exp2(jnp.minimum(row[:, :half] - col[:half], 0.0))
                e1 = jnp.exp2(row[:, half:] - col[:half])
                e2_ = jnp.exp2(jnp.minimum(row[:, half:] - col[half:], 0.0))
                p0 = (e0 * gt[:half, :half]).astype(BF)
                p1 = (e1 * gt[:half, half:]).astype(BF)
                p2 = (e2_ * gt[half:, half:]).astype(BF)
                top = top + dot(jnp.concatenate([p0, p1], 1), mine)
                low = low + dot(p2, mine[half:])
                d = dot(v[:half], mine, NT)
                dgt[:half, :half] += e0 * d[:, :half]
                dgt[:half, half:] += e1 * d[:, half:]
                dgt[half:, half:] += e2_ * dot(v[half:], mine[half:], NT)
            z[0:half, at] = top
            z[half:L, at] = low

    masked = (dgt[...] * triangle(F32, True)).astype(BF)
    dk = dk + dot(masked, queries)
    dq = dq + dot(masked, keys, TN)

    def respread(i, at):
        weight[i % 2, 0] = dot(steps, e2[:, at])

    def unwind(i, at):
        for rows, lanes, within in pieces_of(at):
            dvp = z[rows, lanes]
            p = dvp * vp_ref[rows, lanes].astype(F32)
            hi = p.astype(BF)
            fine[0, rows, lanes] = hi
            fine[1, rows, lanes] = (p - hi.astype(F32)).astype(BF)
            dv = weight[i % 2, 0, rows, within] * dvp + sk_ref[:, lanes] * dmix_ref[rows, lanes].astype(F32)
            dbuf[lanes.start // LANES, rows, :] = dv * cs_ref[rows, lanes].astype(F32)

    staged(tiles(DI), respread, unwind)
    own = dot(fine[0], e2[0:LANES], NT) + dot(fine[1], e2[0:LANES], NT)
    slope = cs_ref[:, DI:].astype(F32)
    dbuf[DI // LANES, 0:L, :] = dk * slope[:, :NS]
    dbuf[DI // LANES + 1, 0:L, :] = dq * slope[:, NS:]

    row = lax.broadcasted_iota(jnp.int32, (L, LANES), 0)
    dtotal = yd_ref[...] - own + jnp.where(row == L - 1, at_end, 0.0)
    drate = tri_sum(triangle(BF, True), dtotal)
    decay = sp_ref[1:2, :]
    dstep = own / jnp.maximum(step, 1e-30) - decay * drate
    draw = jnp.where(lax.broadcasted_iota(jnp.int32, (L, LANES), 1) < H, dstep * sig_ref[...], 0.0)
    gp_ref[:, CH : CH + LANES] = draw.astype(BF)
    turned_ref[CH : CH + LANES, :] = draw.astype(BF).T
    if gp_ref.shape[1] > CH + LANES:
        gp_ref[:, CH + LANES :] = jnp.zeros((L, gp_ref.shape[1] - CH - LANES), BF)
        turned_ref[CH + LANES :, :] = jnp.zeros((gp_ref.shape[1] - CH - LANES, L), BF)
    hsum_ref[0:1, :] += jnp.sum(draw, 0, keepdims=True)
    hsum_ref[1:2, :] += jnp.sum(-decay * step * drate, 0, keepdims=True)

    for lt in range(CH // LANES):
        at = slice(lt * LANES, (lt + 1) * LANES)
        sums = [jnp.zeros((8, LANES), F32) for _ in range(CONVW + 1)]
        made = []
        for q in range(L // 64):
            lo = 64 * q
            here = dbuf[lt, lo : lo + 64, :]
            c = cin_ref[lo : lo + 64, at].astype(F32)
            acc = cw_ref[3:4, at] * here
            sums[3] = sums[3] + jnp.sum((here * c).reshape(8, 8, LANES), 0)
            sums[4] = sums[4] + jnp.sum(here.reshape(8, 8, LANES), 0)
            for ahead in range(1, CONVW):
                there = dbuf[lt, lo + ahead : lo + ahead + 64, :]
                acc = acc + cw_ref[3 - ahead : 4 - ahead, at] * there
                sums[3 - ahead] = sums[3 - ahead] + jnp.sum((there * c).reshape(8, 8, LANES), 0)
            made.append(acc.astype(BF))
            gp_ref[lo : lo + 64, at] = made[-1]
        turned_ref[at, :] = jnp.concatenate(made, 0).T
        for k in range(CONVW + 1):
            csum_ref[k : k + 1, at] += jnp.sum(sums[k], 0, keepdims=True)

    @pl.when(b == 0)
    def _():
        gph_ref[...] = jnp.zeros_like(gph_ref)
        turned_halo_ref[...] = jnp.zeros_like(turned_halo_ref)
        for lt in range(CH // LANES):
            at = slice(lt * LANES, (lt + 1) * LANES)
            d = dbuf[lt, 0:8, :] * cont[0].astype(F32)
            d0, d1, d2 = d[0:1], d[1:2], d[2:3]
            w0, w1, w2 = cw_ref[0:1, at], cw_ref[1:2, at], cw_ref[2:3, at]
            c5, c6, c7 = ch_ref[5:6, at], ch_ref[6:7, at], ch_ref[7:8, at]
            made = [jnp.zeros((13, LANES), F32), w0 * d0, w1 * d0 + w0 * d1, w2 * d0 + w1 * d1 + w0 * d2]
            made = jnp.concatenate(made, 0)
            gph_ref[:, at] = made.astype(BF)
            turned_halo_ref[at, :] = jnp.concatenate([made, jnp.zeros((LANES - 16, LANES), F32)], 0).T.astype(BF)
            csum_ref[0:1, at] += c5 * d0 + c6 * d1 + c7 * d2
            csum_ref[1:2, at] += c6 * d0 + c7 * d1
            csum_ref[2:3, at] += c7 * d0


def wide_grad_kernel(cont, gn_ref, dy_ref, normed_ref, dgate_ref, out_ref, buf, sems):
    k = pl.program_id(0)
    reps, shards, _, m = buf.shape
    o = dot(gn_ref[...], dy_ref[...], TN).astype(BF)
    part = o.shape[0] // reps
    first = D // m * part
    each = reps // shards

    def copies(step):
        made = [(r, step, pl.ds(0, first)) for r in range(reps)]
        made += [(step * each + i, s, pl.ds(first, DI // reps)) for i in range(each) for s in range(shards)]
        return [
            pltpu.make_async_copy(buf.at[at], out_ref.at[at], sems.at[step, i]) for i, at in enumerate(made)
        ]

    for r in range(reps):
        for u in range(D // m):
            buf[r, k, u * part : (u + 1) * part, :] = o[r * part : (r + 1) * part, u * m : (u + 1) * m]
    part = DI // reps
    g = dot(dgate_ref[...], normed_ref[...], TN).astype(BF)
    for i in range(each):
        for s in range(shards):
            buf[k * each + i, s, first:, :] = g[i * part : (i + 1) * part, s * m : (s + 1) * m]
    for c in copies(k):
        c.start()

    @pl.when(k == shards - 1)
    def _():
        for step in range(shards):
            for c in copies(step):
                c.wait()


def conv_grad_kernel(nb, cont, normed_ref, turned_ref, nh_ref, turned_halo_ref, out_ref):
    half, _, part, _ = out_ref.shape
    full = (dot(turned_ref[...], normed_ref[...]) + dot(turned_halo_ref[...], nh_ref[...])).astype(BF)
    for chip in range(half):
        out_ref[(cont[nb + 2] // 2) ^ chip, 0] = full[chip * part : (chip + 1) * part]


def input_grad_kernel(convs, gates, cont, x_ref, dy_ref, gp_ref, dgate_ref, ahead_ref, ng_ref, *rest):
    crefs, grefs = rest[:convs], rest[convs : convs + gates]
    gt_ref, gn_ref, wc, wg, csems, gsems, acc = rest[convs + gates :]
    b = pl.program_id(0)
    nb = pl.num_programs(0)

    @pl.when(b == 0)
    def _():
        place = cont[nb + 1], cont[nb + 2], convs - 1
        loads = copies_of(features(crefs, wc, wc.shape[1] // (convs - 1), *place), csems)
        loads += copies_of(features(grefs, wg, DI // (convs - 1), *place), gsems)
        for c in loads:
            c.start()
        gn_ref[...] = jnp.zeros_like(gn_ref)
        for c in loads:
            c.wait()

    m = wc.shape[2]
    for s, at in enumerate(tiles(D, m)):
        acc[:, at] = dot(gp_ref[...], wc[s]) + dot(dgate_ref[...], wg[s])

    @pl.when(b == nb - 1)
    def _():
        keep = cont[nb].astype(F32)
        for s, at in enumerate(tiles(D, m)):
            acc[L - 16 : L, at] += keep * dot(ahead_ref[...], wc[s])

    for q in range(L // 32):
        rows = slice(32 * q, 32 * q + 32)
        x = x_ref[rows].astype(F32)
        inv = lax.rsqrt(jnp.mean(x * x, 1, keepdims=True) + EPSILON)
        g = acc[rows]
        gn_ref[...] += jnp.sum((g * (x * inv)).reshape(4, 8, D), 0)
        v = g * ng_ref[...]
        mean = jnp.mean(v * x, 1, keepdims=True)
        gt_ref[rows] = (inv * v - x * (inv * inv * inv * mean) + dy_ref[rows].astype(F32)).astype(BF)


def finish_wide_kernel(cont, wide_ref, gin_ref, gout_ref, buf, sems):
    i = pl.program_id(0)
    reps, rows, m = wide_ref.shape
    part = buf.shape[1] // reps
    for r in range(reps):
        buf[i, r * part : (r + 1) * part, :] = wide_ref[r, rows - part :, :].astype(F32)

    def copy(step):
        to = pl.ds(pl.multiple_of(step * reps * part, 16), reps * part)
        return pltpu.make_async_copy(buf.at[step], gin_ref.at[to], sems.at[step])

    copy(i).start()
    lines = (rows - part) * m // D
    for r in range(reps):
        for u in range(D // m):
            block = wide_ref[r, u * lines : (u + 1) * lines, :]
            gout_ref[r * lines : (r + 1) * lines, u * m : (u + 1) * m] = block.astype(F32)

    @pl.when(i == pl.num_programs(0) - 1)
    def _():
        for step in range(buf.shape[0]):
            copy(step).wait()


def finish_conv_kernel(nb, count, part, cont, *rest):
    pieces = rest[:count]
    gin_ref, small_ref, buf, sems = rest[count + 1 :]
    full, left = divmod(CH + H, part)

    def each(i, act):
        place = slot_of(cont[nb + 2] ^ i, count)
        first = pl.multiple_of(DI + place * part, 16)

        @pl.when(place < full)
        def _():
            act(pltpu.make_async_copy(buf.at[i], gin_ref.at[pl.ds(first, part)], sems.at[i]))

        if left:

            @pl.when(place == full)
            def _():
                act(pltpu.make_async_copy(buf.at[i, pl.ds(0, left)], gin_ref.at[pl.ds(first, left)], sems.at[i]))

    for i, piece in enumerate(pieces):
        buf[i] = piece[0:part].astype(F32)
        each(i, lambda c: c.start())
    m = buf.shape[2]
    half = small_ref.shape[1] // m
    small = jnp.zeros((half, m), F32)
    for piece in pieces:
        small = small + (piece[part : part + half].astype(F32) + piece[part + half :].astype(F32))
    for r in range(half):
        small_ref[:, r * m : (r + 1) * m] = small[r : r + 1]
    for i in range(count):
        each(i, lambda c: c.wait())


def rows_of(width, reverse=0, column=0):
    if reverse:
        return pl.BlockSpec((L, width), lambda b, cont: (reverse - 1 - b, column))
    return pl.BlockSpec((L, width), lambda b, cont: (b, column))


def whole(*shape):
    return pl.BlockSpec(shape, lambda b, cont: (0,) * len(shape), pipeline_mode=pl.Buffered(1))


def fixed(*shape):
    return pl.BlockSpec(shape, lambda b, cont: (0,) * len(shape))


def lead_of(reverse, *shape):
    if reverse:
        return pl.BlockSpec((1, *shape), lambda b, cont: (reverse - 1 - b, 0, 0))
    return pl.BlockSpec((1, *shape), lambda b, cont: (b, 0, 0))


def anywhere(count):
    return [pl.BlockSpec(memory_space=pl.ANY)] * count


def call(kernel, grid, in_specs, out_specs, outs, scratch, flops, nbytes, name, aliases=None):
    return pl.pallas_call(
        kernel,
        grid_spec=pltpu.PrefetchScalarGridSpec(
            num_scalar_prefetch=1, grid=(grid,), in_specs=in_specs, out_specs=out_specs, scratch_shapes=scratch
        ),
        out_shape=[jax.ShapeDtypeStruct(s, d) for s, d in outs],
        input_output_aliases=aliases or {},
        compiler_params=pltpu.CompilerParams(vmem_limit_bytes=VMEM),
        cost_estimate=pl.CostEstimate(flops=flops, bytes_accessed=nbytes, transcendentals=0),
        name=name,
    )


def loaded(count, shards, *shape):
    return [pltpu.VMEM(shape, BF), pltpu.SemaphoreType.DMA((copy_count(count - 1, shards),))]


def front(cont, x, xh, ng, wc, cw, sp, shards):
    rows = x.shape[0]
    nb = rows // L
    count = len(wc)
    return call(
        partial(front_kernel, count), nb,
        [rows_of(D), whole(16, D), whole(1, D), whole(8, CH), whole(8, LANES), *anywhere(count)],
        [rows_of(D), rows_of(CH), rows_of(DI), rows_of(CH), rows_of(CH), rows_of(LANES), rows_of(LANES), rows_of(LANES),
         lead_of(0, LANES, L), lead_of(0, NS, DI), fixed(NS, DI), fixed(LANES, D), fixed(8, CH)],
        [((rows, D), BF), ((rows, CH), BF), ((rows, DI), BF), ((rows, CH), BF), ((rows, CH), BF), ((rows, LANES), F32),
         ((rows, LANES), F32), ((rows, LANES), F32), ((nb, LANES, L), F32), ((nb, NS, DI), BF), ((NS, DI), BF),
         ((LANES, D), BF), ((8, CH), F32)],
        [pltpu.VMEM((CH // LANES, L + 8, LANES), F32), pltpu.VMEM((NS, DI), F32), pltpu.VMEM((2 * LANES, DI), BF),
         pltpu.VMEM((L, DI), BF), pltpu.VMEM((2, 2, L, TILE), F32), *loaded(count, shards, shards, *wc[0].shape)],
        1_000_000, 1 << 20, "front",
    )(cont, x, xh, ng, cw, sp, *wc)


def scan(cont, inner, vp, tot, tott):
    rows = inner.shape[0]
    nb = rows // L
    return call(
        scan_kernel, nb,
        [rows_of(2 * NS, 0, DI // (2 * NS)), rows_of(DI), rows_of(LANES), lead_of(0, LANES, L)],
        [rows_of(DI)],
        [((rows, DI), F32)],
        [pltpu.VMEM((L, L), F32)],
        1_000_000, 1 << 20, "scan",
    )(cont, inner, vp, tot, tott)[0]


def gating(cont, x, dy, normed, inner, y, tot, sloc, sin, wg, wo_own, gg, sk, shards):
    rows = x.shape[0]
    nb = rows // L
    count = len(wg)
    wide = pltpu.VMEM((L, DI), F32)
    return call(
        partial(gate_kernel, count), nb,
        [rows_of(D), rows_of(D), rows_of(D), rows_of(CH), rows_of(DI), rows_of(LANES), lead_of(0, NS, DI), whole(NS, DI),
         whole(1, DI), whole(1, DI), *anywhere(count + 1)],
        [rows_of(D), rows_of(DI), rows_of(DI), rows_of(DI), rows_of(LANES), lead_of(0, NS, DI), fixed(NS, DI),
         fixed(8, DI)],
        [((rows, D), BF), ((rows, DI), BF), ((rows, DI), BF), ((rows, DI), BF), ((rows, LANES), F32),
         ((nb, NS, DI), BF), ((NS, DI), BF), ((8, DI), F32)],
        [pltpu.VMEM((2 * LANES, DI), BF), wide, wide, wide, wide, wide,
         pltpu.VMEM((NS, DI), F32), pltpu.VMEM((1, DI), F32), pltpu.VMEM((shards, *wg[0].shape), BF),
         pltpu.VMEM((wo_own.shape[0], DI, wo_own.shape[2]), BF),
         pltpu.SemaphoreType.DMA((copy_count(count - 1, shards),)),
         pltpu.SemaphoreType.DMA((copy_count(count - 1, shards, shards),))],
        35_000_000_000, 40 << 20, "gating",
    )(cont, x, dy, normed, inner, y, tot, sloc, sin, gg, sk, *wg, wo_own)


def back(cont, inner, vp, cs, cin, stp, sig, tot, tott, sc, dmix, yd, din, cw, sp, sk, ch, width):
    rows = inner.shape[0]
    nb = rows // L
    return call(
        back_kernel, nb,
        [rows_of(2 * NS, nb, DI // (2 * NS)), rows_of(DI, nb), rows_of(CH, nb), rows_of(CH, nb), rows_of(LANES, nb),
         rows_of(LANES, nb), rows_of(LANES, nb), lead_of(nb, LANES, L), lead_of(nb, NS, DI), rows_of(DI, nb),
         rows_of(LANES, nb), whole(NS, DI), whole(8, CH), whole(8, LANES), whole(1, DI), whole(8, CH)],
        [rows_of(width, nb), pl.BlockSpec((width, L), lambda b, cont: (0, nb - 1 - b)), fixed(16, width),
         fixed(width, LANES), fixed(8, CH), fixed(8, LANES)],
        [((rows, width), BF), ((width, rows), BF), ((16, width), BF), ((width, LANES), BF), ((8, CH), F32),
         ((8, LANES), F32)],
        [pltpu.VMEM((NS, DI), F32), pltpu.VMEM((2 * LANES, DI), BF), pltpu.VMEM((L, DI), F32),
         pltpu.VMEM((CH // LANES, L + 8, LANES), F32), pltpu.VMEM((L, L), F32), pltpu.VMEM((L, L), F32),
         pltpu.VMEM((2, 2, L, TILE), F32), pltpu.VMEM((L, DI), BF), pltpu.VMEM((L, DI), BF), pltpu.VMEM((8, DI), F32),
         pltpu.VMEM((2, L, DI), BF)],
        60_000_000_000, 30 << 20, "back",
    )(cont, inner, vp, cs, cin, stp, sig, tot, tott, sc, dmix, yd, din, cw, sp, sk, ch)


def wide_grad(cont, gn, dy, normed, dgate, reps, shards):
    rows = dy.shape[0]
    block = DI // shards
    shape = (reps, shards, 2 * DI // reps, D // shards)
    return call(
        wide_grad_kernel, shards,
        [pl.BlockSpec((rows, block), lambda k, c: (0, k)), whole(rows, D), whole(rows, D),
         pl.BlockSpec((rows, block), lambda k, c: (0, k))],
        anywhere(1),
        [(shape, BF)],
        [pltpu.VMEM(shape, BF), pltpu.SemaphoreType.DMA((shards, 2 * reps))], 8_600_000_000, 24 << 20, "wide_grad",
    )(cont, gn, dy, normed, dgate)[0]


def conv_grad(cont, normed, turned, nh, turned_halo, reps, shards, other):
    width, rows = turned.shape
    nb = rows // L
    m = D // shards
    half, part = width // 2, width // reps
    return call(
        partial(conv_grad_kernel, nb), shards,
        [pl.BlockSpec((rows, m), lambda k, c: (0, c[nb + 1] ^ k)),
         pl.BlockSpec((half, rows), lambda k, c: (lax.rem(c[nb + 2], 2) ^ other, 0)),
         pl.BlockSpec((LANES, m), lambda k, c: (0, c[nb + 1] ^ k)),
         pl.BlockSpec((half, LANES), lambda k, c: (lax.rem(c[nb + 2], 2) ^ other, 0))],
        [pl.BlockSpec((reps // 2, 1, part, m), lambda k, c: (0, k, 0, 0))],
        [((reps // 2, shards, part, m), BF)],
        [], 5_000_000_000, 8 << 20, "conv_grad",
    )(cont, normed, turned, nh, turned_halo)[0]


def input_grad(cont, x, dy, gp, dgate, ahead, ng, wc, wg, shards):
    rows, width = gp.shape
    nb = rows // L
    convs, gates = len(wc), len(wg)
    return call(
        partial(input_grad_kernel, convs, gates), nb,
        [rows_of(D), rows_of(D), rows_of(width), rows_of(DI), whole(16, width), whole(1, D), *anywhere(convs + gates)],
        [rows_of(D), fixed(8, D)],
        [((rows, D), BF), ((8, D), F32)],
        [pltpu.VMEM((shards, *wc[0].shape), BF), pltpu.VMEM((shards, *wg[0].shape), BF),
         pltpu.SemaphoreType.DMA((copy_count(convs - 1, shards),)), pltpu.SemaphoreType.DMA((copy_count(gates - 1, shards),)),
         pltpu.VMEM((L, D), F32)],
        10_000_000_000, 24 << 20, "input_grad",
    )(cont, x, dy, gp, dgate, ahead, ng, *wc, *wg)


def finish_wide(cont, wide):
    reps, rows, m = wide.shape
    shards = D // m
    steps = 4
    return call(
        finish_wide_kernel, steps,
        [pl.BlockSpec((reps // steps, rows, m), lambda i, c: (i, 0, 0))],
        [pl.BlockSpec(memory_space=pl.ANY), pl.BlockSpec((DI // shards // steps, D), lambda i, c: (i, 0))],
        [((DI + CH + H, m), F32), ((DI // shards, D), F32)],
        [pltpu.VMEM((steps, DI // steps, m), F32), pltpu.SemaphoreType.DMA((steps,))],
        1_000_000, 8 << 20, "finish_wide",
    )(cont, wide)


def finish_conv(cont, nb, pieces, gin, part):
    rows, m = pieces[0].shape
    count = len(pieces)
    flat = (rows - part) // 2 * m
    return call(
        partial(finish_conv_kernel, nb, count, part), 1,
        [*[whole(rows, m)] * count, pl.BlockSpec(memory_space=pl.ANY)],
        [pl.BlockSpec(memory_space=pl.ANY), fixed(1, flat)],
        [(gin.shape, F32), ((1, flat), F32)],
        [pltpu.VMEM((count, part, m), F32), pltpu.SemaphoreType.DMA((count,))],
        1_000_000, 5 << 20, "finish_conv", {1 + count: 0},
    )(cont, *pieces, gin)


def shift(v, by):
    n = lax.axis_size(BOTH)
    return lax.ppermute(v, BOTH, [(i, (i + by) % n) for i in range(n)])


def swap(v, mask):
    n = lax.axis_size(BOTH)
    return lax.ppermute(v, BOTH, [(i, i ^ mask) for i in range(n)])


def part_of(w):
    reps = lax.axis_size("rep")
    part = w.shape[0] // reps
    return lax.dynamic_slice(w, (slot_of(lax.axis_index("rep"), reps) * part, 0), (part, w.shape[1]))


def over_reps(column):
    reps, shards = lax.axis_size("rep"), lax.axis_size("shard")
    return [column] + [swap(column, 2 * shards * j) for j in range(1, reps // 2)]


def over_cores(plane):
    shards = lax.axis_size("shard")
    other = [swap(v, shards) for v in plane]
    return [v for pair in zip(plane, other) for v in pair]


def after(value, *first):
    return lax.optimization_barrier((value, first))[0]


def total_of(first, *others):
    out = first.astype(F32)
    for v in others:
        out = out + v.astype(F32)
    return out.astype(first.dtype)


def two_halves(v, m):
    rows = -(-v.size // (16 * m)) * 16
    v = jnp.pad(v, (0, rows * m - v.size)).reshape(rows, m)
    hi = v.astype(BF)
    return jnp.concatenate([hi, (v - hi.astype(F32)).astype(BF)], 0)


def one_value(v):
    half = v.shape[0] // 2
    return v[:half].astype(F32) + v[half:].astype(F32)


def local(
    tokens, cotangent, seq_lengths, deal_order, norm_gain, in_proj, conv_weight, conv_bias, step_bias, decay_log,
    skip_gain, gate_gain, out_proj,
):
    n = lax.axis_size(BOTH)
    me = lax.axis_index(BOTH)
    reps, shards = lax.axis_size("rep"), lax.axis_size("shard")
    rep, mine = lax.axis_index("rep"), lax.axis_index("shard")
    rows = tokens.shape[0]
    nb = rows // L
    unit = lcm(LANES, 16 * reps)
    width = -(-(CH + LANES) // unit) * unit

    seqs = seq_lengths.shape[0]
    order = jnp.arange(seqs, dtype=jnp.int32)
    starts = jnp.sum(jnp.where(order[None, :] < order[:, None], seq_lengths[None, :], 0), 1)
    edge = (me * nb + jnp.arange(nb + 1, dtype=jnp.int32)) * L
    cont = jnp.where(jnp.any(starts[None, :] == edge[:, None], 1) | (edge >= n * rows), 0, 1)
    cont = jnp.concatenate([cont.astype(jnp.int32), jnp.stack([mine, rep]).astype(jnp.int32)])

    turned = in_proj.T
    wcs = jnp.pad(turned[DI:], ((0, width - CH - H), (0, 0)))
    wgs = turned[:DI]
    m = wcs.shape[1]
    own_small = [*conv_weight, conv_bias, gate_gain, norm_gain, step_bias, decay_log, skip_gain]
    count = sum(v.size for v in own_small)
    extra = -(-count // (16 * m)) * 16
    small, at = jnp.zeros((extra * m,), BF), 0
    for v in own_small:
        small = small + lax.pad(v, jnp.zeros((), BF), [(at, extra * m - at - v.size, 0)])
        at += v.size
    piece = jnp.concatenate([part_of(wcs), small.reshape(extra, m)], 0)
    small = small[:count]
    part = width // reps
    column = [swap(piece, k) for k in range(1, shards)]
    small = jnp.stack([small] + [v[part:].reshape(-1)[:count] for v in column])
    conv_column = jnp.stack(column)
    halo = shift(tokens[rows - 16 :], 1)
    wo_own = jnp.stack([out_proj[:, at] for at in tiles(D, m)])
    out_rows = out_proj.shape[0] // reps
    out_part = lax.dynamic_slice(wo_own, (0, slot_of(rep, reps) * out_rows, 0), (D // m, out_rows, m))
    piece = jnp.concatenate([part_of(wgs), out_part.reshape(-1, m)], 0)
    gate_column = lax.all_gather(piece, "shard", axis=0)
    gate_column = jnp.take(gate_column, mine ^ jnp.arange(1, shards), axis=0)
    small = jnp.take(small, mine ^ jnp.arange(shards), axis=0).astype(F32)
    sizes = [conv_weight.size, conv_bias.size, gate_gain.size, norm_gain.size, step_bias.size, decay_log.size,
             skip_gain.size]
    parts, at = [], 0
    for size in sizes:
        parts.append(small[:, at : at + size])
        at += size
    taps = parts[0].reshape(shards, CONVW, -1).transpose(1, 0, 2).reshape(CONVW, CH)
    cw = jnp.concatenate([taps, parts[1].reshape(1, CH), jnp.zeros((3, CH), F32)], 0)
    gg = parts[2].reshape(1, DI)
    ng = parts[3].reshape(1, D)
    rate_scale = jnp.exp(parts[5].reshape(1, H))
    sp = jnp.pad(jnp.concatenate([parts[4].reshape(1, H), rate_scale], 0), ((0, 6), (0, LANES - H)))
    sk = jnp.repeat(parts[6].reshape(1, H), P_SIZE, axis=1)

    conv_plane = over_reps(conv_column)
    wc = [wcs, *over_cores(conv_plane[:1] + after(conv_plane[1:], gate_column))]
    gate_plane = over_reps(after(gate_column, conv_plane))

    normed, inner, vp, cs, cin, stp, sig, tot, tott, sloc, fin, nh, ch = front(cont, tokens, halo, ng, wc, cw, sp, shards)
    sin = shift(fin, 1)
    y = scan(cont, inner, vp, tot, tott)
    wg = [wgs, *over_cores(gate_plane[:1] + after(gate_plane[1:], y, sin))]
    output, gn, dgate, dmix, yd, sc, dlead, sums = gating(
        cont, tokens, cotangent, normed, inner, y, tot, sloc, sin, wg, wo_own, gg, sk, shards
    )
    din = shift(dlead, -1)
    wide = after(wide_grad(cont, gn, cotangent, normed, dgate, reps, shards), din)
    wide = lax.psum_scatter(wide, "rep", scatter_dimension=0, tiled=True)[0]
    gp, turned_gp, gph, turned_gph, csum, hsum = back(cont, inner, vp, cs, cin, stp, sig, tot, tott, sc, dmix, yd, din, cw, sp, sk, ch, width)

    ahead = shift(gph, -1)
    theirs = swap(after(conv_grad(cont, normed, turned_gp, nh, turned_gph, reps, shards, 1), ahead), shards)
    w = conv_grad(cont, normed, turned_gp, nh, turned_gph, reps, shards, 0)
    w = [total_of(w[j], theirs[j]) for j in range(reps // 2)]
    gp = after(gp, w, wide)
    wide = lax.psum_scatter(after(wide, w), "shard", scatter_dimension=0, tiled=True)[0]
    grad_tokens, grad_norm = input_grad(cont, tokens, cotangent, gp, dgate, ahead, ng, wc, wg, shards)
    csum, hsum, sums, grad_norm, wide = lax.optimization_barrier((csum, hsum, sums, grad_norm, wide))
    wide = lax.all_gather(wide, "rep", axis=0)
    packed = jnp.concatenate(
        [csum[0:CONVW].reshape(CONVW, shards, -1).transpose(1, 0, 2).reshape(shards, -1), csum[4].reshape(shards, -1),
         sums[0].reshape(shards, -1), grad_norm.sum(0).reshape(shards, -1), hsum[0, :H].reshape(shards, -1),
         hsum[1, :H].reshape(shards, -1), sums[1].reshape(H, P_SIZE).sum(1).reshape(shards, -1)], 1)
    packed = jnp.take(packed, mine ^ jnp.arange(shards), axis=0)
    others = [swap(w[j], 2 * shards * j) for j in range(1, reps // 2)]
    halves = [two_halves(packed[k], m) for k in range(shards)]
    others, halves = lax.optimization_barrier((others, halves))
    w = total_of(w[0], *others)
    w = [jnp.concatenate([w[k], halves[k]], 0) for k in range(shards)]
    w = w[:1] + [swap(w[k], k) for k in range(1, shards)]
    rest = sum(one_value(v[part:]) for v in w)
    w = jnp.concatenate([total_of(*[v[:part] for v in w]), two_halves(rest.reshape(-1), m)], 0)
    pieces = over_cores(over_reps(w))
    gin, grad_out = finish_wide(cont, wide)
    grad_in, small = finish_conv(cont, nb, pieces, gin, part)
    grad_in = grad_in.T
    own = small.reshape(-1)
    got, at = [], 0
    for size in sizes:
        got.append(own[at : at + size])
        at += size
    return (
        output, grad_tokens, got[3], grad_in, got[0].reshape(CONVW, -1), got[1], got[4], got[5], got[6], got[2],
        grad_out,
    )


def solution(mesh):
    both = P(BOTH, None)
    in_specs = (
        both, both, P(), P(), P("shard"), P("shard", None), P(None, "shard"), P("shard"), P("shard"), P("shard"),
        P("shard"), P("shard"), P("shard", None),
    )
    out_specs = (
        both, both, P("shard"), P("shard", None), P(None, "shard"), P("shard"), P("shard"), P("shard"), P("shard"),
        P("shard"), P("shard", None),
    )
    return jax.shard_map(local, mesh=mesh, in_specs=in_specs, out_specs=out_specs, check_vma=False)
```

```python
from functools import partial
from math import lcm

import jax
import jax.numpy as jnp
from jax import lax
from jax.experimental import pallas as pl
from jax.experimental.pallas import tpu as pltpu
from jax.sharding import PartitionSpec as P

D = 1024
DI = 2048
H = 32
P_SIZE = 64
NS = 128
CONVW = 4
CH = DI + 2 * NS
L = 256
LANES = 128
TILE = 256
EPSILON = 1e-05
LOG2E = 1.4426950408889634
VMEM = 58 << 20
F32 = jnp.float32
BF = jnp.bfloat16
NN = (((1,), (0,)), ((), ()))
NT = (((1,), (1,)), ((), ()))
TN = (((0,), (0,)), ((), ()))
BOTH = ("rep", "shard")


def dot(a, b, dims=NN):
    return lax.dot_general(a, b, dims, preferred_element_type=F32)


def sigmoid(v):
    return 0.5 * jnp.tanh(0.5 * v) + 0.5


def silu_and_slope(v):
    half = 0.5 * v
    bent = jnp.tanh(half)
    part = half * bent
    return half + part, (0.5 + 0.5 * bent) * (1.0 + half - part)


def split2(v):
    hi = v.astype(BF)
    return jnp.concatenate([hi, (v - hi.astype(F32)).astype(BF)], 1)


def tri_sum(tri, v):
    hi = v.astype(BF)
    rest = v - hi.astype(F32)
    mid = rest.astype(BF)
    low = (rest - mid.astype(F32)).astype(BF)
    got = dot(tri, jnp.concatenate([hi, mid, low], 1))
    return got[:, :LANES] + got[:, LANES : 2 * LANES] + got[:, 2 * LANES :]


def head_spread():
    row = lax.broadcasted_iota(jnp.int32, (2 * LANES, DI), 0)
    col = lax.broadcasted_iota(jnp.int32, (2 * LANES, DI), 1)
    return jnp.where((row % LANES) == col // P_SIZE, 1.0, 0.0).astype(BF)


def head_sum(v, e2, at):
    hi = v.astype(BF)
    low = (v - hi.astype(F32)).astype(BF)
    return dot(hi, e2[0:LANES, at], NT) + dot(low, e2[0:LANES, at], NT)


def triangle(kind, up):
    row = lax.broadcasted_iota(jnp.int32, (L, L), 0)
    col = lax.broadcasted_iota(jnp.int32, (L, L), 1)
    return jnp.where(row <= col if up else row >= col, 1.0, 0.0).astype(kind)


def tile_at(t, size=TILE):
    return pl.ds(pl.multiple_of(t * size, size), size)


def tiles(width, size=TILE):
    return [slice(t, t + size) for t in range(0, width, size)]


STEP = 64


def pieces_of(at):
    for lanes in range(at.start, at.stop, LANES):
        for q in range(0, L, STEP):
            yield slice(q, q + STEP), slice(lanes, lanes + LANES), slice(lanes - at.start, lanes - at.start + LANES)


def fold(v):
    return jnp.sum(v.reshape(STEP // 8, 8, LANES), 0)


def staged(parts, first, then):
    first(0, parts[0])
    for i, part in enumerate(parts):
        if i + 1 < len(parts):
            first(i + 1, parts[i + 1])
        then(i, part)


def slot_of(rep, reps):
    return lax.rem(rep, 2) * (reps // 2) + rep // 2


def span(first, size):
    return pl.ds(pl.multiple_of(first, 16), size)


def features(refs, place, part, shard, rep, reps):
    made = [(refs[0], place.at[shard])]
    for i, ref in enumerate(refs[1:]):
        first = slot_of(rep ^ i, reps) * part
        for k in range(1, ref.shape[0] + 1):
            source = ref.at[k - 1] if part == ref.shape[1] else ref.at[k - 1, pl.ds(0, part)]
            made.append((source, place.at[shard ^ k, span(first, part)]))
    return made


def rows_behind(own, refs, place, skip, shard, rep, reps):
    groups, n, _ = own.shape
    part = n // reps
    made = [(own.at[u], place.at[u, span(shard * n, n)]) for u in range(groups)]
    for i, ref in enumerate(refs):
        first = slot_of(rep ^ i, reps) * part
        for k in range(1, ref.shape[0] + 1):
            for u in range(groups):
                source = ref.at[k - 1, pl.ds(skip + u * part, part)]
                made.append((source, place.at[u, span((shard ^ k) * n + first, part)]))
    return made


def across(a, w, rows):
    m = w.shape[2]
    out = dot(a[:, 0:m], w[0, rows], NT)
    for s in range(1, w.shape[0]):
        out = out + dot(a[:, s * m : (s + 1) * m], w[s, rows], NT)
    return out


def copies_of(made, sems):
    return [pltpu.make_async_copy(source, place, sems.at[i]) for i, (source, place) in enumerate(made)]


def copy_count(reps, shards, each=1):
    return each + reps * (shards - 1) * each


def rms(x, gain):
    xf = x.astype(F32)
    inv = lax.rsqrt(jnp.mean(xf * xf, 1, keepdims=True) + EPSILON)
    return (xf * inv * gain).astype(BF)


def front_kernel(count, cont, x_ref, xh_ref, ng_ref, cw_ref, sp_ref, *rest):
    wrefs = rest[:count]
    (normed_ref, inner_ref, vp_ref, cs_ref, cin_ref, stp_ref, sig_ref, tot_ref, tott_ref, sloc_ref, fin_ref, nh_ref, ch_ref,
     cbuf, state, e2, part, weight, wc, sems) = rest[count:]
    b = pl.program_id(0)
    nb = pl.num_programs(0)
    gain = ng_ref[...]

    @pl.when(b == 0)
    def _():
        loads = copies_of(features(wrefs, wc, wc.shape[1] // (count - 1), cont[nb + 1], cont[nb + 2], count - 1), sems)
        for c in loads:
            c.start()
        e2[...] = head_spread()
        state[...] = jnp.zeros_like(state)
        halo = rms(xh_ref[...], gain)
        nh_ref[...] = jnp.zeros_like(nh_ref)
        nh_ref[0:16] = halo
        for c in loads:
            c.wait()
        for at in tiles(CH):
            c = across(halo, wc, at)[8:16]
            ch_ref[:, at] = c
            for u in range(TILE // LANES):
                cbuf[at.start // LANES + u, 0:8, :] = c[:, u * LANES : (u + 1) * LANES]

    @pl.when(b > 0)
    def _():
        cbuf[:, 0:8, :] = cbuf[:, L : L + 8, :]

    keep = cont[b].astype(F32)
    cbuf[:, 0:8, :] = cbuf[:, 0:8, :] * keep
    normed = rms(x_ref[...], gain)
    normed_ref[...] = normed

    raw = across(normed, wc, slice(CH, CH + LANES)) + sp_ref[0:1, :]
    small = jnp.exp(-jnp.abs(raw))
    series = small * (1.0 - small * (0.5 - small * (1.0 / 3.0)))
    step = jnp.maximum(raw, 0.0) + jnp.where(small < 0.01, series, jnp.log(1.0 + small))
    rate = -sp_ref[1:2, :] * step
    total = tri_sum(triangle(BF, False), rate)
    stp_ref[...] = step
    sig_ref[...] = sigmoid(raw)
    tot_ref[...] = total
    tott_ref[0] = total.T
    last = total[L - 1 : L, :]
    steps = split2(step)
    leaving = split2(jnp.exp(last - total))
    kept = dot(split2(jnp.exp(jnp.broadcast_to(last, (8, LANES)))), e2[...])[0:1]
    state[...] = state[...] * keep
    sloc_ref[0] = state[...].astype(BF)

    def project(i, at):
        c = across(normed, wc, at)
        for u in range(TILE // LANES):
            cbuf[at.start // LANES + u, 8 : L + 8, :] = c[:, u * LANES : (u + 1) * LANES]
        if at.start < DI:
            weight[i % 2, 0] = dot(steps, e2[:, at])
            weight[i % 2, 1] = dot(leaving, e2[:, at])

    def convolve(i, at):
        for rows, lanes, within in pieces_of(at):
            lo = 8 + rows.start
            buf = cbuf.at[lanes.start // LANES]
            here = buf[lo : lo + STEP, :]
            cin_ref[rows, lanes] = here.astype(BF)
            acc = cw_ref[4:5, lanes] + cw_ref[3:4, lanes] * here
            for back in range(1, CONVW):
                acc = acc + cw_ref[3 - back : 4 - back, lanes] * buf[lo - back : lo - back + STEP, :]
            v, slope = silu_and_slope(acc)
            cs_ref[rows, lanes] = slope.astype(BF)
            inner_ref[rows, lanes] = v.astype(BF)
            if at.start < DI:
                v = v * weight[i % 2, 0, rows, within]
                vp_ref[rows, lanes] = v.astype(BF)
                part[rows, lanes] = (v * weight[i % 2, 1, rows, within]).astype(BF)

    staged([slice(DI, CH)] + tiles(DI), project, convolve)
    keys = inner_ref[:, DI : DI + NS].T
    for at in tiles(DI):
        state[:, at] = state[:, at] * kept[:, at] + dot(keys, part[:, at])

    @pl.when(b == nb - 1)
    def _():
        fin_ref[...] = state[...].astype(BF)


def scan_kernel(cont, kq_ref, vp_ref, tot_ref, tott_ref, y_ref, gm):
    total = tot_ref[...] * LOG2E
    keys = kq_ref[:, :NS]
    queries = kq_ref[:, NS:]
    gm[...] = dot(queries, keys, NT) * triangle(F32, False)
    half = L // 2
    lane = lax.broadcasted_iota(jnp.int32, (L, LANES), 1)

    @pl.loop(0, H // 8)
    def _(g):
        cols = pltpu.roll(total, lax.rem(LANES - 8 * g, LANES), 1)
        rows = tott_ref[0, pl.ds(pl.multiple_of(g * 8, 8), 8), :] * LOG2E
        for pair in range(4):
            at = tile_at(g * 4 + pair, LANES)
            both = vp_ref[:, at]
            top, low = 0.0, 0.0
            for odd in range(2):
                i = 2 * pair + odd
                mine = jnp.where((lane >= P_SIZE) == (odd == 1), both, jnp.zeros_like(both))
                col = cols[:, i : i + 1]
                row = rows[i : i + 1, :]
                p0 = jnp.exp2(jnp.minimum(col[:half] - row[:, :half], 0.0)) * gm[:half, :half]
                p1 = jnp.exp2(col[half:] - row[:, :half]) * gm[half:, :half]
                p2 = jnp.exp2(jnp.minimum(col[half:] - row[:, half:], 0.0)) * gm[half:, half:]
                top = top + dot(p0.astype(BF), mine[:half])
                low = low + dot(jnp.concatenate([p1.astype(BF), p2.astype(BF)], 1), mine)
            y_ref[0:half, at] = top
            y_ref[half:L, at] = low


def gate_kernel(
    count, cont, x_ref, dy_ref, normed_ref, inner_ref, y_ref, tot_ref, sloc_ref, sin_ref, gg_ref, sk_ref, *rest
):
    grefs, own_ref = rest[:count], rest[count]
    (out_ref, gn_ref, dgate_ref, dmix_ref, yd_ref, sc_ref, dlead_ref, sums_ref,
     e2, gate, gated, dn, etot, yfull, dlead, lead, wg, wo, gsems, osems) = rest[count + 1 :]
    b = pl.program_id(0)
    nb = pl.num_programs(0)

    @pl.when(b == 0)
    def _():
        place = cont[nb + 1], cont[nb + 2], count - 1
        part = DI // (count - 1)
        loads = copies_of(features(grefs, wg, part, *place), gsems)
        loads += copies_of(rows_behind(own_ref, grefs[1:], wo, part, *place), osems)
        for c in loads:
            c.start()
        e2[...] = head_spread()
        dlead[...] = jnp.zeros_like(dlead)
        sums_ref[...] = jnp.zeros_like(sums_ref)
        lead[...] = jnp.ones_like(lead)
        for c in loads:
            c.wait()

    keep = cont[b].astype(F32)
    first = cont[0].astype(F32)
    lead[...] = lead[...] * jnp.where(b == 0, 1.0, keep)
    normed = normed_ref[...]
    queries = inner_ref[:, DI + NS :]
    reach = split2(jnp.exp(tot_ref[...]))
    square = jnp.zeros((L, TILE), F32)
    for at in tiles(DI):
        g = across(normed, wg, at)
        gate[:, at] = g
        start = (sloc_ref[0, :, at].astype(F32) + (lead[0:1, at] * first) * sin_ref[:, at].astype(F32)).astype(BF)
        sc_ref[0, :, at] = start
        e = dot(reach, e2[:, at])
        etot[:, at] = e
        y = y_ref[:, at] + e * dot(queries, start)
        yfull[:, at] = y
        v = (y + sk_ref[:, at] * inner_ref[:, at].astype(F32)) * silu_and_slope(g)[0]
        gated[:, at] = v
        square = square + v * v
    rinv = lax.rsqrt(jnp.sum(square, 1, keepdims=True) * (1.0 / DI) + EPSILON)
    for at in tiles(DI):
        gn_ref[:, at] = (gated[:, at] * rinv * gg_ref[:, at]).astype(BF)
    dy = dy_ref[...]
    inner_sum = jnp.zeros((L, TILE), F32)
    for at in tiles(DI):
        back = across(dy, wo, at)
        v = gated[:, at]
        sums_ref[0:1, at] += jnp.sum(back * (v * rinv), 0, keepdims=True)
        back = back * gg_ref[:, at]
        dn[:, at] = back
        inner_sum = inner_sum + back * v
    for u, at in enumerate(tiles(D, wo.shape[2])):
        out_ref[:, at] = (x_ref[:, at].astype(F32) + dot(gn_ref[...], wo[u])).astype(BF)
    shared = jnp.sum(inner_sum, 1, keepdims=True) * (1.0 / DI) * (rinv * rinv * rinv)
    turned = queries.T
    yd = jnp.zeros((L, LANES), F32)
    for at in tiles(DI):
        dgated = rinv * dn[:, at] - gated[:, at] * shared
        s, slope = silu_and_slope(gate[:, at])
        y = yfull[:, at]
        v = inner_ref[:, at].astype(F32)
        dgate_ref[:, at] = (dgated * (y + sk_ref[:, at] * v) * slope).astype(BF)
        dmix = (dgated * s).astype(BF)
        dmix_ref[:, at] = dmix
        dmix = dmix.astype(F32)
        sums_ref[1:2, at] += jnp.sum(dmix * v, 0, keepdims=True)
        yd = yd + head_sum(dmix * y, e2, at)
        dlead[:, at] += lead[0:1, at] * dot(turned, (dmix * etot[:, at]).astype(BF))
    yd_ref[...] = yd
    lead[...] = lead[...] * etot[L - 1 : L, :]

    @pl.when(b == nb - 1)
    def _():
        dlead_ref[...] = dlead[...].astype(BF)


def back_kernel(
    cont, kq_ref, vp_ref, cs_ref, cin_ref, stp_ref, sig_ref, tot_ref, tott_ref, sc_ref, dmix_ref, yd_ref, din_ref,
    cw_ref, sp_ref, sk_ref, ch_ref,
    gp_ref, turned_ref, gph_ref, turned_halo_ref, csum_ref, hsum_ref,
    dstate, e2, z, dbuf, gt, dgt, weight, sent, reached, ends, fine,
):
    nb = pl.num_programs(0)
    b = nb - 1 - pl.program_id(0)
    after = cont[b + 1].astype(F32)

    @pl.when(b == nb - 1)
    def _():
        e2[...] = head_spread()
        dstate[...] = din_ref[...].astype(F32)
        csum_ref[...] = jnp.zeros_like(csum_ref)
        hsum_ref[...] = jnp.zeros_like(hsum_ref)
        dbuf[:, L : L + 8, :] = jnp.zeros((CH // LANES, 8, LANES), F32)

    @pl.when(b < nb - 1)
    def _():
        dbuf[:, L : L + 8, :] = dbuf[:, 0:8, :] * after

    dstate[...] = dstate[...] * after
    step = stp_ref[...]
    total = tot_ref[...]
    last = total[L - 1 : L, :]
    keys = kq_ref[:, :NS]
    queries = kq_ref[:, NS:]
    gt[...] = dot(keys, queries, NT) * triangle(F32, True)
    dgt[...] = jnp.zeros_like(dgt)
    steps = split2(step)
    leaving = split2(jnp.exp(last - total))
    reach = split2(jnp.exp(total))
    kept = dot(split2(jnp.exp(jnp.broadcast_to(last, (8, LANES)))), e2[...])[0:1]

    turned = queries.T
    ended = dstate[...].astype(BF)

    def spread(i, at):
        z[:, at] = dot(keys, ended[:, at])
        weight[i % 2, 0] = dot(leaving, e2[:, at])
        weight[i % 2, 1] = dot(reach, e2[:, at])

    def reweigh(i, at):
        for u in range(TILE // LANES):
            summed = jnp.zeros((8, LANES), F32)
            for rows, lanes, _ in pieces_of(slice(at.start + u * LANES, at.start + (u + 1) * LANES)):
                within = slice(u * LANES, (u + 1) * LANES)
                w = weight[i % 2, 0, rows, within]
                scaled = w * z[rows, lanes]
                z[rows, lanes] = scaled
                v = vp_ref[rows, lanes].astype(F32)
                summed = summed + fold(v * scaled)
                sent[rows, lanes] = (v * w).astype(BF)
                reached[rows, lanes] = (dmix_ref[rows, lanes].astype(F32) * weight[i % 2, 1, rows, within]).astype(BF)
            ends[:, lanes] = summed

    staged(tiles(DI), spread, reweigh)
    dk = dot(sent[...], ended, NT)
    dq = dot(reached[...], sc_ref[0], NT)
    for at in tiles(DI):
        old = dstate[:, at] * kept[:, at]
        ends[:, at] += jnp.sum((old * sc_ref[0, :, at].astype(F32)).reshape(NS // 8, 8, TILE), 0)
        dstate[:, at] = old + dot(turned, reached[:, at])
    ends_hi = ends[...].astype(BF)
    ends_lo = (ends[...] - ends_hi.astype(F32)).astype(BF)
    at_end = dot(ends_hi, e2[0:LANES], NT) + dot(ends_lo, e2[0:LANES], NT)
    at_end = jnp.sum(at_end, 0, keepdims=True)
    scaled_total = total * LOG2E

    half = L // 2
    lane = lax.broadcasted_iota(jnp.int32, (L, LANES), 1)

    @pl.loop(0, H // 8)
    def _(g):
        cols = pltpu.roll(scaled_total, lax.rem(LANES - 8 * g, LANES), 1)
        rows = tott_ref[0, pl.ds(pl.multiple_of(g * 8, 8), 8), :] * LOG2E
        for pair in range(4):
            at = tile_at(g * 4 + pair, LANES)
            dy = dmix_ref[:, at]
            v = vp_ref[:, at]
            top = z[0:half, at]
            low = z[half:L, at]
            for odd in range(2):
                i = 2 * pair + odd
                mine = jnp.where((lane >= P_SIZE) == (odd == 1), dy, jnp.zeros_like(dy))
                col = cols[:, i : i + 1]
                row = rows[i : i + 1, :]
                e0 = jnp.exp2(jnp.minimum(row[:, :half] - col[:half], 0.0))
                e1 = jnp.exp2(row[:, half:] - col[:half])
                e2_ = jnp.exp2(jnp.minimum(row[:, half:] - col[half:], 0.0))
                p0 = (e0 * gt[:half, :half]).astype(BF)
                p1 = (e1 * gt[:half, half:]).astype(BF)
                p2 = (e2_ * gt[half:, half:]).astype(BF)
                top = top + dot(jnp.concatenate([p0, p1], 1), mine)
                low = low + dot(p2, mine[half:])
                d = dot(v[:half], mine, NT)
                dgt[:half, :half] += e0 * d[:, :half]
                dgt[:half, half:] += e1 * d[:, half:]
                dgt[half:, half:] += e2_ * dot(v[half:], mine[half:], NT)
            z[0:half, at] = top
            z[half:L, at] = low

    masked = (dgt[...] * triangle(F32, True)).astype(BF)
    dk = dk + dot(masked, queries)
    dq = dq + dot(masked, keys, TN)

    def respread(i, at):
        weight[i % 2, 0] = dot(steps, e2[:, at])

    def unwind(i, at):
        for rows, lanes, within in pieces_of(at):
            dvp = z[rows, lanes]
            p = dvp * vp_ref[rows, lanes].astype(F32)
            hi = p.astype(BF)
            fine[0, rows, lanes] = hi
            fine[1, rows, lanes] = (p - hi.astype(F32)).astype(BF)
            dv = weight[i % 2, 0, rows, within] * dvp + sk_ref[:, lanes] * dmix_ref[rows, lanes].astype(F32)
            dbuf[lanes.start // LANES, rows, :] = dv * cs_ref[rows, lanes].astype(F32)

    staged(tiles(DI), respread, unwind)
    own = dot(fine[0], e2[0:LANES], NT) + dot(fine[1], e2[0:LANES], NT)
    slope = cs_ref[:, DI:].astype(F32)
    dbuf[DI // LANES, 0:L, :] = dk * slope[:, :NS]
    dbuf[DI // LANES + 1, 0:L, :] = dq * slope[:, NS:]

    row = lax.broadcasted_iota(jnp.int32, (L, LANES), 0)
    dtotal = yd_ref[...] - own + jnp.where(row == L - 1, at_end, 0.0)
    drate = tri_sum(triangle(BF, True), dtotal)
    decay = sp_ref[1:2, :]
    dstep = own / jnp.maximum(step, 1e-30) - decay * drate
    draw = jnp.where(lax.broadcasted_iota(jnp.int32, (L, LANES), 1) < H, dstep * sig_ref[...], 0.0)
    gp_ref[:, CH : CH + LANES] = draw.astype(BF)
    turned_ref[CH : CH + LANES, :] = draw.astype(BF).T
    if gp_ref.shape[1] > CH + LANES:
        gp_ref[:, CH + LANES :] = jnp.zeros((L, gp_ref.shape[1] - CH - LANES), BF)
        turned_ref[CH + LANES :, :] = jnp.zeros((gp_ref.shape[1] - CH - LANES, L), BF)
    hsum_ref[0:1, :] += jnp.sum(draw, 0, keepdims=True)
    hsum_ref[1:2, :] += jnp.sum(-decay * step * drate, 0, keepdims=True)

    for lt in range(CH // LANES):
        at = slice(lt * LANES, (lt + 1) * LANES)
        sums = [jnp.zeros((8, LANES), F32) for _ in range(CONVW + 1)]
        made = []
        for q in range(L // 64):
            lo = 64 * q
            here = dbuf[lt, lo : lo + 64, :]
            c = cin_ref[lo : lo + 64, at].astype(F32)
            acc = cw_ref[3:4, at] * here
            sums[3] = sums[3] + jnp.sum((here * c).reshape(8, 8, LANES), 0)
            sums[4] = sums[4] + jnp.sum(here.reshape(8, 8, LANES), 0)
            for ahead in range(1, CONVW):
                there = dbuf[lt, lo + ahead : lo + ahead + 64, :]
                acc = acc + cw_ref[3 - ahead : 4 - ahead, at] * there
                sums[3 - ahead] = sums[3 - ahead] + jnp.sum((there * c).reshape(8, 8, LANES), 0)
            made.append(acc.astype(BF))
            gp_ref[lo : lo + 64, at] = made[-1]
        turned_ref[at, :] = jnp.concatenate(made, 0).T
        for k in range(CONVW + 1):
            csum_ref[k : k + 1, at] += jnp.sum(sums[k], 0, keepdims=True)

    @pl.when(b == 0)
    def _():
        gph_ref[...] = jnp.zeros_like(gph_ref)
        turned_halo_ref[...] = jnp.zeros_like(turned_halo_ref)
        for lt in range(CH // LANES):
            at = slice(lt * LANES, (lt + 1) * LANES)
            d = dbuf[lt, 0:8, :] * cont[0].astype(F32)
            d0, d1, d2 = d[0:1], d[1:2], d[2:3]
            w0, w1, w2 = cw_ref[0:1, at], cw_ref[1:2, at], cw_ref[2:3, at]
            c5, c6, c7 = ch_ref[5:6, at], ch_ref[6:7, at], ch_ref[7:8, at]
            made = [jnp.zeros((13, LANES), F32), w0 * d0, w1 * d0 + w0 * d1, w2 * d0 + w1 * d1 + w0 * d2]
            made = jnp.concatenate(made, 0)
            gph_ref[:, at] = made.astype(BF)
            turned_halo_ref[at, :] = jnp.concatenate([made, jnp.zeros((LANES - 16, LANES), F32)], 0).T.astype(BF)
            csum_ref[0:1, at] += c5 * d0 + c6 * d1 + c7 * d2
            csum_ref[1:2, at] += c6 * d0 + c7 * d1
            csum_ref[2:3, at] += c7 * d0


def wide_grad_kernel(cont, gn_ref, dy_ref, normed_ref, dgate_ref, out_ref, buf, sems):
    k = pl.program_id(0)
    reps, shards, _, m = buf.shape
    o = dot(gn_ref[...], dy_ref[...], TN).astype(BF)
    part = o.shape[0] // reps
    first = D // m * part
    each = reps // shards

    def copies(step):
        made = [(r, step, pl.ds(0, first)) for r in range(reps)]
        made += [(step * each + i, s, pl.ds(first, DI // reps)) for i in range(each) for s in range(shards)]
        return [
            pltpu.make_async_copy(buf.at[at], out_ref.at[at], sems.at[step, i]) for i, at in enumerate(made)
        ]

    for r in range(reps):
        for u in range(D // m):
            buf[r, k, u * part : (u + 1) * part, :] = o[r * part : (r + 1) * part, u * m : (u + 1) * m]
    part = DI // reps
    g = dot(dgate_ref[...], normed_ref[...], TN).astype(BF)
    for i in range(each):
        for s in range(shards):
            buf[k * each + i, s, first:, :] = g[i * part : (i + 1) * part, s * m : (s + 1) * m]
    for c in copies(k):
        c.start()

    @pl.when(k == shards - 1)
    def _():
        for step in range(shards):
            for c in copies(step):
                c.wait()


def conv_grad_kernel(nb, cont, normed_ref, turned_ref, nh_ref, turned_halo_ref, out_ref):
    half, _, part, _ = out_ref.shape
    full = (dot(turned_ref[...], normed_ref[...]) + dot(turned_halo_ref[...], nh_ref[...])).astype(BF)
    for chip in range(half):
        out_ref[(cont[nb + 2] // 2) ^ chip, 0] = full[chip * part : (chip + 1) * part]


def input_grad_kernel(convs, gates, cont, x_ref, dy_ref, gp_ref, dgate_ref, ahead_ref, ng_ref, *rest):
    crefs, grefs = rest[:convs], rest[convs : convs + gates]
    gt_ref, gn_ref, wc, wg, csems, gsems, acc = rest[convs + gates :]
    b = pl.program_id(0)
    nb = pl.num_programs(0)

    @pl.when(b == 0)
    def _():
        place = cont[nb + 1], cont[nb + 2], convs - 1
        loads = copies_of(features(crefs, wc, wc.shape[1] // (convs - 1), *place), csems)
        loads += copies_of(features(grefs, wg, DI // (convs - 1), *place), gsems)
        for c in loads:
            c.start()
        gn_ref[...] = jnp.zeros_like(gn_ref)
        for c in loads:
            c.wait()

    m = wc.shape[2]
    for s, at in enumerate(tiles(D, m)):
        acc[:, at] = dot(gp_ref[...], wc[s]) + dot(dgate_ref[...], wg[s])

    @pl.when(b == nb - 1)
    def _():
        keep = cont[nb].astype(F32)
        for s, at in enumerate(tiles(D, m)):
            acc[L - 16 : L, at] += keep * dot(ahead_ref[...], wc[s])

    for q in range(L // 32):
        rows = slice(32 * q, 32 * q + 32)
        x = x_ref[rows].astype(F32)
        inv = lax.rsqrt(jnp.mean(x * x, 1, keepdims=True) + EPSILON)
        g = acc[rows]
        gn_ref[...] += jnp.sum((g * (x * inv)).reshape(4, 8, D), 0)
        v = g * ng_ref[...]
        mean = jnp.mean(v * x, 1, keepdims=True)
        gt_ref[rows] = (inv * v - x * (inv * inv * inv * mean) + dy_ref[rows].astype(F32)).astype(BF)


def finish_wide_kernel(nb, count, cont, *rest):
    pieces = rest[:count]
    gin_ref, gout_ref, buf, lines, sems = rest[count:]
    part, m = buf.shape[1:]
    rows = lines.shape[1]

    def copies(i):
        place = cont[nb + 2] ^ i
        first = pl.ds(pl.multiple_of(place * part, 16), part)
        second = pl.ds(pl.multiple_of(place * rows, 16), rows)
        return [
            pltpu.make_async_copy(buf.at[i], gin_ref.at[first], sems.at[0, i]),
            pltpu.make_async_copy(lines.at[i], gout_ref.at[second], sems.at[1, i]),
        ]

    for i, piece in enumerate(pieces):
        buf[i] = piece[rows * D // m :].astype(F32)
        for u in range(D // m):
            lines[i, :, u * m : (u + 1) * m] = piece[u * rows : (u + 1) * rows].astype(F32)
        for c in copies(i):
            c.start()
    for i in range(count):
        for c in copies(i):
            c.wait()


def finish_conv_kernel(nb, count, part, cont, *rest):
    pieces = rest[:count]
    gin_ref, small_ref, buf, sems = rest[count + 1 :]
    full, left = divmod(CH + H, part)

    def each(i, act):
        place = slot_of(cont[nb + 2] ^ i, count)
        first = pl.multiple_of(DI + place * part, 16)

        @pl.when(place < full)
        def _():
            act(pltpu.make_async_copy(buf.at[i], gin_ref.at[pl.ds(first, part)], sems.at[i]))

        if left:

            @pl.when(place == full)
            def _():
                act(pltpu.make_async_copy(buf.at[i, pl.ds(0, left)], gin_ref.at[pl.ds(first, left)], sems.at[i]))

    for i, piece in enumerate(pieces):
        buf[i] = piece[0:part].astype(F32)
        each(i, lambda c: c.start())
    m = buf.shape[2]
    half = small_ref.shape[0]
    small = jnp.zeros((half, m), F32)
    for piece in pieces:
        small = small + (piece[part : part + half].astype(F32) + piece[part + half :].astype(F32))
    small_ref[...] = small
    for i in range(count):
        each(i, lambda c: c.wait())


def rows_of(width, reverse=0, column=0):
    if reverse:
        return pl.BlockSpec((L, width), lambda b, cont: (reverse - 1 - b, column))
    return pl.BlockSpec((L, width), lambda b, cont: (b, column))


def whole(*shape):
    return pl.BlockSpec(shape, lambda b, cont: (0,) * len(shape), pipeline_mode=pl.Buffered(1))


def fixed(*shape):
    return pl.BlockSpec(shape, lambda b, cont: (0,) * len(shape))


def lead_of(reverse, *shape):
    if reverse:
        return pl.BlockSpec((1, *shape), lambda b, cont: (reverse - 1 - b, 0, 0))
    return pl.BlockSpec((1, *shape), lambda b, cont: (b, 0, 0))


def anywhere(count):
    return [pl.BlockSpec(memory_space=pl.ANY)] * count


def call(kernel, grid, in_specs, out_specs, outs, scratch, flops, nbytes, name, aliases=None):
    return pl.pallas_call(
        kernel,
        grid_spec=pltpu.PrefetchScalarGridSpec(
            num_scalar_prefetch=1, grid=(grid,), in_specs=in_specs, out_specs=out_specs, scratch_shapes=scratch
        ),
        out_shape=[jax.ShapeDtypeStruct(s, d) for s, d in outs],
        input_output_aliases=aliases or {},
        compiler_params=pltpu.CompilerParams(vmem_limit_bytes=VMEM),
        cost_estimate=pl.CostEstimate(flops=flops, bytes_accessed=nbytes, transcendentals=0),
        name=name,
    )


def loaded(count, shards, *shape):
    return [pltpu.VMEM(shape, BF), pltpu.SemaphoreType.DMA((copy_count(count - 1, shards),))]


def front(cont, x, xh, ng, wc, cw, sp, shards):
    rows = x.shape[0]
    nb = rows // L
    count = len(wc)
    return call(
        partial(front_kernel, count), nb,
        [rows_of(D), whole(16, D), whole(1, D), whole(8, CH), whole(8, LANES), *anywhere(count)],
        [rows_of(D), rows_of(CH), rows_of(DI), rows_of(CH), rows_of(CH), rows_of(LANES), rows_of(LANES), rows_of(LANES),
         lead_of(0, LANES, L), lead_of(0, NS, DI), fixed(NS, DI), fixed(LANES, D), fixed(8, CH)],
        [((rows, D), BF), ((rows, CH), BF), ((rows, DI), BF), ((rows, CH), BF), ((rows, CH), BF), ((rows, LANES), F32),
         ((rows, LANES), F32), ((rows, LANES), F32), ((nb, LANES, L), F32), ((nb, NS, DI), BF), ((NS, DI), BF),
         ((LANES, D), BF), ((8, CH), F32)],
        [pltpu.VMEM((CH // LANES, L + 8, LANES), F32), pltpu.VMEM((NS, DI), F32), pltpu.VMEM((2 * LANES, DI), BF),
         pltpu.VMEM((L, DI), BF), pltpu.VMEM((2, 2, L, TILE), F32), *loaded(count, shards, shards, *wc[0].shape)],
        1_000_000, 1 << 20, "front",
    )(cont, x, xh, ng, cw, sp, *wc)


def scan(cont, inner, vp, tot, tott):
    rows = inner.shape[0]
    nb = rows // L
    return call(
        scan_kernel, nb,
        [rows_of(2 * NS, 0, DI // (2 * NS)), rows_of(DI), rows_of(LANES), lead_of(0, LANES, L)],
        [rows_of(DI)],
        [((rows, DI), F32)],
        [pltpu.VMEM((L, L), F32)],
        1_000_000, 1 << 20, "scan",
    )(cont, inner, vp, tot, tott)[0]


def gating(cont, x, dy, normed, inner, y, tot, sloc, sin, wg, wo_own, gg, sk, shards):
    rows = x.shape[0]
    nb = rows // L
    count = len(wg)
    wide = pltpu.VMEM((L, DI), F32)
    return call(
        partial(gate_kernel, count), nb,
        [rows_of(D), rows_of(D), rows_of(D), rows_of(CH), rows_of(DI), rows_of(LANES), lead_of(0, NS, DI), whole(NS, DI),
         whole(1, DI), whole(1, DI), *anywhere(count + 1)],
        [rows_of(D), rows_of(DI), rows_of(DI), rows_of(DI), rows_of(LANES), lead_of(0, NS, DI), fixed(NS, DI),
         fixed(8, DI)],
        [((rows, D), BF), ((rows, DI), BF), ((rows, DI), BF), ((rows, DI), BF), ((rows, LANES), F32),
         ((nb, NS, DI), BF), ((NS, DI), BF), ((8, DI), F32)],
        [pltpu.VMEM((2 * LANES, DI), BF), wide, wide, wide, wide, wide,
         pltpu.VMEM((NS, DI), F32), pltpu.VMEM((1, DI), F32), pltpu.VMEM((shards, *wg[0].shape), BF),
         pltpu.VMEM((wo_own.shape[0], DI, wo_own.shape[2]), BF),
         pltpu.SemaphoreType.DMA((copy_count(count - 1, shards),)),
         pltpu.SemaphoreType.DMA((copy_count(count - 1, shards, shards),))],
        35_000_000_000, 40 << 20, "gating",
    )(cont, x, dy, normed, inner, y, tot, sloc, sin, gg, sk, *wg, wo_own)


def back(cont, inner, vp, cs, cin, stp, sig, tot, tott, sc, dmix, yd, din, cw, sp, sk, ch, width):
    rows = inner.shape[0]
    nb = rows // L
    return call(
        back_kernel, nb,
        [rows_of(2 * NS, nb, DI // (2 * NS)), rows_of(DI, nb), rows_of(CH, nb), rows_of(CH, nb), rows_of(LANES, nb),
         rows_of(LANES, nb), rows_of(LANES, nb), lead_of(nb, LANES, L), lead_of(nb, NS, DI), rows_of(DI, nb),
         rows_of(LANES, nb), whole(NS, DI), whole(8, CH), whole(8, LANES), whole(1, DI), whole(8, CH)],
        [rows_of(width, nb), pl.BlockSpec((width, L), lambda b, cont: (0, nb - 1 - b)), fixed(16, width),
         fixed(width, LANES), fixed(8, CH), fixed(8, LANES)],
        [((rows, width), BF), ((width, rows), BF), ((16, width), BF), ((width, LANES), BF), ((8, CH), F32),
         ((8, LANES), F32)],
        [pltpu.VMEM((NS, DI), F32), pltpu.VMEM((2 * LANES, DI), BF), pltpu.VMEM((L, DI), F32),
         pltpu.VMEM((CH // LANES, L + 8, LANES), F32), pltpu.VMEM((L, L), F32), pltpu.VMEM((L, L), F32),
         pltpu.VMEM((2, 2, L, TILE), F32), pltpu.VMEM((L, DI), BF), pltpu.VMEM((L, DI), BF), pltpu.VMEM((8, DI), F32),
         pltpu.VMEM((2, L, DI), BF)],
        60_000_000_000, 30 << 20, "back",
    )(cont, inner, vp, cs, cin, stp, sig, tot, tott, sc, dmix, yd, din, cw, sp, sk, ch)


def wide_grad(cont, gn, dy, normed, dgate, reps, shards):
    rows = dy.shape[0]
    block = DI // shards
    shape = (reps, shards, 2 * DI // reps, D // shards)
    return call(
        wide_grad_kernel, shards,
        [pl.BlockSpec((rows, block), lambda k, c: (0, k)), whole(rows, D), whole(rows, D),
         pl.BlockSpec((rows, block), lambda k, c: (0, k))],
        anywhere(1),
        [(shape, BF)],
        [pltpu.VMEM(shape, BF), pltpu.SemaphoreType.DMA((shards, 2 * reps))], 8_600_000_000, 24 << 20, "wide_grad",
    )(cont, gn, dy, normed, dgate)[0]


def conv_grad(cont, normed, turned, nh, turned_halo, reps, shards, other):
    width, rows = turned.shape
    nb = rows // L
    m = D // shards
    half, part = width // 2, width // reps
    return call(
        partial(conv_grad_kernel, nb), shards,
        [pl.BlockSpec((rows, m), lambda k, c: (0, c[nb + 1] ^ k)),
         pl.BlockSpec((half, rows), lambda k, c: (lax.rem(c[nb + 2], 2) ^ other, 0)),
         pl.BlockSpec((LANES, m), lambda k, c: (0, c[nb + 1] ^ k)),
         pl.BlockSpec((half, LANES), lambda k, c: (lax.rem(c[nb + 2], 2) ^ other, 0))],
        [pl.BlockSpec((reps // 2, 1, part, m), lambda k, c: (0, k, 0, 0))],
        [((reps // 2, shards, part, m), BF)],
        [], 5_000_000_000, 8 << 20, "conv_grad",
    )(cont, normed, turned, nh, turned_halo)[0]


def input_grad(cont, x, dy, gp, dgate, ahead, ng, wc, wg, shards):
    rows, width = gp.shape
    nb = rows // L
    convs, gates = len(wc), len(wg)
    return call(
        partial(input_grad_kernel, convs, gates), nb,
        [rows_of(D), rows_of(D), rows_of(width), rows_of(DI), whole(16, width), whole(1, D), *anywhere(convs + gates)],
        [rows_of(D), fixed(8, D)],
        [((rows, D), BF), ((8, D), F32)],
        [pltpu.VMEM((shards, *wc[0].shape), BF), pltpu.VMEM((shards, *wg[0].shape), BF),
         pltpu.SemaphoreType.DMA((copy_count(convs - 1, shards),)), pltpu.SemaphoreType.DMA((copy_count(gates - 1, shards),)),
         pltpu.VMEM((L, D), F32)],
        10_000_000_000, 24 << 20, "input_grad",
    )(cont, x, dy, gp, dgate, ahead, ng, *wc, *wg)


def finish_wide(cont, nb, pieces):
    rows, m = pieces[0].shape
    count = len(pieces)
    part = DI // count
    lines = DI * m // D // count
    return call(
        partial(finish_wide_kernel, nb, count), 1,
        [whole(rows, m)] * count,
        anywhere(2),
        [((DI + CH + H, m), F32), ((lines * count, D), F32)],
        [pltpu.VMEM((count, part, m), F32), pltpu.VMEM((count, lines, D), F32), pltpu.SemaphoreType.DMA((2, count))],
        1_000_000, 8 << 20, "finish_wide",
    )(cont, *pieces)


def finish_conv(cont, nb, pieces, gin, part):
    rows, m = pieces[0].shape
    count = len(pieces)
    half = (rows - part) // 2
    return call(
        partial(finish_conv_kernel, nb, count, part), 1,
        [*[whole(rows, m)] * count, pl.BlockSpec(memory_space=pl.ANY)],
        [pl.BlockSpec(memory_space=pl.ANY), fixed(half, m)],
        [(gin.shape, F32), ((half, m), F32)],
        [pltpu.VMEM((count, part, m), F32), pltpu.SemaphoreType.DMA((count,))],
        1_000_000, 5 << 20, "finish_conv", {1 + count: 0},
    )(cont, *pieces, gin)


def shift(v, by):
    n = lax.axis_size(BOTH)
    return lax.ppermute(v, BOTH, [(i, (i + by) % n) for i in range(n)])


def swap(v, mask):
    n = lax.axis_size(BOTH)
    return lax.ppermute(v, BOTH, [(i, i ^ mask) for i in range(n)])


def part_of(w):
    reps = lax.axis_size("rep")
    part = w.shape[0] // reps
    return lax.dynamic_slice(w, (slot_of(lax.axis_index("rep"), reps) * part, 0), (part, w.shape[1]))


def over_reps(column):
    reps, shards = lax.axis_size("rep"), lax.axis_size("shard")
    return [column] + [swap(column, 2 * shards * j) for j in range(1, reps // 2)]


def over_cores(plane):
    shards = lax.axis_size("shard")
    other = [swap(v, shards) for v in plane]
    return [v for pair in zip(plane, other) for v in pair]


def after(value, *first):
    return lax.optimization_barrier((value, first))[0]


def total_of(first, *others):
    out = first.astype(F32)
    for v in others:
        out = out + v.astype(F32)
    return out.astype(first.dtype)


def two_halves(v, m):
    rows = -(-v.size // (16 * m)) * 16
    v = jnp.pad(v, (0, rows * m - v.size)).reshape(rows, m)
    hi = lax.reduce_precision(v, 8, 7)
    return jnp.concatenate([hi, v - hi], 0).astype(BF)


def one_value(v):
    half = v.shape[0] // 2
    return v[:half].astype(F32) + v[half:].astype(F32)


def local(
    tokens, cotangent, seq_lengths, deal_order, norm_gain, in_proj, conv_weight, conv_bias, step_bias, decay_log,
    skip_gain, gate_gain, out_proj,
):
    n = lax.axis_size(BOTH)
    me = lax.axis_index(BOTH)
    reps, shards = lax.axis_size("rep"), lax.axis_size("shard")
    rep, mine = lax.axis_index("rep"), lax.axis_index("shard")
    rows = tokens.shape[0]
    nb = rows // L
    unit = lcm(LANES, 16 * reps)
    width = -(-(CH + LANES) // unit) * unit

    seqs = seq_lengths.shape[0]
    order = jnp.arange(seqs, dtype=jnp.int32)
    starts = jnp.sum(jnp.where(order[None, :] < order[:, None], seq_lengths[None, :], 0), 1)
    edge = (me * nb + jnp.arange(nb + 1, dtype=jnp.int32)) * L
    cont = jnp.where(jnp.any(starts[None, :] == edge[:, None], 1) | (edge >= n * rows), 0, 1)
    cont = jnp.concatenate([cont.astype(jnp.int32), jnp.stack([mine, rep]).astype(jnp.int32)])

    turned = in_proj.T
    wcs = jnp.pad(turned[DI:], ((0, width - CH - H), (0, 0)))
    wgs = turned[:DI]
    m = wcs.shape[1]
    own_small = [*conv_weight, conv_bias, gate_gain, norm_gain, step_bias, decay_log, skip_gain]
    count = sum(v.size for v in own_small)
    extra = -(-count // (16 * m)) * 16
    small, at = jnp.zeros((extra * m,), BF), 0
    for v in own_small:
        small = small + lax.pad(v, jnp.zeros((), BF), [(at, extra * m - at - v.size, 0)])
        at += v.size
    piece = jnp.concatenate([part_of(wcs), small.reshape(extra, m)], 0)
    small = small[:count]
    part = width // reps
    column = [swap(piece, k) for k in range(1, shards)]
    small = jnp.stack([small] + [v[part:].reshape(-1)[:count] for v in column])
    conv_column = jnp.stack(column)
    halo = shift(tokens[rows - 16 :], 1)
    wo_own = jnp.stack([out_proj[:, at] for at in tiles(D, m)])
    out_rows = out_proj.shape[0] // reps
    out_part = lax.dynamic_slice(wo_own, (0, slot_of(rep, reps) * out_rows, 0), (D // m, out_rows, m))
    piece = jnp.concatenate([part_of(wgs), out_part.reshape(-1, m)], 0)
    gate_column = lax.all_gather(piece, "shard", axis=0)
    gate_column = jnp.take(gate_column, mine ^ jnp.arange(1, shards), axis=0)
    small = jnp.take(small, mine ^ jnp.arange(shards), axis=0).astype(F32)
    sizes = [conv_weight.size, conv_bias.size, gate_gain.size, norm_gain.size, step_bias.size, decay_log.size,
             skip_gain.size]
    parts, at = [], 0
    for size in sizes:
        parts.append(small[:, at : at + size])
        at += size
    taps = parts[0].reshape(shards, CONVW, -1).transpose(1, 0, 2).reshape(CONVW, CH)
    cw = jnp.concatenate([taps, parts[1].reshape(1, CH), jnp.zeros((3, CH), F32)], 0)
    gg = parts[2].reshape(1, DI)
    ng = parts[3].reshape(1, D)
    rate_scale = jnp.exp(parts[5].reshape(1, H))
    sp = jnp.pad(jnp.concatenate([parts[4].reshape(1, H), rate_scale], 0), ((0, 6), (0, LANES - H)))
    sk = jnp.repeat(parts[6].reshape(1, H), P_SIZE, axis=1)

    conv_plane = over_reps(conv_column)
    wc = [wcs, *over_cores(conv_plane[:1] + after(conv_plane[1:], gate_column))]
    gate_plane = over_reps(after(gate_column, conv_plane))

    normed, inner, vp, cs, cin, stp, sig, tot, tott, sloc, fin, nh, ch = front(cont, tokens, halo, ng, wc, cw, sp, shards)
    sin = shift(fin, 1)
    y = scan(cont, inner, vp, tot, tott)
    wg = [wgs, *over_cores(gate_plane[:1] + after(gate_plane[1:], y, sin))]
    output, gn, dgate, dmix, yd, sc, dlead, sums = gating(
        cont, tokens, cotangent, normed, inner, y, tot, sloc, sin, wg, wo_own, gg, sk, shards
    )
    din = shift(dlead, -1)
    wide = after(wide_grad(cont, gn, cotangent, normed, dgate, reps, shards), din)
    wide = lax.psum_scatter(wide, "rep", scatter_dimension=0, tiled=True)[0]
    gp, turned_gp, gph, turned_gph, csum, hsum = back(cont, inner, vp, cs, cin, stp, sig, tot, tott, sc, dmix, yd, din, cw, sp, sk, ch, width)

    ahead = shift(gph, -1)
    theirs = swap(after(conv_grad(cont, normed, turned_gp, nh, turned_gph, reps, shards, 1), ahead), shards)
    w = conv_grad(cont, normed, turned_gp, nh, turned_gph, reps, shards, 0)
    w = [total_of(w[j], theirs[j]) for j in range(reps // 2)]
    gp = after(gp, w, wide)
    wide = lax.psum_scatter(after(wide, w), "shard", scatter_dimension=0, tiled=True)[0]
    grad_tokens, grad_norm = input_grad(cont, tokens, cotangent, gp, dgate, ahead, ng, wc, wg, shards)
    csum, hsum, sums, grad_norm = lax.optimization_barrier((csum, hsum, sums, grad_norm))
    csum, wide = lax.optimization_barrier((csum, wide))
    wide = over_cores(over_reps(wide))
    packed = jnp.concatenate(
        [csum[0:CONVW].reshape(CONVW, shards, -1).transpose(1, 0, 2).reshape(shards, -1), csum[4].reshape(shards, -1),
         sums[0].reshape(shards, -1), grad_norm.sum(0).reshape(shards, -1), hsum[0, :H].reshape(shards, -1),
         hsum[1, :H].reshape(shards, -1), sums[1].reshape(H, P_SIZE).sum(1).reshape(shards, -1)], 1)
    packed = jnp.take(packed, mine ^ jnp.arange(shards), axis=0)
    others = [swap(w[j], 2 * shards * j) for j in range(1, reps // 2)]
    halves = [two_halves(packed[k], m) for k in range(shards)]
    others, halves = lax.optimization_barrier((others, halves))
    w = total_of(w[0], *others)
    w = [jnp.concatenate([w[k], halves[k]], 0) for k in range(shards)]
    w = w[:1] + [swap(w[k], k) for k in range(1, shards)]
    rest = sum(one_value(v[part:]) for v in w)
    w = jnp.concatenate([total_of(*[v[:part] for v in w]), two_halves(rest.reshape(-1), m)], 0)
    pieces = over_cores(over_reps(w))
    gin, grad_out = finish_wide(cont, nb, wide)
    grad_in, small = finish_conv(cont, nb, pieces, gin, part)
    grad_in = grad_in.T
    own = small.reshape(-1)
    got, at = [], 0
    for size in sizes:
        got.append(own[at : at + size])
        at += size
    return (
        output, grad_tokens, got[3], grad_in, got[0].reshape(CONVW, -1), got[1], got[4], got[5], got[6], got[2],
        grad_out,
    )


def solution(mesh):
    both = P(BOTH, None)
    in_specs = (
        both, both, P(), P(), P("shard"), P("shard", None), P(None, "shard"), P("shard"), P("shard"), P("shard"),
        P("shard"), P("shard"), P("shard", None),
    )
    out_specs = (
        both, both, P("shard"), P("shard", None), P(None, "shard"), P("shard"), P("shard"), P("shard"), P("shard"),
        P("shard"), P("shard", None),
    )
    return jax.shard_map(local, mesh=mesh, in_specs=in_specs, out_specs=out_specs, check_vma=False)
```

```python
from functools import partial
from math import lcm

import jax
import jax.numpy as jnp
from jax import lax
from jax.experimental import pallas as pl
from jax.experimental.pallas import tpu as pltpu
from jax.sharding import PartitionSpec as P

D = 1024
DI = 2048
H = 32
P_SIZE = 64
NS = 128
CONVW = 4
CH = DI + 2 * NS
L = 256
LANES = 128
TILE = 256
EPSILON = 1e-05
LOG2E = 1.4426950408889634
VMEM = 58 << 20
F32 = jnp.float32
BF = jnp.bfloat16
NN = (((1,), (0,)), ((), ()))
NT = (((1,), (1,)), ((), ()))
TN = (((0,), (0,)), ((), ()))
BOTH = ("rep", "shard")


def dot(a, b, dims=NN):
    return lax.dot_general(a, b, dims, preferred_element_type=F32)


def sigmoid(v):
    return 0.5 * jnp.tanh(0.5 * v) + 0.5


def silu_and_slope(v):
    half = 0.5 * v
    bent = jnp.tanh(half)
    part = half * bent
    return half + part, (0.5 + 0.5 * bent) * (1.0 + half - part)


def split2(v):
    hi = v.astype(BF)
    return jnp.concatenate([hi, (v - hi.astype(F32)).astype(BF)], 1)


def tri_sum(tri, v):
    hi = v.astype(BF)
    rest = v - hi.astype(F32)
    mid = rest.astype(BF)
    low = (rest - mid.astype(F32)).astype(BF)
    got = dot(tri, jnp.concatenate([hi, mid, low], 1))
    return got[:, :LANES] + got[:, LANES : 2 * LANES] + got[:, 2 * LANES :]


def head_spread():
    row = lax.broadcasted_iota(jnp.int32, (2 * LANES, DI), 0)
    col = lax.broadcasted_iota(jnp.int32, (2 * LANES, DI), 1)
    return jnp.where((row % LANES) == col // P_SIZE, 1.0, 0.0).astype(BF)


def head_sum(v, e2, at):
    hi = v.astype(BF)
    low = (v - hi.astype(F32)).astype(BF)
    return dot(hi, e2[0:LANES, at], NT) + dot(low, e2[0:LANES, at], NT)


def triangle(kind, up):
    row = lax.broadcasted_iota(jnp.int32, (L, L), 0)
    col = lax.broadcasted_iota(jnp.int32, (L, L), 1)
    return jnp.where(row <= col if up else row >= col, 1.0, 0.0).astype(kind)


def tile_at(t, size=TILE):
    return pl.ds(pl.multiple_of(t * size, size), size)


def tiles(width, size=TILE):
    return [slice(t, t + size) for t in range(0, width, size)]


STEP = 64


def pieces_of(at):
    for lanes in range(at.start, at.stop, LANES):
        for q in range(0, L, STEP):
            yield slice(q, q + STEP), slice(lanes, lanes + LANES), slice(lanes - at.start, lanes - at.start + LANES)


def fold(v):
    return jnp.sum(v.reshape(STEP // 8, 8, LANES), 0)


def staged(parts, first, then):
    first(0, parts[0])
    for i, part in enumerate(parts):
        if i + 1 < len(parts):
            first(i + 1, parts[i + 1])
        then(i, part)


def slot_of(rep, reps):
    return lax.rem(rep, 2) * (reps // 2) + rep // 2


def span(first, size):
    return pl.ds(pl.multiple_of(first, 16), size)


def features(refs, place, part, shard, rep, reps):
    made = [(refs[0], place.at[shard])]
    for i, ref in enumerate(refs[1:]):
        first = slot_of(rep ^ i, reps) * part
        for k in range(1, ref.shape[0] + 1):
            source = ref.at[k - 1] if part == ref.shape[1] else ref.at[k - 1, pl.ds(0, part)]
            made.append((source, place.at[shard ^ k, span(first, part)]))
    return made


def rows_behind(own, refs, place, skip, shard, rep, reps):
    groups, n, _ = own.shape
    part = n // reps
    made = [(own.at[u], place.at[u, span(shard * n, n)]) for u in range(groups)]
    for i, ref in enumerate(refs):
        first = slot_of(rep ^ i, reps) * part
        for k in range(1, ref.shape[0] + 1):
            for u in range(groups):
                source = ref.at[k - 1, pl.ds(skip + u * part, part)]
                made.append((source, place.at[u, span((shard ^ k) * n + first, part)]))
    return made


def across(a, w, rows):
    m = w.shape[2]
    out = dot(a[:, 0:m], w[0, rows], NT)
    for s in range(1, w.shape[0]):
        out = out + dot(a[:, s * m : (s + 1) * m], w[s, rows], NT)
    return out


def copies_of(made, sems):
    return [pltpu.make_async_copy(source, place, sems.at[i]) for i, (source, place) in enumerate(made)]


def copy_count(reps, shards, each=1):
    return each + reps * (shards - 1) * each


def rms(x, gain):
    xf = x.astype(F32)
    inv = lax.rsqrt(jnp.mean(xf * xf, 1, keepdims=True) + EPSILON)
    return (xf * inv * gain).astype(BF)


def front_kernel(count, cont, x_ref, xh_ref, ng_ref, cw_ref, sp_ref, *rest):
    wrefs = rest[:count]
    (normed_ref, inner_ref, vp_ref, cs_ref, cin_ref, stp_ref, sig_ref, tot_ref, tott_ref, sloc_ref, fin_ref, nh_ref, ch_ref,
     cbuf, state, e2, part, weight, wc, sems) = rest[count:]
    b = pl.program_id(0)
    nb = pl.num_programs(0)
    gain = ng_ref[...]

    @pl.when(b == 0)
    def _():
        loads = copies_of(features(wrefs, wc, wc.shape[1] // (count - 1), cont[nb + 1], cont[nb + 2], count - 1), sems)
        for c in loads:
            c.start()
        e2[...] = head_spread()
        state[...] = jnp.zeros_like(state)
        halo = rms(xh_ref[...], gain)
        nh_ref[...] = jnp.zeros_like(nh_ref)
        nh_ref[0:16] = halo
        for c in loads:
            c.wait()
        for at in tiles(CH):
            c = across(halo, wc, at)[8:16]
            ch_ref[:, at] = c
            for u in range(TILE // LANES):
                cbuf[at.start // LANES + u, 0:8, :] = c[:, u * LANES : (u + 1) * LANES]

    @pl.when(b > 0)
    def _():
        cbuf[:, 0:8, :] = cbuf[:, L : L + 8, :]

    keep = cont[b].astype(F32)
    cbuf[:, 0:8, :] = cbuf[:, 0:8, :] * keep
    normed = rms(x_ref[...], gain)
    normed_ref[...] = normed

    raw = across(normed, wc, slice(CH, CH + LANES)) + sp_ref[0:1, :]
    small = jnp.exp(-jnp.abs(raw))
    series = small * (1.0 - small * (0.5 - small * (1.0 / 3.0)))
    step = jnp.maximum(raw, 0.0) + jnp.where(small < 0.01, series, jnp.log(1.0 + small))
    rate = -sp_ref[1:2, :] * step
    total = tri_sum(triangle(BF, False), rate)
    stp_ref[...] = step
    sig_ref[...] = sigmoid(raw)
    tot_ref[...] = total
    tott_ref[0] = total.T
    last = total[L - 1 : L, :]
    steps = split2(step)
    leaving = split2(jnp.exp(last - total))
    kept = dot(split2(jnp.exp(jnp.broadcast_to(last, (8, LANES)))), e2[...])[0:1]
    state[...] = state[...] * keep
    sloc_ref[0] = state[...].astype(BF)

    def project(i, at):
        c = across(normed, wc, at)
        for u in range(TILE // LANES):
            cbuf[at.start // LANES + u, 8 : L + 8, :] = c[:, u * LANES : (u + 1) * LANES]
        if at.start < DI:
            weight[i % 2, 0] = dot(steps, e2[:, at])
            weight[i % 2, 1] = dot(leaving, e2[:, at])

    def convolve(i, at):
        for rows, lanes, within in pieces_of(at):
            lo = 8 + rows.start
            buf = cbuf.at[lanes.start // LANES]
            here = buf[lo : lo + STEP, :]
            cin_ref[rows, lanes] = here.astype(BF)
            acc = cw_ref[4:5, lanes] + cw_ref[3:4, lanes] * here
            for back in range(1, CONVW):
                acc = acc + cw_ref[3 - back : 4 - back, lanes] * buf[lo - back : lo - back + STEP, :]
            v, slope = silu_and_slope(acc)
            cs_ref[rows, lanes] = slope.astype(BF)
            inner_ref[rows, lanes] = v.astype(BF)
            if at.start < DI:
                v = v * weight[i % 2, 0, rows, within]
                vp_ref[rows, lanes] = v.astype(BF)
                part[rows, lanes] = (v * weight[i % 2, 1, rows, within]).astype(BF)

    staged([slice(DI, CH)] + tiles(DI), project, convolve)
    keys = inner_ref[:, DI : DI + NS].T
    for at in tiles(DI):
        state[:, at] = state[:, at] * kept[:, at] + dot(keys, part[:, at])

    @pl.when(b == nb - 1)
    def _():
        fin_ref[...] = state[...].astype(BF)


def scan_kernel(cont, kq_ref, vp_ref, tot_ref, tott_ref, y_ref, gm):
    total = tot_ref[...] * LOG2E
    keys = kq_ref[:, :NS]
    queries = kq_ref[:, NS:]
    gm[...] = dot(queries, keys, NT) * triangle(F32, False)
    half = L // 2
    lane = lax.broadcasted_iota(jnp.int32, (L, LANES), 1)

    @pl.loop(0, H // 8)
    def _(g):
        cols = pltpu.roll(total, lax.rem(LANES - 8 * g, LANES), 1)
        rows = tott_ref[0, pl.ds(pl.multiple_of(g * 8, 8), 8), :] * LOG2E
        for pair in range(4):
            at = tile_at(g * 4 + pair, LANES)
            both = vp_ref[:, at]
            top, low = 0.0, 0.0
            for odd in range(2):
                i = 2 * pair + odd
                mine = jnp.where((lane >= P_SIZE) == (odd == 1), both, jnp.zeros_like(both))
                col = cols[:, i : i + 1]
                row = rows[i : i + 1, :]
                p0 = jnp.exp2(jnp.minimum(col[:half] - row[:, :half], 0.0)) * gm[:half, :half]
                p1 = jnp.exp2(col[half:] - row[:, :half]) * gm[half:, :half]
                p2 = jnp.exp2(jnp.minimum(col[half:] - row[:, half:], 0.0)) * gm[half:, half:]
                top = top + dot(p0.astype(BF), mine[:half])
                low = low + dot(jnp.concatenate([p1.astype(BF), p2.astype(BF)], 1), mine)
            y_ref[0:half, at] = top
            y_ref[half:L, at] = low


def gate_kernel(
    count, cont, x_ref, dy_ref, normed_ref, inner_ref, y_ref, tot_ref, sloc_ref, sin_ref, gg_ref, sk_ref, *rest
):
    grefs, own_ref = rest[:count], rest[count]
    (out_ref, gn_ref, dgate_ref, dmix_ref, yd_ref, sc_ref, dlead_ref, sums_ref,
     e2, gate, gated, dn, etot, yfull, dlead, lead, wg, wo, gsems, osems) = rest[count + 1 :]
    b = pl.program_id(0)
    nb = pl.num_programs(0)

    @pl.when(b == 0)
    def _():
        place = cont[nb + 1], cont[nb + 2], count - 1
        part = DI // (count - 1)
        loads = copies_of(features(grefs, wg, part, *place), gsems)
        loads += copies_of(rows_behind(own_ref, grefs[1:], wo, part, *place), osems)
        for c in loads:
            c.start()
        e2[...] = head_spread()
        dlead[...] = jnp.zeros_like(dlead)
        sums_ref[...] = jnp.zeros_like(sums_ref)
        lead[...] = jnp.ones_like(lead)
        for c in loads:
            c.wait()

    keep = cont[b].astype(F32)
    first = cont[0].astype(F32)
    lead[...] = lead[...] * jnp.where(b == 0, 1.0, keep)
    normed = normed_ref[...]
    queries = inner_ref[:, DI + NS :]
    reach = split2(jnp.exp(tot_ref[...]))
    square = jnp.zeros((L, TILE), F32)
    for at in tiles(DI):
        g = across(normed, wg, at)
        gate[:, at] = g
        start = (sloc_ref[0, :, at].astype(F32) + (lead[0:1, at] * first) * sin_ref[:, at].astype(F32)).astype(BF)
        sc_ref[0, :, at] = start
        e = dot(reach, e2[:, at])
        etot[:, at] = e
        y = y_ref[:, at] + e * dot(queries, start)
        yfull[:, at] = y
        v = (y + sk_ref[:, at] * inner_ref[:, at].astype(F32)) * silu_and_slope(g)[0]
        gated[:, at] = v
        square = square + v * v
    rinv = lax.rsqrt(jnp.sum(square, 1, keepdims=True) * (1.0 / DI) + EPSILON)
    for at in tiles(DI):
        gn_ref[:, at] = (gated[:, at] * rinv * gg_ref[:, at]).astype(BF)
    dy = dy_ref[...]
    inner_sum = jnp.zeros((L, TILE), F32)
    for at in tiles(DI):
        back = across(dy, wo, at)
        v = gated[:, at]
        sums_ref[0:1, at] += jnp.sum(back * (v * rinv), 0, keepdims=True)
        back = back * gg_ref[:, at]
        dn[:, at] = back
        inner_sum = inner_sum + back * v
    for u, at in enumerate(tiles(D, wo.shape[2])):
        out_ref[:, at] = (x_ref[:, at].astype(F32) + dot(gn_ref[...], wo[u])).astype(BF)
    shared = jnp.sum(inner_sum, 1, keepdims=True) * (1.0 / DI) * (rinv * rinv * rinv)
    turned = queries.T
    yd = jnp.zeros((L, LANES), F32)
    for at in tiles(DI):
        dgated = rinv * dn[:, at] - gated[:, at] * shared
        s, slope = silu_and_slope(gate[:, at])
        y = yfull[:, at]
        v = inner_ref[:, at].astype(F32)
        dgate_ref[:, at] = (dgated * (y + sk_ref[:, at] * v) * slope).astype(BF)
        dmix = (dgated * s).astype(BF)
        dmix_ref[:, at] = dmix
        dmix = dmix.astype(F32)
        sums_ref[1:2, at] += jnp.sum(dmix * v, 0, keepdims=True)
        yd = yd + head_sum(dmix * y, e2, at)
        dlead[:, at] += lead[0:1, at] * dot(turned, (dmix * etot[:, at]).astype(BF))
    yd_ref[...] = yd
    lead[...] = lead[...] * etot[L - 1 : L, :]

    @pl.when(b == nb - 1)
    def _():
        dlead_ref[...] = dlead[...].astype(BF)


def back_kernel(
    cont, kq_ref, vp_ref, cs_ref, cin_ref, stp_ref, sig_ref, tot_ref, tott_ref, sc_ref, dmix_ref, yd_ref, din_ref,
    cw_ref, sp_ref, sk_ref, ch_ref,
    gp_ref, turned_ref, gph_ref, turned_halo_ref, csum_ref, hsum_ref,
    dstate, e2, z, dbuf, gt, dgt, weight, sent, reached, ends, fine,
):
    nb = pl.num_programs(0)
    b = nb - 1 - pl.program_id(0)
    after = cont[b + 1].astype(F32)

    @pl.when(b == nb - 1)
    def _():
        e2[...] = head_spread()
        dstate[...] = din_ref[...].astype(F32)
        csum_ref[...] = jnp.zeros_like(csum_ref)
        hsum_ref[...] = jnp.zeros_like(hsum_ref)
        dbuf[:, L : L + 8, :] = jnp.zeros((CH // LANES, 8, LANES), F32)

    @pl.when(b < nb - 1)
    def _():
        dbuf[:, L : L + 8, :] = dbuf[:, 0:8, :] * after

    dstate[...] = dstate[...] * after
    step = stp_ref[...]
    total = tot_ref[...]
    last = total[L - 1 : L, :]
    keys = kq_ref[:, :NS]
    queries = kq_ref[:, NS:]
    gt[...] = dot(keys, queries, NT) * triangle(F32, True)
    dgt[...] = jnp.zeros_like(dgt)
    steps = split2(step)
    leaving = split2(jnp.exp(last - total))
    reach = split2(jnp.exp(total))
    kept = dot(split2(jnp.exp(jnp.broadcast_to(last, (8, LANES)))), e2[...])[0:1]

    turned = queries.T
    ended = dstate[...].astype(BF)

    def spread(i, at):
        z[:, at] = dot(keys, ended[:, at])
        weight[i % 2, 0] = dot(leaving, e2[:, at])
        weight[i % 2, 1] = dot(reach, e2[:, at])

    def reweigh(i, at):
        for u in range(TILE // LANES):
            summed = jnp.zeros((8, LANES), F32)
            for rows, lanes, _ in pieces_of(slice(at.start + u * LANES, at.start + (u + 1) * LANES)):
                within = slice(u * LANES, (u + 1) * LANES)
                w = weight[i % 2, 0, rows, within]
                scaled = w * z[rows, lanes]
                z[rows, lanes] = scaled
                v = vp_ref[rows, lanes].astype(F32)
                summed = summed + fold(v * scaled)
                sent[rows, lanes] = (v * w).astype(BF)
                reached[rows, lanes] = (dmix_ref[rows, lanes].astype(F32) * weight[i % 2, 1, rows, within]).astype(BF)
            ends[:, lanes] = summed

    staged(tiles(DI), spread, reweigh)
    dk = dot(sent[...], ended, NT)
    dq = dot(reached[...], sc_ref[0], NT)
    for at in tiles(DI):
        old = dstate[:, at] * kept[:, at]
        ends[:, at] += jnp.sum((old * sc_ref[0, :, at].astype(F32)).reshape(NS // 8, 8, TILE), 0)
        dstate[:, at] = old + dot(turned, reached[:, at])
    ends_hi = ends[...].astype(BF)
    ends_lo = (ends[...] - ends_hi.astype(F32)).astype(BF)
    at_end = dot(ends_hi, e2[0:LANES], NT) + dot(ends_lo, e2[0:LANES], NT)
    at_end = jnp.sum(at_end, 0, keepdims=True)
    scaled_total = total * LOG2E

    half = L // 2
    lane = lax.broadcasted_iota(jnp.int32, (L, LANES), 1)

    @pl.loop(0, H // 8)
    def _(g):
        cols = pltpu.roll(scaled_total, lax.rem(LANES - 8 * g, LANES), 1)
        rows = tott_ref[0, pl.ds(pl.multiple_of(g * 8, 8), 8), :] * LOG2E
        for pair in range(4):
            at = tile_at(g * 4 + pair, LANES)
            dy = dmix_ref[:, at]
            v = vp_ref[:, at]
            top = z[0:half, at]
            low = z[half:L, at]
            for odd in range(2):
                i = 2 * pair + odd
                mine = jnp.where((lane >= P_SIZE) == (odd == 1), dy, jnp.zeros_like(dy))
                col = cols[:, i : i + 1]
                row = rows[i : i + 1, :]
                e0 = jnp.exp2(jnp.minimum(row[:, :half] - col[:half], 0.0))
                e1 = jnp.exp2(row[:, half:] - col[:half])
                e2_ = jnp.exp2(jnp.minimum(row[:, half:] - col[half:], 0.0))
                p0 = (e0 * gt[:half, :half]).astype(BF)
                p1 = (e1 * gt[:half, half:]).astype(BF)
                p2 = (e2_ * gt[half:, half:]).astype(BF)
                top = top + dot(jnp.concatenate([p0, p1], 1), mine)
                low = low + dot(p2, mine[half:])
                d = dot(v[:half], mine, NT)
                dgt[:half, :half] += e0 * d[:, :half]
                dgt[:half, half:] += e1 * d[:, half:]
                dgt[half:, half:] += e2_ * dot(v[half:], mine[half:], NT)
            z[0:half, at] = top
            z[half:L, at] = low

    masked = (dgt[...] * triangle(F32, True)).astype(BF)
    dk = dk + dot(masked, queries)
    dq = dq + dot(masked, keys, TN)

    def respread(i, at):
        weight[i % 2, 0] = dot(steps, e2[:, at])

    def unwind(i, at):
        for rows, lanes, within in pieces_of(at):
            dvp = z[rows, lanes]
            p = dvp * vp_ref[rows, lanes].astype(F32)
            hi = p.astype(BF)
            fine[0, rows, lanes] = hi
            fine[1, rows, lanes] = (p - hi.astype(F32)).astype(BF)
            dv = weight[i % 2, 0, rows, within] * dvp + sk_ref[:, lanes] * dmix_ref[rows, lanes].astype(F32)
            dbuf[lanes.start // LANES, rows, :] = dv * cs_ref[rows, lanes].astype(F32)

    staged(tiles(DI), respread, unwind)
    own = dot(fine[0], e2[0:LANES], NT) + dot(fine[1], e2[0:LANES], NT)
    slope = cs_ref[:, DI:].astype(F32)
    dbuf[DI // LANES, 0:L, :] = dk * slope[:, :NS]
    dbuf[DI // LANES + 1, 0:L, :] = dq * slope[:, NS:]

    row = lax.broadcasted_iota(jnp.int32, (L, LANES), 0)
    dtotal = yd_ref[...] - own + jnp.where(row == L - 1, at_end, 0.0)
    drate = tri_sum(triangle(BF, True), dtotal)
    decay = sp_ref[1:2, :]
    dstep = own / jnp.maximum(step, 1e-30) - decay * drate
    draw = jnp.where(lax.broadcasted_iota(jnp.int32, (L, LANES), 1) < H, dstep * sig_ref[...], 0.0)
    gp_ref[:, CH : CH + LANES] = draw.astype(BF)
    turned_ref[CH : CH + LANES, :] = draw.astype(BF).T
    if gp_ref.shape[1] > CH + LANES:
        gp_ref[:, CH + LANES :] = jnp.zeros((L, gp_ref.shape[1] - CH - LANES), BF)
        turned_ref[CH + LANES :, :] = jnp.zeros((gp_ref.shape[1] - CH - LANES, L), BF)
    hsum_ref[0:1, :] += jnp.sum(draw, 0, keepdims=True)
    hsum_ref[1:2, :] += jnp.sum(-decay * step * drate, 0, keepdims=True)

    for lt in range(CH // LANES):
        at = slice(lt * LANES, (lt + 1) * LANES)
        sums = [jnp.zeros((8, LANES), F32) for _ in range(CONVW + 1)]
        made = []
        for q in range(L // 64):
            lo = 64 * q
            here = dbuf[lt, lo : lo + 64, :]
            c = cin_ref[lo : lo + 64, at].astype(F32)
            acc = cw_ref[3:4, at] * here
            sums[3] = sums[3] + jnp.sum((here * c).reshape(8, 8, LANES), 0)
            sums[4] = sums[4] + jnp.sum(here.reshape(8, 8, LANES), 0)
            for ahead in range(1, CONVW):
                there = dbuf[lt, lo + ahead : lo + ahead + 64, :]
                acc = acc + cw_ref[3 - ahead : 4 - ahead, at] * there
                sums[3 - ahead] = sums[3 - ahead] + jnp.sum((there * c).reshape(8, 8, LANES), 0)
            made.append(acc.astype(BF))
            gp_ref[lo : lo + 64, at] = made[-1]
        turned_ref[at, :] = jnp.concatenate(made, 0).T
        for k in range(CONVW + 1):
            csum_ref[k : k + 1, at] += jnp.sum(sums[k], 0, keepdims=True)

    @pl.when(b == 0)
    def _():
        gph_ref[...] = jnp.zeros_like(gph_ref)
        turned_halo_ref[...] = jnp.zeros_like(turned_halo_ref)
        for lt in range(CH // LANES):
            at = slice(lt * LANES, (lt + 1) * LANES)
            d = dbuf[lt, 0:8, :] * cont[0].astype(F32)
            d0, d1, d2 = d[0:1], d[1:2], d[2:3]
            w0, w1, w2 = cw_ref[0:1, at], cw_ref[1:2, at], cw_ref[2:3, at]
            c5, c6, c7 = ch_ref[5:6, at], ch_ref[6:7, at], ch_ref[7:8, at]
            made = [jnp.zeros((13, LANES), F32), w0 * d0, w1 * d0 + w0 * d1, w2 * d0 + w1 * d1 + w0 * d2]
            made = jnp.concatenate(made, 0)
            gph_ref[:, at] = made.astype(BF)
            turned_halo_ref[at, :] = jnp.concatenate([made, jnp.zeros((LANES - 16, LANES), F32)], 0).T.astype(BF)
            csum_ref[0:1, at] += c5 * d0 + c6 * d1 + c7 * d2
            csum_ref[1:2, at] += c6 * d0 + c7 * d1
            csum_ref[2:3, at] += c7 * d0


def wide_grad_kernel(cont, gn_ref, dy_ref, normed_ref, dgate_ref, out_ref, buf, sems):
    k = pl.program_id(0)
    reps, shards, _, m = buf.shape
    o = dot(gn_ref[...], dy_ref[...], TN).astype(BF)
    part = o.shape[0] // reps
    first = D // m * part
    each = reps // shards

    def copies(step):
        made = [(r, step, pl.ds(0, first)) for r in range(reps)]
        made += [(step * each + i, s, pl.ds(first, DI // reps)) for i in range(each) for s in range(shards)]
        return [
            pltpu.make_async_copy(buf.at[at], out_ref.at[at], sems.at[step, i]) for i, at in enumerate(made)
        ]

    for r in range(reps):
        for u in range(D // m):
            buf[r, k, u * part : (u + 1) * part, :] = o[r * part : (r + 1) * part, u * m : (u + 1) * m]
    part = DI // reps
    g = dot(dgate_ref[...], normed_ref[...], TN).astype(BF)
    for i in range(each):
        for s in range(shards):
            buf[k * each + i, s, first:, :] = g[i * part : (i + 1) * part, s * m : (s + 1) * m]
    for c in copies(k):
        c.start()

    @pl.when(k == shards - 1)
    def _():
        for step in range(shards):
            for c in copies(step):
                c.wait()


def conv_grad_kernel(nb, cont, normed_ref, turned_ref, nh_ref, turned_halo_ref, out_ref):
    half, _, part, _ = out_ref.shape
    full = (dot(turned_ref[...], normed_ref[...]) + dot(turned_halo_ref[...], nh_ref[...])).astype(BF)
    for chip in range(half):
        out_ref[(cont[nb + 2] // 2) ^ chip, 0] = full[chip * part : (chip + 1) * part]


def input_grad_kernel(convs, gates, cont, x_ref, dy_ref, gp_ref, dgate_ref, ahead_ref, ng_ref, *rest):
    crefs, grefs = rest[:convs], rest[convs : convs + gates]
    gt_ref, gn_ref, wc, wg, csems, gsems, acc = rest[convs + gates :]
    b = pl.program_id(0)
    nb = pl.num_programs(0)

    @pl.when(b == 0)
    def _():
        place = cont[nb + 1], cont[nb + 2], convs - 1
        loads = copies_of(features(crefs, wc, wc.shape[1] // (convs - 1), *place), csems)
        loads += copies_of(features(grefs, wg, DI // (convs - 1), *place), gsems)
        for c in loads:
            c.start()
        gn_ref[...] = jnp.zeros_like(gn_ref)
        for c in loads:
            c.wait()

    m = wc.shape[2]
    for s, at in enumerate(tiles(D, m)):
        acc[:, at] = dot(gp_ref[...], wc[s]) + dot(dgate_ref[...], wg[s])

    @pl.when(b == nb - 1)
    def _():
        keep = cont[nb].astype(F32)
        for s, at in enumerate(tiles(D, m)):
            acc[L - 16 : L, at] += keep * dot(ahead_ref[...], wc[s])

    for q in range(L // 32):
        rows = slice(32 * q, 32 * q + 32)
        x = x_ref[rows].astype(F32)
        inv = lax.rsqrt(jnp.mean(x * x, 1, keepdims=True) + EPSILON)
        g = acc[rows]
        gn_ref[...] += jnp.sum((g * (x * inv)).reshape(4, 8, D), 0)
        v = g * ng_ref[...]
        mean = jnp.mean(v * x, 1, keepdims=True)
        gt_ref[rows] = (inv * v - x * (inv * inv * inv * mean) + dy_ref[rows].astype(F32)).astype(BF)


def finish_wide_kernel(nb, count, cont, *rest):
    pieces = rest[:count]
    gin_ref, gout_ref, buf, lines, sems = rest[count:]
    part, m = buf.shape[1:]
    rows = lines.shape[1]

    def copies(i):
        place = cont[nb + 2] ^ i
        first = pl.ds(pl.multiple_of(place * part, 16), part)
        second = pl.ds(pl.multiple_of(place * rows, 16), rows)
        return [
            pltpu.make_async_copy(buf.at[i], gin_ref.at[first], sems.at[0, i]),
            pltpu.make_async_copy(lines.at[i], gout_ref.at[second], sems.at[1, i]),
        ]

    for i, piece in enumerate(pieces):
        buf[i] = piece[rows * D // m :].astype(F32)
        for u in range(D // m):
            lines[i, :, u * m : (u + 1) * m] = piece[u * rows : (u + 1) * rows].astype(F32)
        for c in copies(i):
            c.start()
    for i in range(count):
        for c in copies(i):
            c.wait()


def finish_conv_kernel(nb, count, part, cont, *rest):
    pieces = rest[:count]
    gin_ref, small_ref, buf, sems = rest[count + 1 :]
    full, left = divmod(CH + H, part)

    def each(i, act):
        place = slot_of(cont[nb + 2] ^ i, count)
        first = pl.multiple_of(DI + place * part, 16)

        @pl.when(place < full)
        def _():
            act(pltpu.make_async_copy(buf.at[i], gin_ref.at[pl.ds(first, part)], sems.at[i]))

        if left:

            @pl.when(place == full)
            def _():
                act(pltpu.make_async_copy(buf.at[i, pl.ds(0, left)], gin_ref.at[pl.ds(first, left)], sems.at[i]))

    for i, piece in enumerate(pieces):
        buf[i] = piece[0:part].astype(F32)
        each(i, lambda c: c.start())
    m = buf.shape[2]
    half = small_ref.shape[0]
    small = jnp.zeros((half, m), F32)
    for piece in pieces:
        small = small + (piece[part : part + half].astype(F32) + piece[part + half :].astype(F32))
    small_ref[...] = small
    for i in range(count):
        each(i, lambda c: c.wait())


def rows_of(width, reverse=0, column=0):
    if reverse:
        return pl.BlockSpec((L, width), lambda b, cont: (reverse - 1 - b, column))
    return pl.BlockSpec((L, width), lambda b, cont: (b, column))


def whole(*shape):
    return pl.BlockSpec(shape, lambda b, cont: (0,) * len(shape), pipeline_mode=pl.Buffered(1))


def fixed(*shape):
    return pl.BlockSpec(shape, lambda b, cont: (0,) * len(shape))


def lead_of(reverse, *shape):
    if reverse:
        return pl.BlockSpec((1, *shape), lambda b, cont: (reverse - 1 - b, 0, 0))
    return pl.BlockSpec((1, *shape), lambda b, cont: (b, 0, 0))


def anywhere(count):
    return [pl.BlockSpec(memory_space=pl.ANY)] * count


def call(kernel, grid, in_specs, out_specs, outs, scratch, flops, nbytes, name, aliases=None):
    return pl.pallas_call(
        kernel,
        grid_spec=pltpu.PrefetchScalarGridSpec(
            num_scalar_prefetch=1, grid=(grid,), in_specs=in_specs, out_specs=out_specs, scratch_shapes=scratch
        ),
        out_shape=[jax.ShapeDtypeStruct(s, d) for s, d in outs],
        input_output_aliases=aliases or {},
        compiler_params=pltpu.CompilerParams(vmem_limit_bytes=VMEM),
        cost_estimate=pl.CostEstimate(flops=flops, bytes_accessed=nbytes, transcendentals=0),
        name=name,
    )


def loaded(count, shards, *shape):
    return [pltpu.VMEM(shape, BF), pltpu.SemaphoreType.DMA((copy_count(count - 1, shards),))]


def front(cont, x, xh, ng, wc, cw, sp, shards):
    rows = x.shape[0]
    nb = rows // L
    count = len(wc)
    return call(
        partial(front_kernel, count), nb,
        [rows_of(D), whole(16, D), whole(1, D), whole(8, CH), whole(8, LANES), *anywhere(count)],
        [rows_of(D), rows_of(CH), rows_of(DI), rows_of(CH), rows_of(CH), rows_of(LANES), rows_of(LANES), rows_of(LANES),
         lead_of(0, LANES, L), lead_of(0, NS, DI), fixed(NS, DI), fixed(LANES, D), fixed(8, CH)],
        [((rows, D), BF), ((rows, CH), BF), ((rows, DI), BF), ((rows, CH), BF), ((rows, CH), BF), ((rows, LANES), F32),
         ((rows, LANES), F32), ((rows, LANES), F32), ((nb, LANES, L), F32), ((nb, NS, DI), BF), ((NS, DI), BF),
         ((LANES, D), BF), ((8, CH), F32)],
        [pltpu.VMEM((CH // LANES, L + 8, LANES), F32), pltpu.VMEM((NS, DI), F32), pltpu.VMEM((2 * LANES, DI), BF),
         pltpu.VMEM((L, DI), BF), pltpu.VMEM((2, 2, L, TILE), F32), *loaded(count, shards, shards, *wc[0].shape)],
        1_000_000, 1 << 20, "front",
    )(cont, x, xh, ng, cw, sp, *wc)


def scan(cont, inner, vp, tot, tott):
    rows = inner.shape[0]
    nb = rows // L
    return call(
        scan_kernel, nb,
        [rows_of(2 * NS, 0, DI // (2 * NS)), rows_of(DI), rows_of(LANES), lead_of(0, LANES, L)],
        [rows_of(DI)],
        [((rows, DI), F32)],
        [pltpu.VMEM((L, L), F32)],
        1_000_000, 1 << 20, "scan",
    )(cont, inner, vp, tot, tott)[0]


def gating(cont, x, dy, normed, inner, y, tot, sloc, sin, wg, wo_own, gg, sk, shards):
    rows = x.shape[0]
    nb = rows // L
    count = len(wg)
    wide = pltpu.VMEM((L, DI), F32)
    return call(
        partial(gate_kernel, count), nb,
        [rows_of(D), rows_of(D), rows_of(D), rows_of(CH), rows_of(DI), rows_of(LANES), lead_of(0, NS, DI), whole(NS, DI),
         whole(1, DI), whole(1, DI), *anywhere(count + 1)],
        [rows_of(D), rows_of(DI), rows_of(DI), rows_of(DI), rows_of(LANES), lead_of(0, NS, DI), fixed(NS, DI),
         fixed(8, DI)],
        [((rows, D), BF), ((rows, DI), BF), ((rows, DI), BF), ((rows, DI), BF), ((rows, LANES), F32),
         ((nb, NS, DI), BF), ((NS, DI), BF), ((8, DI), F32)],
        [pltpu.VMEM((2 * LANES, DI), BF), wide, wide, wide, wide, wide,
         pltpu.VMEM((NS, DI), F32), pltpu.VMEM((1, DI), F32), pltpu.VMEM((shards, *wg[0].shape), BF),
         pltpu.VMEM((wo_own.shape[0], DI, wo_own.shape[2]), BF),
         pltpu.SemaphoreType.DMA((copy_count(count - 1, shards),)),
         pltpu.SemaphoreType.DMA((copy_count(count - 1, shards, shards),))],
        35_000_000_000, 40 << 20, "gating",
    )(cont, x, dy, normed, inner, y, tot, sloc, sin, gg, sk, *wg, wo_own)


def back(cont, inner, vp, cs, cin, stp, sig, tot, tott, sc, dmix, yd, din, cw, sp, sk, ch, width):
    rows = inner.shape[0]
    nb = rows // L
    return call(
        back_kernel, nb,
        [rows_of(2 * NS, nb, DI // (2 * NS)), rows_of(DI, nb), rows_of(CH, nb), rows_of(CH, nb), rows_of(LANES, nb),
         rows_of(LANES, nb), rows_of(LANES, nb), lead_of(nb, LANES, L), lead_of(nb, NS, DI), rows_of(DI, nb),
         rows_of(LANES, nb), whole(NS, DI), whole(8, CH), whole(8, LANES), whole(1, DI), whole(8, CH)],
        [rows_of(width, nb), pl.BlockSpec((width, L), lambda b, cont: (0, nb - 1 - b)), fixed(16, width),
         fixed(width, LANES), fixed(8, CH), fixed(8, LANES)],
        [((rows, width), BF), ((width, rows), BF), ((16, width), BF), ((width, LANES), BF), ((8, CH), F32),
         ((8, LANES), F32)],
        [pltpu.VMEM((NS, DI), F32), pltpu.VMEM((2 * LANES, DI), BF), pltpu.VMEM((L, DI), F32),
         pltpu.VMEM((CH // LANES, L + 8, LANES), F32), pltpu.VMEM((L, L), F32), pltpu.VMEM((L, L), F32),
         pltpu.VMEM((2, 2, L, TILE), F32), pltpu.VMEM((L, DI), BF), pltpu.VMEM((L, DI), BF), pltpu.VMEM((8, DI), F32),
         pltpu.VMEM((2, L, DI), BF)],
        60_000_000_000, 30 << 20, "back",
    )(cont, inner, vp, cs, cin, stp, sig, tot, tott, sc, dmix, yd, din, cw, sp, sk, ch)


def wide_grad(cont, gn, dy, normed, dgate, reps, shards):
    rows = dy.shape[0]
    block = DI // shards
    shape = (reps, shards, 2 * DI // reps, D // shards)
    return call(
        wide_grad_kernel, shards,
        [pl.BlockSpec((rows, block), lambda k, c: (0, k)), whole(rows, D), whole(rows, D),
         pl.BlockSpec((rows, block), lambda k, c: (0, k))],
        anywhere(1),
        [(shape, BF)],
        [pltpu.VMEM(shape, BF), pltpu.SemaphoreType.DMA((shards, 2 * reps))], 8_600_000_000, 24 << 20, "wide_grad",
    )(cont, gn, dy, normed, dgate)[0]


def conv_grad(cont, normed, turned, nh, turned_halo, reps, shards, other):
    width, rows = turned.shape
    nb = rows // L
    m = D // shards
    half, part = width // 2, width // reps
    return call(
        partial(conv_grad_kernel, nb), shards,
        [pl.BlockSpec((rows, m), lambda k, c: (0, c[nb + 1] ^ k)),
         pl.BlockSpec((half, rows), lambda k, c: (lax.rem(c[nb + 2], 2) ^ other, 0)),
         pl.BlockSpec((LANES, m), lambda k, c: (0, c[nb + 1] ^ k)),
         pl.BlockSpec((half, LANES), lambda k, c: (lax.rem(c[nb + 2], 2) ^ other, 0))],
        [pl.BlockSpec((reps // 2, 1, part, m), lambda k, c: (0, k, 0, 0))],
        [((reps // 2, shards, part, m), BF)],
        [], 5_000_000_000, 8 << 20, "conv_grad",
    )(cont, normed, turned, nh, turned_halo)[0]


def input_grad(cont, x, dy, gp, dgate, ahead, ng, wc, wg, shards):
    rows, width = gp.shape
    nb = rows // L
    convs, gates = len(wc), len(wg)
    return call(
        partial(input_grad_kernel, convs, gates), nb,
        [rows_of(D), rows_of(D), rows_of(width), rows_of(DI), whole(16, width), whole(1, D), *anywhere(convs + gates)],
        [rows_of(D), fixed(8, D)],
        [((rows, D), BF), ((8, D), F32)],
        [pltpu.VMEM((shards, *wc[0].shape), BF), pltpu.VMEM((shards, *wg[0].shape), BF),
         pltpu.SemaphoreType.DMA((copy_count(convs - 1, shards),)), pltpu.SemaphoreType.DMA((copy_count(gates - 1, shards),)),
         pltpu.VMEM((L, D), F32)],
        10_000_000_000, 24 << 20, "input_grad",
    )(cont, x, dy, gp, dgate, ahead, ng, *wc, *wg)


def finish_wide(cont, nb, pieces):
    rows, m = pieces[0].shape
    count = len(pieces)
    part = DI // count
    lines = DI * m // D // count
    return call(
        partial(finish_wide_kernel, nb, count), 1,
        [whole(rows, m)] * count,
        anywhere(2),
        [((DI + CH + H, m), F32), ((lines * count, D), F32)],
        [pltpu.VMEM((count, part, m), F32), pltpu.VMEM((count, lines, D), F32), pltpu.SemaphoreType.DMA((2, count))],
        1_000_000, 8 << 20, "finish_wide",
    )(cont, *pieces)


def finish_conv(cont, nb, pieces, gin, part):
    rows, m = pieces[0].shape
    count = len(pieces)
    half = (rows - part) // 2
    return call(
        partial(finish_conv_kernel, nb, count, part), 1,
        [*[whole(rows, m)] * count, pl.BlockSpec(memory_space=pl.ANY)],
        [pl.BlockSpec(memory_space=pl.ANY), fixed(half, m)],
        [(gin.shape, F32), ((half, m), F32)],
        [pltpu.VMEM((count, part, m), F32), pltpu.SemaphoreType.DMA((count,))],
        1_000_000, 5 << 20, "finish_conv", {1 + count: 0},
    )(cont, *pieces, gin)


def shift(v, by):
    n = lax.axis_size(BOTH)
    return lax.ppermute(v, BOTH, [(i, (i + by) % n) for i in range(n)])


def swap(v, mask):
    n = lax.axis_size(BOTH)
    return lax.ppermute(v, BOTH, [(i, i ^ mask) for i in range(n)])


def part_of(w):
    reps = lax.axis_size("rep")
    part = w.shape[0] // reps
    return lax.dynamic_slice(w, (slot_of(lax.axis_index("rep"), reps) * part, 0), (part, w.shape[1]))


def over_reps(column):
    reps, shards = lax.axis_size("rep"), lax.axis_size("shard")
    return [column] + [swap(column, 2 * shards * j) for j in range(1, reps // 2)]


def over_cores(plane):
    shards = lax.axis_size("shard")
    other = [swap(v, shards) for v in plane]
    return [v for pair in zip(plane, other) for v in pair]


def after(value, *first):
    return lax.optimization_barrier((value, first))[0]


def total_of(first, *others):
    out = first.astype(F32)
    for v in others:
        out = out + v.astype(F32)
    return out.astype(first.dtype)


def two_halves(v, m):
    rows = -(-v.size // (16 * m)) * 16
    v = jnp.pad(v, (0, rows * m - v.size)).reshape(rows, m)
    hi = lax.reduce_precision(v, 8, 7)
    return jnp.concatenate([hi, v - hi], 0).astype(BF)


def one_value(v):
    half = v.shape[0] // 2
    return v[:half].astype(F32) + v[half:].astype(F32)


def local(
    tokens, cotangent, seq_lengths, deal_order, norm_gain, in_proj, conv_weight, conv_bias, step_bias, decay_log,
    skip_gain, gate_gain, out_proj,
):
    n = lax.axis_size(BOTH)
    me = lax.axis_index(BOTH)
    reps, shards = lax.axis_size("rep"), lax.axis_size("shard")
    rep, mine = lax.axis_index("rep"), lax.axis_index("shard")
    rows = tokens.shape[0]
    nb = rows // L
    unit = lcm(LANES, 16 * reps)
    width = -(-(CH + LANES) // unit) * unit

    seqs = seq_lengths.shape[0]
    order = jnp.arange(seqs, dtype=jnp.int32)
    starts = jnp.sum(jnp.where(order[None, :] < order[:, None], seq_lengths[None, :], 0), 1)
    edge = (me * nb + jnp.arange(nb + 1, dtype=jnp.int32)) * L
    cont = jnp.where(jnp.any(starts[None, :] == edge[:, None], 1) | (edge >= n * rows), 0, 1)
    cont = jnp.concatenate([cont.astype(jnp.int32), jnp.stack([mine, rep]).astype(jnp.int32)])

    turned = in_proj.T
    wcs = jnp.pad(turned[DI:], ((0, width - CH - H), (0, 0)))
    wgs = turned[:DI]
    m = wcs.shape[1]
    own_small = [*conv_weight, conv_bias, gate_gain, norm_gain, step_bias, decay_log, skip_gain]
    count = sum(v.size for v in own_small)
    extra = -(-count // (16 * m)) * 16
    small, at = jnp.zeros((extra * m,), BF), 0
    for v in own_small:
        small = small + lax.pad(v, jnp.zeros((), BF), [(at, extra * m - at - v.size, 0)])
        at += v.size
    piece = jnp.concatenate([part_of(wcs), small.reshape(extra, m)], 0)
    small = small[:count]
    part = width // reps
    column = [swap(piece, k) for k in range(1, shards)]
    small = jnp.stack([small] + [v[part:].reshape(-1)[:count] for v in column])
    conv_column = jnp.stack(column)
    halo = shift(tokens[rows - 16 :], 1)
    wo_own = jnp.stack([out_proj[:, at] for at in tiles(D, m)])
    out_rows = out_proj.shape[0] // reps
    out_part = lax.dynamic_slice(wo_own, (0, slot_of(rep, reps) * out_rows, 0), (D // m, out_rows, m))
    piece = jnp.concatenate([part_of(wgs), out_part.reshape(-1, m)], 0)
    gate_column = lax.all_gather(piece, "shard", axis=0)
    gate_column = jnp.take(gate_column, mine ^ jnp.arange(1, shards), axis=0)
    small = jnp.take(small, mine ^ jnp.arange(shards), axis=0).astype(F32)
    sizes = [conv_weight.size, conv_bias.size, gate_gain.size, norm_gain.size, step_bias.size, decay_log.size,
             skip_gain.size]
    parts, at = [], 0
    for size in sizes:
        parts.append(small[:, at : at + size])
        at += size
    taps = parts[0].reshape(shards, CONVW, -1).transpose(1, 0, 2).reshape(CONVW, CH)
    cw = jnp.concatenate([taps, parts[1].reshape(1, CH), jnp.zeros((3, CH), F32)], 0)
    gg = parts[2].reshape(1, DI)
    ng = parts[3].reshape(1, D)
    rate_scale = jnp.exp(parts[5].reshape(1, H))
    sp = jnp.pad(jnp.concatenate([parts[4].reshape(1, H), rate_scale], 0), ((0, 6), (0, LANES - H)))
    sk = jnp.repeat(parts[6].reshape(1, H), P_SIZE, axis=1)

    conv_plane = over_reps(conv_column)
    wc = [wcs, *over_cores(conv_plane[:1] + after(conv_plane[1:], gate_column))]
    gate_plane = over_reps(after(gate_column, conv_plane))

    normed, inner, vp, cs, cin, stp, sig, tot, tott, sloc, fin, nh, ch = front(cont, tokens, halo, ng, wc, cw, sp, shards)
    sin = shift(fin, 1)
    y = scan(cont, inner, vp, tot, tott)
    wg = [wgs, *over_cores(gate_plane[:1] + after(gate_plane[1:-1], y) + after(gate_plane[-1:], y, sin))]
    output, gn, dgate, dmix, yd, sc, dlead, sums = gating(
        cont, tokens, cotangent, normed, inner, y, tot, sloc, sin, wg, wo_own, gg, sk, shards
    )
    din = shift(dlead, -1)
    wide = after(wide_grad(cont, gn, cotangent, normed, dgate, reps, shards), din)
    wide = lax.psum_scatter(wide, "rep", scatter_dimension=0, tiled=True)[0]
    gp, turned_gp, gph, turned_gph, csum, hsum = back(cont, inner, vp, cs, cin, stp, sig, tot, tott, sc, dmix, yd, din, cw, sp, sk, ch, width)

    ahead = shift(gph, -1)
    theirs = swap(after(conv_grad(cont, normed, turned_gp, nh, turned_gph, reps, shards, 1), ahead), shards)
    w = conv_grad(cont, normed, turned_gp, nh, turned_gph, reps, shards, 0)
    w = [total_of(w[j], theirs[j]) for j in range(reps // 2)]
    gp = after(gp, w, wide)
    wide = lax.psum_scatter(after(wide, w), "shard", scatter_dimension=0, tiled=True)[0]
    grad_tokens, grad_norm = input_grad(cont, tokens, cotangent, gp, dgate, ahead, ng, wc, wg, shards)
    csum, hsum, sums, grad_norm = lax.optimization_barrier((csum, hsum, sums, grad_norm))
    csum, wide = lax.optimization_barrier((csum, wide))
    wide = over_cores(over_reps(wide))
    packed = jnp.concatenate(
        [csum[0:CONVW].reshape(CONVW, shards, -1).transpose(1, 0, 2).reshape(shards, -1), csum[4].reshape(shards, -1),
         sums[0].reshape(shards, -1), grad_norm.sum(0).reshape(shards, -1), hsum[0, :H].reshape(shards, -1),
         hsum[1, :H].reshape(shards, -1), sums[1].reshape(H, P_SIZE).sum(1).reshape(shards, -1)], 1)
    packed = jnp.take(packed, mine ^ jnp.arange(shards), axis=0)
    others = [swap(w[j], 2 * shards * j) for j in range(1, reps // 2)]
    halves = [two_halves(packed[k], m) for k in range(shards)]
    others, halves = lax.optimization_barrier((others, halves))
    w = total_of(w[0], *others)
    w = [jnp.concatenate([w[k], halves[k]], 0) for k in range(shards)]
    w = w[:1] + [swap(w[k], k) for k in range(1, shards)]
    rest = sum(one_value(v[part:]) for v in w)
    w = jnp.concatenate([total_of(*[v[:part] for v in w]), two_halves(rest.reshape(-1), m)], 0)
    pieces = over_cores(over_reps(w))
    gin, grad_out = finish_wide(cont, nb, wide)
    grad_in, small = finish_conv(cont, nb, pieces, gin, part)
    grad_in = grad_in.T
    own = small.reshape(-1)
    got, at = [], 0
    for size in sizes:
        got.append(own[at : at + size])
        at += size
    return (
        output, grad_tokens, got[3], grad_in, got[0].reshape(CONVW, -1), got[1], got[4], got[5], got[6], got[2],
        grad_out,
    )


def solution(mesh):
    both = P(BOTH, None)
    in_specs = (
        both, both, P(), P(), P("shard"), P("shard", None), P(None, "shard"), P("shard"), P("shard"), P("shard"),
        P("shard"), P("shard"), P("shard", None),
    )
    out_specs = (
        both, both, P("shard"), P("shard", None), P(None, "shard"), P("shard"), P("shard"), P("shard"), P("shard"),
        P("shard"), P("shard", None),
    )
    return jax.shard_map(local, mesh=mesh, in_specs=in_specs, out_specs=out_specs, check_vma=False)
```
